32 devices in a mesh: dp: 16 (over z, y, core), seq: 2 (over x).
Axes of the slice: x: 2, y: 2, z: 4, core: 2. Of those that a mesh axis runs over, the one named last changes fastest.
Arguments:
- small_tokens: bfloat16 [32, 196, 768], P(('dp', 'seq')), may hold values from -6 to 6
- large_tokens: bfloat16 [16, 784, 768], P('dp', 'seq'), may hold values from -6 to 6
- small_counts: int32 [32], P(('dp', 'seq')), may hold values from 166 to 196, as said below
- large_counts: int32 [16], P('dp'), may hold values from 666 to 784, as said below
- small_cot: bfloat16 [32, 196, 768], P(('dp', 'seq')), may hold values from -6 to 6
- large_cot: bfloat16 [16, 784, 768], P('dp', 'seq'), may hold values from -6 to 6
- w_qkv: float32 [768, 2304], P(('dp', 'seq')), may hold values from -0.21875 to 0.21875
- w_out: float32 [768, 768], P(('dp', 'seq')), may hold values from -0.875 to 0.875
- w_up: float32 [768, 3072], P(('dp', 'seq')), may hold values from -0.21875 to 0.21875
- w_down: float32 [3072, 768], P(('dp', 'seq')), may hold values from -0.109375 to 0.109375
- norm_params: float32 [4, 768], P(None, ('dp', 'seq')), as said below
- proj_bias: float32 [4, 768], P(None, ('dp', 'seq')), may hold values from -1.8 to 1.8
- up_bias: float32 [3072], P(('dp', 'seq')), may hold values from -1.8 to 1.8
Outputs:
- small_out: bfloat16 [32, 196, 768], P(('dp', 'seq'))
- large_out: bfloat16 [16, 784, 768], P('dp', 'seq')
- small_grad: bfloat16 [32, 196, 768], P(('dp', 'seq'))
- large_grad: bfloat16 [16, 784, 768], P('dp', 'seq')
- grad_qkv: float32 [768, 2304], P(('dp', 'seq'))
- grad_out: float32 [768, 768], P(('dp', 'seq'))
- grad_up: float32 [768, 3072], P(('dp', 'seq'))
- grad_down: float32 [3072, 768], P(('dp', 'seq'))
- grad_norm: float32 [4, 768], P(None, ('dp', 'seq'))
- grad_bias: float32 [4, 768], P(None, ('dp', 'seq'))
- grad_up_bias: float32 [3072], P(('dp', 'seq'))
The draws below stay inside these ranges and needn't reach their ends.
Inputs may be any that keep to these rules, and one draw needn't show every extreme that they name: `small_counts`: an image's kept patches fill its first slots, the others are padding; some small image keeps all 196 and some keeps the fewest. `large_counts`: an image's kept patches fill its first slots, the others are padding; some large image keeps all 784 and some keeps the fewest. `norm_params`: rows 0 and 2 are gains between 0.5 and 1.5, rows 1 and 3 shifts.
All inputs are finite; a program needn't handle non-finite values.
Results may differ from the reference program's by a relative error of at most 0.012.
The reference program's roundings to bfloat16 on the way count: a program that leaves them out, or rounds other values in their place, can miss the bound.
Values may be sent and summed in bfloat16 or wider, within the bound.
A program may use at most 192 MiB of HBM per device.

```python
import jax
import jax.numpy as jnp
from jax import lax

D = 768
HEADS = 12
HEAD_DIM = 64
FF = 3072
PS = 196
PL = 784
IMAGES_S = 32
IMAGES_L = 16


def draw_small_counts(key, part):
    key = jax.random.fold_in(key, 11)
    key_count, key_order = jax.random.split(key)
    counts = jax.random.randint(key_count, (IMAGES_S,), PS * 17 // 20, PS + 1)
    ordering = jax.random.permutation(key_order, IMAGES_S)
    counts = counts.at[ordering[0]].set(PS)
    counts = counts.at[ordering[1]].set(PS * 17 // 20)
    return counts.astype(jnp.int32)


def draw_large_counts(key, part):
    key = jax.random.fold_in(key, 23)
    key_count, key_order = jax.random.split(key)
    counts = jax.random.randint(key_count, (IMAGES_L,), PL * 17 // 20, PL + 1)
    ordering = jax.random.permutation(key_order, IMAGES_L)
    counts = counts.at[ordering[0]].set(PL)
    counts = counts.at[ordering[1]].set(PL * 17 // 20)
    return counts.astype(jnp.int32)


def draw_norm_params(key, part):
    key = jax.random.fold_in(key, 5)
    key_gain, key_shift = jax.random.split(key)
    gains = jax.random.uniform(key_gain, (2, D), jnp.float32, 0.5, 1.5)
    shifts = 0.3 * jax.random.normal(key_shift, (2, D), jnp.float32)
    return jnp.stack([gains[0], shifts[0], gains[1], shifts[1]])


def raised(values, rng, source, target, shards_of, factor):
    def block_of(position):
        return (jnp.arange(values.shape[position]) // (values.shape[position] // shards_of)).reshape((-1,) + (1,) * (values.ndim - 1 - position))

    near = jax.random.permutation(rng, shards_of)[block_of(target)]
    far = (block_of(target) + shards_of // 2) % shards_of
    return jnp.where((block_of(source) == near) | (block_of(source) == far), factor * values, values)


def steps_of(stream_key, extent, cuts, low, high):
    level = 1.0
    for position, blocks in cuts:
        steps = jax.random.uniform(jax.random.fold_in(jax.random.fold_in(stream_key, 6), position), (blocks,), jnp.float32, low / len(cuts), high / len(cuts))
        level = level * jnp.repeat(jnp.exp(steps), extent[position] // blocks).reshape((-1,) + (1,) * (len(extent) - 1 - position))
    return level


def centred(rng, shape, width, reach, pieces=(), kind=jnp.bfloat16):
    array = width * jax.random.normal(rng, shape, jnp.float32)
    if pieces:
        array = array * steps_of(rng, shape, pieces, -0.22, 0.18)
    return jnp.clip(array, -reach, reach).astype(kind)


def heavy_noise(rng, shape, width, reach, cuts, heavy, kind=jnp.bfloat16):
    entries = width * jax.random.normal(rng, shape, jnp.float32)
    if cuts:
        entries = entries * steps_of(rng, shape, cuts, -0.22, 0.18)
    return jnp.clip(raised(entries, jax.random.fold_in(rng, 3), *heavy), -reach, reach).astype(kind)


def setup_inputs(seed: int = 0) -> dict:
    seeds = jax.random.split(jax.random.key(seed), 14)
    small_tokens = centred(seeds[0], (IMAGES_S, PS, D), 1.0, 6.0, ((0, 32),))
    large_tokens = centred(seeds[1], (IMAGES_L, PL, D), 1.0, 6.0, ((0, 16), (1, 2)))
    small_counts = draw_small_counts(jax.random.fold_in(seeds[13], 71), 0)
    large_counts = draw_large_counts(jax.random.fold_in(seeds[13], 71), 0)
    small_cot = heavy_noise(seeds[4], (IMAGES_S, PS, D), 1.0, 6.0, ((0, 32),), (0, 2, 32, 2.75))
    large_cot = heavy_noise(seeds[5], (IMAGES_L, PL, D), 1.0, 6.0, ((0, 16), (1, 2)), (0, 2, 16, 2.0))
    w_qkv = centred(seeds[6], (D, 3 * D), D ** -0.5, 0.21875, ((0, 32),), jnp.float32)
    w_out = centred(seeds[7], (D, D), (D // 16) ** -0.5, 0.875, ((0, 32),), jnp.float32)
    w_up = centred(seeds[8], (D, FF), D ** -0.5, 0.21875, ((0, 32),), jnp.float32)
    w_down = centred(seeds[9], (FF, D), FF ** -0.5, 0.109375, ((0, 32),), jnp.float32)
    norm_params = draw_norm_params(jax.random.fold_in(seeds[13], 71), 0)
    proj_bias = centred(seeds[11], (4, D), 0.3, 1.8, ((1, 32),), jnp.float32)
    up_bias = centred(seeds[12], (FF,), 0.3, 1.8, ((0, 32),), jnp.float32)
    return {"small_tokens": small_tokens, "large_tokens": large_tokens, "small_counts": small_counts, "large_counts": large_counts, "small_cot": small_cot, "large_cot": large_cot, "w_qkv": w_qkv, "w_out": w_out, "w_up": w_up, "w_down": w_down, "norm_params": norm_params, "proj_bias": proj_bias, "up_bias": up_bias}


@jax.custom_vjp
def low(v):
    return lax.optimization_barrier(v.astype(jnp.bfloat16)).astype(jnp.float32)

@jax.custom_vjp
def low_back(v):
    return v

def low_keep(v):
    return (low(v), None)

def low_pass(kept, grad):
    return (grad,)

def back_keep(v):
    return (v, None)

def back_low(kept, grad):
    return (low(grad),)
low.defvjp(low_keep, low_pass)
low_back.defvjp(back_keep, back_low)
PRECISE = lax.Precision.HIGHEST

def norm_rows(values, gain, shift):
    centre = lax.optimization_barrier(jnp.mean(values, -1, keepdims=True))
    centered = values - centre
    spread = lax.optimization_barrier(jnp.mean(centered * centered, -1, keepdims=True))
    return centered * lax.rsqrt(spread + 1e-06) * gain + shift

def layer_block(params, tokens, counts):
    param_qkv, param_out, param_up, param_down, param_norm, param_bias, param_upbias = params
    batch_size, length, width_dim = tokens.shape
    valid_keys = jnp.arange(length, dtype=jnp.int32)[None, :] < counts[:, None]
    normed_one = low(norm_rows(tokens, param_norm[0], param_norm[1]))
    qkv_bias = jnp.concatenate([param_bias[0], jnp.zeros((width_dim,), jnp.float32), param_bias[1]])
    qkv_rows = jnp.einsum('bld,df->blf', normed_one, param_qkv, precision=PRECISE) + qkv_bias
    qkv_rows = low(low_back(qkv_rows))
    split_heads = qkv_rows.reshape(batch_size, length, 3, HEADS, HEAD_DIM)
    query = split_heads[:, :, 0]
    key_part = split_heads[:, :, 1]
    value = split_heads[:, :, 2]
    raw_scores = low_back(jnp.einsum('bqhe,bkhe->bhqk', query, key_part, precision=PRECISE))
    scaled = jnp.where(valid_keys[:, None, None, :], raw_scores * HEAD_DIM ** (-0.5), -1e+30)
    row_top = lax.optimization_barrier(jnp.max(scaled, -1, keepdims=True))
    expo_rows = jnp.exp(scaled - row_top)
    probs_full = expo_rows / lax.optimization_barrier(jnp.sum(expo_rows, -1, keepdims=True))
    probs_low = low(probs_full)
    mixed = jnp.einsum('bhqk,bkhe->bqhe', probs_low, value, precision=PRECISE).reshape(batch_size, length, width_dim)
    mixed = low(low_back(mixed))
    attn_out = low_back(jnp.einsum('bld,df->blf', mixed, param_out, precision=PRECISE) + param_bias[2])
    middle = tokens + attn_out
    normed_two = low(norm_rows(middle, param_norm[2], param_norm[3]))
    up_proj = low_back(jnp.einsum('bld,df->blf', normed_two, param_up, precision=PRECISE) + param_upbias)
    act_low = low(jax.nn.gelu(up_proj, approximate=False))
    down_proj = low_back(jnp.einsum('blf,fd->bld', act_low, param_down, precision=PRECISE) + param_bias[3])
    return middle + down_proj

def reference(small_tokens, large_tokens, small_counts, large_counts, small_cot, large_cot, w_qkv, w_out, w_up, w_down, norm_params, proj_bias, up_bias):

    def forward(small_x, large_x, param_qkv, param_out, param_up, param_down, param_norm, param_bias, param_upbias):
        params = (low(param_qkv), low(param_out), low(param_up), low(param_down), low(param_norm), low(param_bias), low(param_upbias))

        def run_group(group_pair):
            return layer_block(params, group_pair[0], group_pair[1])
        run_saved = jax.checkpoint(run_group)
        small_groups = small_x.reshape(IMAGES_S // 16, 16, PS, D)
        small_sizes = small_counts.reshape(IMAGES_S // 16, 16)
        small_result = lax.map(run_saved, (small_groups, small_sizes)).reshape(IMAGES_S, PS, D)
        large_groups = large_x.reshape(IMAGES_L // 4, 4, PL, D)
        large_sizes = large_counts.reshape(IMAGES_L // 4, 4)
        large_result = lax.map(run_saved, (large_groups, large_sizes)).reshape(IMAGES_L, PL, D)
        return (small_result, large_result)
    primals = (small_tokens.astype(jnp.float32), large_tokens.astype(jnp.float32), w_qkv, w_out, w_up, w_down, norm_params, proj_bias, up_bias)
    outputs, pullback = jax.vjp(forward, *primals)
    grads = pullback((small_cot.astype(jnp.float32), large_cot.astype(jnp.float32)))
    return (outputs[0].astype(jnp.bfloat16), outputs[1].astype(jnp.bfloat16), grads[0].astype(jnp.bfloat16), grads[1].astype(jnp.bfloat16), grads[2], grads[3], grads[4], grads[5], grads[6], grads[7], grads[8])
```

```python
import functools

import jax
import jax.numpy as jnp
from jax import lax
from jax.experimental import pallas as pl
from jax.experimental.pallas import tpu as pltpu
from jax.sharding import PartitionSpec as P

HEAD_DIM = 64
MESH = pl.DeviceIdType.MESH
BF = jnp.bfloat16
F32 = jnp.float32


def dot(a, b):
    return lax.dot_general(a, b, (((1,), (0,)), ((), ())), preferred_element_type=F32)


def dot_rows(a, b):
    return lax.dot_general(a, b, (((0,), (0,)), ((), ())), preferred_element_type=F32)


def dot_cols(a, b):
    return lax.dot_general(a, b, (((1,), (1,)), ((), ())), preferred_element_type=F32)


def place():
    d = lax.axis_index("dp")
    return lax.axis_index("seq"), (d // 2) % 2, d // 4, d % 2


def device(x, y, z, c):
    return ((z * 2 + y) * 2 + c, x)


def greet(partners):
    bar = pltpu.get_barrier_semaphore()
    for p in partners:
        pl.semaphore_signal(bar, inc=1, device_id=p, device_id_type=MESH)
    pl.semaphore_wait(bar, len(partners))


def neighbours(x, y, z, c):
    zs = [(z + k) % 4 for k in (1, 2, 3)]
    return (
        device(x, y, z, 1 - c),
        device(1 - x, y, z, c),
        device(x, 1 - y, z, c),
        [device(x, y, k, c) for k in zs],
        zs,
    )


def rcopy(src, dst, send, recv, dev):
    return pltpu.make_async_remote_copy(
        src_ref=src, dst_ref=dst, send_sem=send, recv_sem=recv, device_id=dev, device_id_type=MESH
    )


def stack_halves(g):
    n = g.shape[1] // 2
    return jnp.concatenate([g[:, :n], g[:, n:]], axis=0)


def assemble(S, b, dst, col):
    w, h = b // 2, b % 2
    n = S.shape[-1]

    def step(j, _):
        z, y, c = j // 4, (j // 2) % 2, j % 2
        a = S[w, h, 0, y, z, c].astype(F32)
        e = S[w, h, 1, y, z, c].astype(F32)
        k = a.shape[0] // 2
        rows = pl.ds(pl.multiple_of(j * 2 * k, 16), 2 * k)
        dst[rows, col : col + n] = jnp.concatenate([a[:k], e[:k]], axis=0).astype(BF)
        dst[rows, col + n : col + 2 * n] = jnp.concatenate([a[k:], e[k:]], axis=0).astype(BF)
        return 0

    lax.fori_loop(0, 16, step, 0)


def assemble_down(S, b, dst):
    w, h = b // 2, b % 2
    n = S.shape[-1]
    half = (b - 8) // 2

    def step(j, _):
        z, y, c = j // 4, (j // 2) % 2, j % 2
        for x in range(2):
            rows = pl.ds(pl.multiple_of(96 * (2 * j + x) + 48 * half, 16), 48)
            dst[rows, n * h : n * h + n] = S[w, h, x, y, z, c]
        return 0

    lax.fori_loop(0, 16, step, 0)


def gather_kernel(
    wqkv, wout, wup, wdown, small, tokens,
    fqkv, fout, fup, fdown, fsmall, ptok,
    own, S, mytok, sm, smland, smb, ss, rs, tsem, sms, smr,
):
    x, y, z, c = place()
    sib, xn, yn, zn, zs = neighbours(x, y, z, c)
    greet([sib, xn, yn] + zn)
    width = tokens.shape[1]
    nrow = tokens.shape[0]
    mytok[0:nrow, :] = tokens[...]
    mytok[nrow:, :] = jnp.zeros((mytok.shape[0] - nrow, width), BF)
    tcp = rcopy(mytok, ptok, tsem.at[0], tsem.at[1], xn)
    tcp.start()
    blocks = [wqkv[:, k * width : (k + 1) * width] for k in range(3)]
    blocks.append(wout[...])
    blocks += [wup[:, k * width : (k + 1) * width] for k in range(4)]
    for b, g in enumerate(blocks):
        own[b // 2, b % 2] = stack_halves(g).astype(BF)
    for b in range(8, 12):
        half, h = (b - 8) // 2, b % 2
        n = width // 2
        own[b // 2, h] = wdown[48 * half : 48 * half + 48, h * n : h * n + n].astype(BF)
    for w in range(6):
        S[w, c, x, y, z, c] = own[w, c]
    c0 = [rcopy(own.at[w, 1 - c], S.at[w, 1 - c, x, y, z, c], ss.at[w, 0], rs.at[w, 0], sib) for w in range(6)]
    for cp in c0:
        cp.start()
    sm[...] = small[...].astype(BF)

    def join(k, dev):
        cp = rcopy(sm, smland.at[k], sms.at[k], smr.at[k], dev)
        cp.start()
        return cp

    def joined(cps, ks):
        for cp in cps:
            cp.wait()
        tot = sm[...].astype(F32)
        for k in ks:
            tot = tot + smland[k].astype(F32)
        sm[...] = tot.astype(BF)

    joined([join(0, sib)], [0])

    def zcopy(w, i):
        k = zs[i]
        src = S.at[w, c, x, y, z]
        return rcopy(src, src, ss.at[w, 1 + i], rs.at[w, 1 + i], zn[i])

    def zwait(w, i):
        dst = S.at[w, c, x, y, zs[i]]
        return rcopy(dst, dst, ss.at[w, 1 + 2 - i], rs.at[w, 1 + 2 - i], zn[i])

    def stage1(w):
        c0[w].wait()
        for i in range(3):
            zcopy(w, i).start()

    def stage2(w, start):
        if start:
            for i in range(3):
                zcopy(w, i).wait_send()
                zwait(w, i).wait_recv()
        src = S.at[w, c, x, y]

        def go(dev, dst):
            if start:
                rcopy(src, src, ss.at[w, 4], rs.at[w, 4], dev).start()
            else:
                cp = rcopy(src, dst, ss.at[w, 4], rs.at[w, 4], dev)
                cp.wait_send()
                cp.wait_recv()

        pl.when(c == 0)(lambda: go(xn, S.at[w, c, 1 - x, y]))
        pl.when(c == 1)(lambda: go(yn, S.at[w, c, x, 1 - y]))

    def stage3(w, start):
        if start:
            stage2(w, False)

        def go(dev, src, dst):
            if start:
                rcopy(src, src, ss.at[w, 5], rs.at[w, 5], dev).start()
            else:
                cp = rcopy(src, dst, ss.at[w, 5], rs.at[w, 5], dev)
                cp.wait_send()
                cp.wait_recv()

        pl.when(c == 0)(lambda: go(yn, S.at[w, c, :, y], S.at[w, c, :, 1 - y]))
        pl.when(c == 1)(lambda: go(xn, S.at[w, c, x], S.at[w, c, 1 - x]))

    def share(w):
        src = S.at[w, c]
        return rcopy(src, src, ss.at[w, 6], rs.at[w, 6], sib)

    def use(w):
        cp = share(w)
        cp.wait_send()
        dst = S.at[w, 1 - c]
        rcopy(dst, dst, ss.at[w, 6], rs.at[w, 6], sib).wait_recv()
        for b in (2 * w, 2 * w + 1):
            if b < 3:
                assemble(S, b, fqkv, b * width)
            elif b == 3:
                assemble(S, b, fout, 0)
            elif b < 8:
                assemble(S, b, fup, (b - 4) * width)
            else:
                assemble_down(S, b, fdown)

    for t in range(10):
        if t < 6:
            stage1(t)
        if t == 0:
            joined([join(1 + i, zn[i]) for i in range(3)], [1, 2, 3])
        if t == 1:
            joined([join(4, xn)], [4])
        if t == 2:
            joined([join(5, yn)], [5])
            fsmall[...] = sm[...].astype(F32)
        if 1 <= t < 7:
            stage2(t - 1, True)
        if 2 <= t < 8:
            stage3(t - 2, True)
        if 3 <= t < 9:
            stage3(t - 3, False)
            share(t - 3).start()
        if t >= 4:
            use(t - 4)
    tcp.wait()


def vm():
    return pl.BlockSpec(memory_space=pltpu.VMEM)


def params(cid=None, limit=62):
    return pltpu.CompilerParams(
        collective_id=cid, has_side_effects=cid is not None, vmem_limit_bytes=limit << 20
    )


def gather(wqkv, wout, wup, wdown, small, tokens):
    D = wout.shape[1]
    FF = wup.shape[1]
    half = D // 2
    rows = -(-tokens.shape[0] // 16) * 16
    sds = jax.ShapeDtypeStruct
    return pl.pallas_call(
        gather_kernel,
        out_shape=(
            sds((D, 3 * D), BF), sds((D, D), BF), sds((D, FF), BF), sds((FF, D), BF),
            sds(small.shape, F32), sds((rows, D), BF),
        ),
        in_specs=[vm()] * 6,
        out_specs=(vm(),) * 6,
        scratch_shapes=[
            pltpu.VMEM((6, 2, 48, half), BF),
            pltpu.VMEM((6, 2, 2, 2, 4, 2, 48, half), BF),
            pltpu.VMEM((rows, D), BF),
            pltpu.VMEM(small.shape, BF),
            pltpu.VMEM((6,) + small.shape, BF),
            pltpu.VMEM(small.shape, BF),
            pltpu.SemaphoreType.DMA((6, 7)),
            pltpu.SemaphoreType.DMA((6, 7)),
            pltpu.SemaphoreType.DMA((2,)),
            pltpu.SemaphoreType.DMA((6,)),
            pltpu.SemaphoreType.DMA((6,)),
        ],
        compiler_params=params(1),
        name="gather",
    )(wqkv, wout, wup, wdown, small, tokens)


def normalize(v):
    centred = v - jnp.mean(v, -1, keepdims=True)
    scale = lax.rsqrt(jnp.mean(centred * centred, -1, keepdims=True) + 1e-06)
    return centred * scale, scale


def norm_back(v, gain, grad):
    unit, scale = normalize(v)
    lifted = grad * gain
    inner = jnp.mean(lifted * unit, -1, keepdims=True)
    return scale * (lifted - jnp.mean(lifted, -1, keepdims=True) - unit * inner), unit


def rows_of(i, size):
    return pl.ds(pl.multiple_of(i * size, 16), size)


def lanes_of(i, size, base=0):
    return pl.ds(pl.multiple_of(base + i * size, 128), size)


def gelu_pair(h):
    p = 0.3275911 * 0.7071067811865476
    a = abs(h)
    t = 1.0 / (1.0 + p * a)
    e = jnp.exp(-0.5 * h * h)
    poly = ((((1.061405429 * t - 1.453152027) * t + 1.421413741) * t - 0.284496736) * t + 0.254829592) * t
    q = 0.5 * poly * e
    phi = jnp.where(h >= 0, 1.0 - q, q)
    return h * phi, phi + h * e * 0.3989422804014327


def head_masks(n):
    lane = lax.broadcasted_iota(jnp.int32, (n, 128), 1)
    return lane < 64


def heads_forward(QKV, MIX, LSE, bias, q0, nq, k0, nk, qb, D):
    lane = lax.broadcasted_iota(jnp.int32, (qb, 128), 1)
    first = lane < 64

    def pair(hp, _):
        k = QKV[k0 : k0 + nk, lanes_of(hp, 128, D)]
        v = QKV[k0 : k0 + nk, lanes_of(hp, 128, 2 * D)]

        def block(i, _):
            rows = pl.ds(pl.multiple_of(q0 + i * qb, 16), qb)
            q = QKV[rows, lanes_of(hp, 128)] * jnp.asarray(HEAD_DIM**-0.5, BF)
            outs = []
            lrows = pl.ds(pl.multiple_of(i * qb, 16), qb)
            logs = LSE[lrows, :]
            for head in range(2):
                keep = first if head == 0 else jnp.logical_not(first)
                qm = jnp.where(keep, q, jnp.zeros_like(q))
                s = dot_cols(qm, k) + bias
                top = jnp.max(s, -1, keepdims=True)
                e = jnp.exp(s - top)
                total = jnp.sum(e, -1, keepdims=True)
                pr = (e * (1.0 / total)).astype(BF)
                outs.append(dot(pr, v))
                logs = jnp.where(lane == 2 * hp + head, top + jnp.log(total), logs)
            LSE[lrows, :] = logs
            MIX[rows, lanes_of(hp, 128)] = jnp.where(first, outs[0], outs[1]).astype(BF)
            return 0

        lax.fori_loop(0, nq // qb, block, 0)
        return 0

    lax.fori_loop(0, D // 128, pair, 0)


def heads_backward(QKV, DMIX, DQKV, LSE, DELTA, DS, KB, q0, nq, k0, nk, kb, D):
    firstq = lax.broadcasted_iota(jnp.int32, (nq, 128), 1) < 64
    firstk = lax.broadcasted_iota(jnp.int32, (kb, 128), 1) < 64

    def pair(hp, _):
        q = QKV[q0 : q0 + nq, lanes_of(hp, 128)] * jnp.asarray(HEAD_DIM**-0.5, BF)
        dm = DMIX[q0 : q0 + nq, lanes_of(hp, 128)]
        zero = jnp.zeros_like(q)
        qs = [jnp.where(firstq, q, zero), jnp.where(firstq, zero, q)]
        dms = [jnp.where(firstq, dm, zero), jnp.where(firstq, zero, dm)]
        lses = [LSE[pl.ds(2 * hp + head, 1), :][:, :nq] for head in range(2)]
        deltas = [DELTA[pl.ds(2 * hp + head, 1), :][:, :nq] for head in range(2)]

        def block(i, _):
            rows = pl.ds(pl.multiple_of(k0 + i * kb, 16), kb)
            lrows = pl.ds(pl.multiple_of(i * kb, 16), kb)
            k = QKV[rows, lanes_of(hp, 128, D)]
            v = QKV[rows, lanes_of(hp, 128, 2 * D)]
            bias = KB[lrows, :][:, :1]
            dks, dvs = [], []
            for head in range(2):
                s = dot_cols(k, qs[head]) + bias
                pr = jnp.exp(s - lses[head])
                dvs.append(dot(pr.astype(BF), dm))
                dp = dot_cols(v, dms[head])
                ds = (pr * (dp - deltas[head])).astype(BF)
                dks.append(dot(ds, q))
                DS[head, lrows, :nq] = ds
            DQKV[rows, lanes_of(hp, 128, D)] = jnp.where(firstk, dks[0], dks[1]).astype(BF)
            DQKV[rows, lanes_of(hp, 128, 2 * D)] = jnp.where(firstk, dvs[0], dvs[1]).astype(BF)
            return 0

        lax.fori_loop(0, nk // kb, block, 0)
        k = QKV[k0 : k0 + nk, lanes_of(hp, 128, D)]
        outs = [dot_rows(DS[head, :nk, :nq], k) for head in range(2)]
        DQKV[q0 : q0 + nq, lanes_of(hp, 128)] = (
            jnp.where(firstq, outs[0], outs[1]) * HEAD_DIM**-0.5
        ).astype(BF)
        return 0

    lax.fori_loop(0, D // 128, pair, 0)


def outer(GB, A, B, a0, b0, n):
    size = GB.shape[0] // 3

    def step(i, _):
        a = A[0:n, lanes_of(i, size, a0)]
        GB[rows_of(i, size), :] = dot_rows(a, B[0:n, b0 : b0 + GB.shape[1]])
        return 0

    lax.fori_loop(0, 3, step, 0)


def store_blocks(GB, P, b):
    w, h = b // 2, b % 2

    def step(j, _):
        z, y, c = j // 4, (j // 2) % 2, j % 2
        g = GB[pl.ds(pl.multiple_of(j * 48, 8), 48), :]
        for x in range(2):
            P[w, h, x, y, z, c] = stack_halves(g[24 * x : 24 * x + 24]).astype(BF)
        return 0

    lax.fori_loop(0, 16, step, 0)


def store_down(GB, P, f):
    def step(j, _):
        y, c = j // 2, j % 2
        for x in range(2):
            for half in range(2):
                g = GB[pl.ds(pl.multiple_of((2 * j + x) * 96 + 48 * half, 8), 48), :]
                for h in range(2):
                    n = P.shape[-1]
                    P[4 + half, h, x, y, f, c] = g[:, h * n : h * n + n].astype(BF)
        return 0

    lax.fori_loop(0, 4, step, 0)


def layer_kernel(
    xs, xl, xp, cs, cl, counts, wqkv, wout, wup, wdown, sp,
    outs, outl, P, DH1, MID, DH1P, SG,
    X, DY, H1, QKV, MIX, H2, DH2, ACT, DHB, GB, DQKV, DML, DMIX,
    LSES, LSEL, DELS, DELL, LSEST, LSELT, DELST, DELLT, DS, KBS, KBL,
):
    D = xs.shape[1]
    ns, nl = xs.shape[0], xl.shape[0]
    rs = -(-ns // 16) * 16
    rl = -(-nl // 16) * 16
    R = rs + rl
    RK = R + rl
    RB = 32
    seq = lax.axis_index("seq")
    zero = functools.partial(jnp.zeros, dtype=BF)
    X[ns - ns % 16 : rs, :] = zero((rs - (ns - ns % 16), D))
    X[R - 16 : R, :] = zero((16, D))
    X[0:ns, :] = xs[...]
    X[rs : rs + nl, :] = xl[...]
    X[R:RK, :] = xp[...]
    DY[ns - ns % 16 : rs, :] = zero((rs - (ns - ns % 16), D))
    DY[R - 16 : R, :] = zero((16, D))
    DY[0:ns, :] = cs[...]
    DY[rs : rs + nl, :] = cl[...]
    SG[...] = jnp.zeros(SG.shape, F32)

    def norm_one(i, _):
        rows = rows_of(i, 48)
        unit, _ = normalize(X[rows, :].astype(F32))
        H1[rows, :] = (unit * sp[0:1, :] + sp[1:2, :]).astype(BF)
        return 0

    lax.fori_loop(0, RK // 48, norm_one, 0)
    third, half = RK // 3, R // 2

    def project(i, _):
        rows = rows_of(i, third)
        h = H1[rows, :]
        QKV[rows, 0:D] = (dot(h, wqkv[:, 0:D]) + sp[4:5, :]).astype(BF)
        QKV[rows, D : 2 * D] = dot(h, wqkv[:, D : 2 * D]).astype(BF)
        QKV[rows, 2 * D :] = (dot(h, wqkv[:, 2 * D :]) + sp[5:6, :]).astype(BF)
        return 0

    lax.fori_loop(0, 3, project, 0)

    small_count = counts[0]
    large_count = counts[1]
    kj = lax.broadcasted_iota(jnp.int32, (1, rs), 1)
    bias_small = jnp.where(kj < small_count, 0.0, -1e30)
    kj = lax.broadcasted_iota(jnp.int32, (1, 2 * rl), 1)

    def large_bias(kj):
        mine = kj < rl
        inside = jnp.where(mine, kj, kj - rl)
        where = inside + jnp.where(mine, seq, 1 - seq) * nl
        return jnp.where((inside < nl) & (where < large_count), 0.0, -1e30)

    heads_forward(QKV, MIX, LSES, bias_small, 0, rs, 0, rs, rs, D)
    heads_forward(QKV, MIX, LSEL, large_bias(kj), rs, rl, rs, 2 * rl, 80, D)

    def project_out(i, _):
        rows = rows_of(i, half)
        MID[rows, :] = dot(MIX[rows, :], wout[...])
        return 0

    lax.fori_loop(0, 2, project_out, 0)

    def norm_two(i, _):
        rows = rows_of(i, RB)
        middle = X[rows, :].astype(F32) + MID[rows, :] + sp[6:7, :]
        MID[rows, :] = middle
        unit, _ = normalize(middle)
        H2[rows, :] = (unit * sp[2:3, :] + sp[3:4, :]).astype(BF)
        DH1[rows, :] = middle + sp[7:8, :]
        return 0

    lax.fori_loop(0, R // RB, norm_two, 0)

    DH2[...] = jnp.zeros(DH2.shape, F32)

    def quarter(f, _):
        fl = lanes_of(f, D)
        fr = pl.ds(pl.multiple_of(f * D, 16), D)
        ub = sp[pl.ds(8 + f, 1), :]

        def part(i, tot):
            rows = rows_of(i, half)
            hidden = dot(H2[rows, :], wup[:, fl]) + ub
            dact = dot_cols(DY[rows, :], wdown[fr, :])
            act, slope = gelu_pair(hidden)
            ACT[rows, :] = act.astype(BF)
            dh = (dact * slope).astype(BF)
            DHB[rows, :] = dh
            return tot + jnp.sum(dh.astype(F32), 0, keepdims=True)

        SG[pl.ds(8 + f, 1), :] = lax.fori_loop(0, 2, part, jnp.zeros((1, D), F32))

        def gather_up(i, _):
            rows = rows_of(i, half)
            DH1[rows, :] += dot(ACT[rows, :], wdown[fr, :])
            DH2[rows, :] += dot_cols(DHB[rows, :], wup[:, fl])
            return 0

        lax.fori_loop(0, 2, gather_up, 0)
        outer(GB, ACT, DY, 0, 0, R)
        store_down(GB, P, f)
        outer(GB, H2, DHB, 0, 0, R)

        def step(j, _):
            z, y, c = j // 4, (j // 2) % 2, j % 2
            g = GB[pl.ds(pl.multiple_of(j * 48, 8), 48), :]
            for x in range(2):
                P[2 + f // 2, f % 2, x, y, z, c] = stack_halves(g[24 * x : 24 * x + 24]).astype(BF)
            return 0

        lax.fori_loop(0, 16, step, 0)
        return 0

    lax.fori_loop(0, 4, quarter, 0)
    outs[...] = DH1[0:ns, :].astype(BF)
    outl[...] = DH1[rs : rs + nl, :].astype(BF)

    def back_two(i, sums):
        rows = rows_of(i, RB)
        grad = DH2[rows, :]
        dy = DY[rows, :].astype(F32)
        dv, unit = norm_back(MID[rows, :], sp[2:3, :], grad)
        dmid = dy + dv
        MID[rows, :] = dmid
        low = dmid.astype(BF)
        DML[rows, :] = low
        return (
            sums[0] + jnp.sum(grad * unit, 0, keepdims=True),
            sums[1] + jnp.sum(grad, 0, keepdims=True),
            sums[2] + jnp.sum(low.astype(F32), 0, keepdims=True),
            sums[3] + jnp.sum(dy, 0, keepdims=True),
        )

    z1 = jnp.zeros((1, D), F32)
    sums = lax.fori_loop(0, R // RB, back_two, (z1, z1, z1, z1))
    SG[2:3, :] = sums[0]
    SG[3:4, :] = sums[1]
    SG[6:7, :] = sums[2]
    SG[7:8, :] = sums[3]

    def back_out(i, _):
        rows = rows_of(i, half)
        DMIX[rows, :] = dot_cols(DML[rows, :], wout[...]).astype(BF)
        return 0

    lax.fori_loop(0, 2, back_out, 0)
    outer(GB, MIX, DML, 0, 0, R)
    store_blocks(GB, P, 3)

    lane = lax.broadcasted_iota(jnp.int32, (16, 128), 1)

    def deltas(base, out):
        def step(i, _):
            rows = pl.ds(pl.multiple_of(base + i * 16, 16), 16)
            acc = jnp.zeros((16, 128), F32)
            for hp in range(D // 128):
                pr = DMIX[rows, hp * 128 : hp * 128 + 128].astype(F32) * MIX[
                    rows, hp * 128 : hp * 128 + 128
                ].astype(F32)
                a = jnp.sum(jnp.where(lane < 64, pr, 0.0), -1, keepdims=True)
                e = jnp.sum(jnp.where(lane < 64, 0.0, pr), -1, keepdims=True)
                acc = jnp.where(lane == 2 * hp, a, jnp.where(lane == 2 * hp + 1, e, acc))
            out[pl.ds(pl.multiple_of(i * 16, 16), 16), :] = acc
            return 0

        return step

    lax.fori_loop(0, rs // 16, deltas(0, DELS), 0)
    lax.fori_loop(0, rl // 16, deltas(rs, DELL), 0)
    kj = lax.broadcasted_iota(jnp.int32, (rs, 128), 0)
    KBS[...] = jnp.where(kj < small_count, 0.0, -1e30)
    kj = lax.broadcasted_iota(jnp.int32, (2 * rl, 128), 0)
    KBL[...] = large_bias(kj)
    LSEST[...] = jnp.transpose(LSES[...])
    DELST[...] = jnp.transpose(DELS[...])
    LSELT[...] = jnp.transpose(LSEL[...])
    DELLT[...] = jnp.transpose(DELL[...])
    heads_backward(QKV, DMIX, DQKV, LSEST, DELST, DS, KBS, 0, rs, 0, rs, rs, D)
    heads_backward(QKV, DMIX, DQKV, LSELT, DELLT, DS, KBL, rs, rl, rs, 2 * rl, 160, D)

    outer(GB, H1, DQKV, 0, 0, R)
    store_blocks(GB, P, 0)
    outer(GB, H1, DQKV, 0, D, RK)
    store_blocks(GB, P, 1)
    outer(GB, H1, DQKV, 0, 2 * D, RK)
    store_blocks(GB, P, 2)
    def back_qkv(i, sums):
        rows = rows_of(i, half)
        DH1[rows, :] = dot_cols(DQKV[rows, :], wqkv[...])
        return (
            sums[0] + jnp.sum(DQKV[rows, 0:D].astype(F32), 0, keepdims=True),
            sums[1] + jnp.sum(DQKV[rows, 2 * D :].astype(F32), 0, keepdims=True),
        )

    sums = lax.fori_loop(0, 2, back_qkv, (z1, z1))
    SG[4:5, :] = sums[0]
    SG[5:6, :] = sums[1] + jnp.sum(DQKV[R:RK, 2 * D :].astype(F32), 0, keepdims=True)
    DH1P[...] = dot_cols(DQKV[R:RK, D:], wqkv[:, D:]).astype(BF)


def scatter_kernel(
    P, DH1, DMID, DH1P, xs, xl, sp, SG,
    gqkv, gout, gup, gdown, dxs, dxl, SGO,
    X, DX, LP, LC, LA, LB, LZ, T, LF, SM, SML, ss, rs, tsem, sms, smr,
):
    x, y, z, c = place()
    sib, xn, yn, zn, zs = neighbours(x, y, z, c)
    greet([sib, xn, yn] + zn)
    D = xs.shape[1]
    ns, nl = xs.shape[0], xl.shape[0]
    r1 = -(-ns // 16) * 16
    rl = -(-nl // 16) * 16
    R = r1 + rl
    tcp = rcopy(DH1P, LP, tsem.at[0], tsem.at[1], xn)
    tcp.start()
    order = [2, 3, 4, 5, 1, 0]

    def add(dst, dsts, src, srcs, n):
        def step(i, _):
            d = dsts(i)
            dst[d] = (dst[d].astype(F32) + src[srcs(i)].astype(F32)).astype(BF)
            return 0

        lax.fori_loop(0, n, step, 0)

    def first(w, start):
        cp = rcopy(P.at[w, 1 - c], LC.at[w], ss.at[w, 0], rs.at[w, 0], sib)
        if start:
            cp.start()
            return
        cp.wait()
        idx = lambda i: (i // 16, (i // 8) % 2, (i // 2) % 4, i % 2)
        add(LC, lambda i: (w,) + idx(i), P, lambda i: (w, c) + idx(i), 32)

    def second(w, start):
        def go(dev, src, kept):
            cp = rcopy(src, LA.at[w], ss.at[w, 1], rs.at[w, 1], dev)
            if start:
                cp.start()
                return
            cp.wait()
            idx = lambda i: (i // 8, (i // 2) % 4, i % 2)
            add(LA, lambda i: (w,) + idx(i), LC, lambda i: (w,) + kept(idx(i)), 16)

        pl.when(c == 0)(lambda: go(yn, LC.at[w, :, 1 - y], lambda i: (i[0], y, i[1], i[2])))
        pl.when(c == 1)(lambda: go(xn, LC.at[w, 1 - x], lambda i: (x, i[0], i[1], i[2])))

    def third(w, start):
        def go(dev, other, kept):
            cp = rcopy(LA.at[w, other], LB.at[w], ss.at[w, 2], rs.at[w, 2], dev)
            if start:
                cp.start()
                return
            cp.wait()
            idx = lambda i: (i // 2, i % 2)
            add(LB, lambda i: (w,) + idx(i), LA, lambda i: (w, kept) + idx(i), 8)

        pl.when(c == 0)(lambda: go(xn, 1 - x, x))
        pl.when(c == 1)(lambda: go(yn, 1 - y, y))

    def fourth(w, start):
        cps = [rcopy(LB.at[w, zs[i]], LZ.at[w, i], ss.at[w, 3 + i], rs.at[w, 3 + i], zn[i]) for i in range(3)]
        if start:
            for cp in cps:
                cp.start()
            return
        for cp in cps:
            cp.wait()
        for k in range(2):
            tot = LB[w, z, k].astype(F32)
            for i in range(3):
                tot = tot + LZ[w, i, k].astype(F32)
            T[w, k] = tot

    def fifth(w, start):
        cp = rcopy(T.at[w, 1 - c], LF.at[w], ss.at[w, 6], rs.at[w, 6], sib)
        if start:
            cp.start()
            return
        cp.wait()
        mine, other = T[w, c], LF[w]
        n = mine.shape[1]
        for h in range(2):
            g = jnp.where(c == h, mine, other)
            b = 2 * w + h
            if b >= 8:
                half = (b - 8) // 2
                gdown[48 * half : 48 * half + 48, n * h : n * h + n] = g
                continue
            dst, col = (gqkv, b * D) if b < 3 else (gout, 0) if b == 3 else (gup, (b - 4) * D)
            dst[:, col : col + n] = g[0:24]
            dst[:, col + n : col + 2 * n] = g[24:48]

    stages = [first, second, third, fourth, fifth]
    for w in order:
        first(w, True)

    X[0:ns, :] = xs[...]
    X[r1 : r1 + nl, :] = xl[...]
    X[ns - ns % 16 : ns, :] = xs[ns - ns % 16 :, :]
    tcp.wait()

    def back_one(base, size, partner):
        def step(i, sums):
            rows = pl.ds(pl.multiple_of(base + i * size, 16), size)
            grad = DH1[rows, :]
            if partner:
                grad = grad + LP[pl.ds(pl.multiple_of(i * size, 16), size), :].astype(F32)
            dv, unit = norm_back(X[rows, :].astype(F32), sp[0:1, :], grad)
            DX[rows, :] = (DMID[rows, :] + dv).astype(BF)
            return (
                sums[0] + jnp.sum(grad * unit, 0, keepdims=True),
                sums[1] + jnp.sum(grad, 0, keepdims=True),
            )

        return step

    z1 = jnp.zeros((1, D), F32)
    sums = lax.fori_loop(0, r1 // 16, back_one(0, 16, False), (z1, z1))
    sums = lax.fori_loop(0, rl // 16, back_one(r1, 16, True), sums)
    dxs[...] = DX[0:ns, :]
    dxl[...] = DX[r1 : r1 + nl, :]
    SM[...] = SG[...]
    SM[0:1, :] = sums[0]
    SM[1:2, :] = sums[1]

    def join(ks, devs):
        cps = [rcopy(SM, SML.at[k], sms.at[k], smr.at[k], dev) for k, dev in zip(ks, devs)]
        for cp in cps:
            cp.start()
        for cp in cps:
            cp.wait()
        tot = SM[...]
        for k in ks:
            tot = tot + SML[k]
        SM[...] = tot

    for t in range(10):
        for s in range(5):
            k = t - s
            if 0 <= k < 6:
                stages[s](order[k], False)
                if s < 4:
                    stages[s + 1](order[k], True)
        if t == 0:
            join([0], [sib])
        if t == 1:
            join([1], [xn])
        if t == 2:
            join([2], [yn])
        if t == 3:
            join([3, 4, 5], zn)
            SGO[...] = SM[...]


def layer(xs, xl, xp, cs, cl, counts, wqkv, wout, wup, wdown, sp):
    D = xs.shape[1]
    ns, nl = xs.shape[0], xl.shape[0]
    rs = -(-ns // 16) * 16
    rl = -(-nl // 16) * 16
    R = rs + rl
    RK = R + rl
    sds = jax.ShapeDtypeStruct
    smem = pl.BlockSpec(memory_space=pltpu.SMEM)
    return pl.pallas_call(
        layer_kernel,
        out_shape=(
            sds((ns, D), BF), sds((nl, D), BF), sds((6, 2, 2, 2, 4, 2, 48, D // 2), BF),
            sds((R, D), F32), sds((R, D), F32), sds((rl, D), BF), sds((16, D), F32),
        ),
        in_specs=[vm()] * 5 + [smem] + [vm()] * 5,
        out_specs=(vm(),) * 7,
        scratch_shapes=[
            pltpu.VMEM((RK, D), BF),
            pltpu.VMEM((R, D), BF),
            pltpu.VMEM((RK, D), BF),
            pltpu.VMEM((RK, 3 * D), BF),
            pltpu.VMEM((R, D), BF),
            pltpu.VMEM((R, D), BF),
            pltpu.VMEM((R, D), F32),
            pltpu.VMEM((R, D), BF),
            pltpu.VMEM((R, D), BF),
            pltpu.VMEM((D, D), F32),
            pltpu.VMEM((RK, 3 * D), BF),
            pltpu.VMEM((R, D), BF),
            pltpu.VMEM((R, D), BF),
            pltpu.VMEM((256, 128), F32),
            pltpu.VMEM((512, 128), F32),
            pltpu.VMEM((256, 128), F32),
            pltpu.VMEM((512, 128), F32),
            pltpu.VMEM((128, 256), F32),
            pltpu.VMEM((128, 512), F32),
            pltpu.VMEM((128, 256), F32),
            pltpu.VMEM((128, 512), F32),
            pltpu.VMEM((2, 2 * rl, rl), BF),
            pltpu.VMEM((rs, 128), F32),
            pltpu.VMEM((2 * rl, 128), F32),
        ],
        compiler_params=params(None, 63),
        name="layer",
    )(xs, xl, xp, cs, cl, counts, wqkv, wout, wup, wdown, sp)


def scatter(blocks, dh1, dmid, dh1p, xs, xl, sp, sg):
    D = xs.shape[1]
    n = D // 2
    rl = dh1p.shape[0]
    R = dh1.shape[0]
    sds = jax.ShapeDtypeStruct
    dma = pltpu.SemaphoreType.DMA
    return pl.pallas_call(
        scatter_kernel,
        out_shape=(
            sds((24, 3 * D), F32), sds((24, D), F32), sds((24, 4 * D), F32), sds((96, D), F32),
            sds(xs.shape, BF), sds(xl.shape, BF), sds(sg.shape, F32),
        ),
        in_specs=[vm()] * 8,
        out_specs=(vm(),) * 7,
        scratch_shapes=[
            pltpu.VMEM((R, D), BF),
            pltpu.VMEM((R, D), BF),
            pltpu.VMEM((rl, D), BF),
            pltpu.VMEM((6, 2, 2, 4, 2, 48, n), BF),
            pltpu.VMEM((6, 2, 4, 2, 48, n), BF),
            pltpu.VMEM((6, 4, 2, 48, n), BF),
            pltpu.VMEM((6, 3, 2, 48, n), BF),
            pltpu.VMEM((6, 2, 48, n), F32),
            pltpu.VMEM((6, 48, n), F32),
            pltpu.VMEM(sg.shape, F32),
            pltpu.VMEM((6,) + sg.shape, F32),
            dma((6, 7)), dma((6, 7)), dma((2,)), dma((6,)), dma((6,)),
        ],
        compiler_params=params(2),
        name="scatter",
    )(blocks, dh1, dmid, dh1p, xs, xl, sp, sg)


def shards(
    small_tokens, large_tokens, small_counts, large_counts, small_cot, large_cot,
    w_qkv, w_out, w_up, w_down, norm_params, proj_bias, up_bias,
):
    D = w_out.shape[1]
    ns, nl = small_tokens.shape[1], large_tokens.shape[1]
    me = lax.axis_index("dp") * 2 + lax.axis_index("seq")
    low = lambda v: v.astype(BF).astype(F32)
    k, m = norm_params.shape[1], up_bias.shape[0]
    small = jnp.zeros((16, D), F32)
    small = lax.dynamic_update_slice(small, jnp.concatenate([low(norm_params), low(proj_bias)]), (0, me * k))
    small = lax.dynamic_update_slice(small, low(up_bias)[None], (8 + me * m // D, me * m % D))
    xs, xl = small_tokens.reshape(ns, D), large_tokens.reshape(nl, D)
    cs, cl = small_cot.reshape(ns, D), large_cot.reshape(nl, D)
    counts = jnp.concatenate([small_counts, large_counts])
    fqkv, fout, fup, fdown, sp, xp = gather(w_qkv, w_out, w_up, w_down, small, xl)
    outs, outl, blocks, dh1, dmid, dh1p, sg = layer(xs, xl, xp, cs, cl, counts, fqkv, fout, fup, fdown, sp)
    gqkv, gout, gup, gdown, dxs, dxl, sg = scatter(blocks, dh1, dmid, dh1p, xs, xl, sp, sg)
    cols = lax.dynamic_slice(sg, (0, me * k), (8, k))
    gub = lax.dynamic_slice(sg, (8 + me * m // D, me * m % D), (1, m))[0]
    return (
        outs.reshape(small_tokens.shape), outl.reshape(large_tokens.shape),
        dxs.reshape(small_tokens.shape), dxl.reshape(large_tokens.shape),
        gqkv, gout, gup, gdown, cols[0:4], cols[4:8], gub,
    )


def norm_rows(values, gain, shift):
    centre = jnp.mean(values, -1, keepdims=True)
    centered = values - centre
    spread = jnp.mean(centered * centered, -1, keepdims=True)
    return centered * lax.rsqrt(spread + 1e-06) * gain + shift


def gelu_exact(values):
    return jax.nn.gelu(values, approximate=False)


def general_rows(left, right):
    return lax.dot_general(
        left, right, (((0,), (0,)), ((), ())), preferred_element_type=jnp.float32
    )


def general_cols(left, right):
    return lax.dot_general(
        left, right, (((1,), (1,)), ((), ())), preferred_element_type=jnp.float32
    )


def attend(query, key_part, value, valid_keys, factor):
    raw_scores = jnp.einsum("bqhe,bkhe->bhqk", query, key_part, preferred_element_type=jnp.float32)
    scaled = jnp.where(valid_keys[:, None, None, :], raw_scores * factor, -1e30)
    row_top = jnp.max(scaled, -1, keepdims=True)
    expo_rows = jnp.exp(scaled - row_top)
    totals = jnp.sum(expo_rows, -1, keepdims=True)
    probs_full = expo_rows / totals
    mixed = jnp.einsum(
        "bhqk,bkhe->bqhe",
        probs_full.astype(jnp.bfloat16),
        value,
        preferred_element_type=jnp.float32,
    )
    return (mixed, row_top + jnp.log(totals))


def attend_back(query, key_part, value, valid_keys, log_total, grad_mixed, factor):
    raw_scores = jnp.einsum("bqhe,bkhe->bhqk", query, key_part, preferred_element_type=jnp.float32)
    scaled = jnp.where(valid_keys[:, None, None, :], raw_scores * factor, -1e30)
    probs_full = jnp.exp(scaled - log_total)
    grad_value = jnp.einsum(
        "bhqk,bqhe->bkhe",
        probs_full.astype(jnp.bfloat16),
        grad_mixed,
        preferred_element_type=jnp.float32,
    )
    grad_probs = jnp.einsum(
        "bqhe,bkhe->bhqk", grad_mixed, value, preferred_element_type=jnp.float32
    )
    row_delta = jnp.sum(probs_full * grad_probs, -1, keepdims=True)
    grad_raw = (probs_full * (grad_probs - row_delta) * factor).astype(jnp.bfloat16)
    grad_query = jnp.einsum(
        "bhqk,bkhe->bqhe", grad_raw, key_part, preferred_element_type=jnp.float32
    )
    grad_key = jnp.einsum("bhqk,bqhe->bkhe", grad_raw, query, preferred_element_type=jnp.float32)
    return (grad_query, grad_key, grad_value)


def shards_general(
    small_tokens,
    large_tokens,
    small_counts,
    large_counts,
    small_cot,
    large_cot,
    w_qkv,
    w_out,
    w_up,
    w_down,
    norm_params,
    proj_bias,
    up_bias,
):
    gathered = (
        lax.all_gather(w_qkv.astype(jnp.bfloat16), ("dp", "seq"), axis=0, tiled=True),
        lax.all_gather(w_out.astype(jnp.bfloat16), ("dp", "seq"), axis=0, tiled=True),
        lax.all_gather(w_up.astype(jnp.bfloat16), ("dp", "seq"), axis=0, tiled=True),
        lax.all_gather(w_down.astype(jnp.bfloat16), ("dp", "seq"), axis=0, tiled=True),
        lax.all_gather(norm_params.astype(jnp.bfloat16), ("dp", "seq"), axis=1, tiled=True),
        lax.all_gather(proj_bias.astype(jnp.bfloat16), ("dp", "seq"), axis=1, tiled=True),
        lax.all_gather(up_bias.astype(jnp.bfloat16), ("dp", "seq"), axis=0, tiled=True),
    )
    full_qkv, full_out, full_up, full_down, full_norm, full_bias, full_upbias = gathered
    norm_vals = full_norm.astype(jnp.float32)
    bias_vals = full_bias.astype(jnp.float32)
    upbias_vals = full_upbias.astype(jnp.float32)
    factor = HEAD_DIM ** (-0.5)
    small_images, small_len, width_dim = small_tokens.shape
    half_len = large_tokens.shape[1]
    small_rows = small_images * small_len
    head_count = width_dim // HEAD_DIM
    rows_in = jnp.concatenate(
        [small_tokens.reshape(small_rows, width_dim), large_tokens.reshape(half_len, width_dim)]
    ).astype(jnp.float32)
    normed_one, norm_one_back = jax.vjp(norm_rows, rows_in, norm_vals[0], norm_vals[1])
    normed_one = normed_one.astype(jnp.bfloat16)
    qkv_bias = jnp.concatenate([bias_vals[0], jnp.zeros((width_dim,), jnp.float32), bias_vals[1]])
    qkv_rows = (
        jnp.dot(normed_one, full_qkv, preferred_element_type=jnp.float32) + qkv_bias
    ).astype(jnp.bfloat16)
    qkv_heads = qkv_rows.reshape(-1, 3, head_count, HEAD_DIM)
    small_heads = qkv_heads[:small_rows].reshape(small_images, small_len, 3, head_count, HEAD_DIM)
    query_small = small_heads[:, :, 0]
    key_small = small_heads[:, :, 1]
    value_small = small_heads[:, :, 2]
    valid_small = jnp.arange(small_len, dtype=jnp.int32)[None, :] < small_counts[:, None]
    large_heads = qkv_heads[small_rows:]
    query_large = large_heads[:, 0][None]
    key_whole, value_whole = (
        lax.all_gather(large_heads[:, 1], "seq", axis=0, tiled=True),
        lax.all_gather(large_heads[:, 2], "seq", axis=0, tiled=True),
    )
    key_large = key_whole[None]
    value_large = value_whole[None]
    valid_large = jnp.arange(key_whole.shape[0], dtype=jnp.int32)[None, :] < large_counts[:, None]
    mixed_small, total_small = attend(query_small, key_small, value_small, valid_small, factor)
    mixed_large, total_large = attend(query_large, key_large, value_large, valid_large, factor)
    mixed = jnp.concatenate(
        [mixed_small.reshape(small_rows, width_dim), mixed_large.reshape(half_len, width_dim)]
    ).astype(jnp.bfloat16)
    middle = rows_in + jnp.dot(mixed, full_out, preferred_element_type=jnp.float32) + bias_vals[2]
    normed_two, norm_two_back = jax.vjp(norm_rows, middle, norm_vals[2], norm_vals[3])
    normed_two = normed_two.astype(jnp.bfloat16)
    up_proj = jnp.dot(normed_two, full_up, preferred_element_type=jnp.float32) + upbias_vals
    act_full, gelu_back = jax.vjp(gelu_exact, up_proj)
    act_low = act_full.astype(jnp.bfloat16)
    result = middle + jnp.dot(act_low, full_down, preferred_element_type=jnp.float32) + bias_vals[3]
    result_low = result.astype(jnp.bfloat16)
    small_out = result_low[:small_rows].reshape(small_tokens.shape)
    large_out = result_low[small_rows:].reshape(large_tokens.shape)
    back_qkv, back_out, back_up, back_down = (full_qkv, full_out, full_up, full_down)
    grad_rows = jnp.concatenate(
        [small_cot.reshape(small_rows, width_dim), large_cot.reshape(half_len, width_dim)]
    )
    grad_rows_full = grad_rows.astype(jnp.float32)
    grad_down = general_rows(act_low, grad_rows)
    grad_bias_down = jnp.sum(grad_rows, 0, dtype=jnp.float32)
    grad_act = general_cols(grad_rows, back_down)
    (grad_hidden,) = gelu_back(grad_act)
    grad_hidden_low = grad_hidden.astype(jnp.bfloat16)
    grad_up = general_rows(normed_two, grad_hidden_low)
    grad_up_bias = jnp.sum(grad_hidden_low, 0, dtype=jnp.float32)
    grad_normed_two = general_cols(grad_hidden_low, back_up)
    grad_mid_norm, grad_gain_two, grad_shift_two = norm_two_back(grad_normed_two)
    grad_middle = grad_rows_full + grad_mid_norm
    grad_middle_low = grad_middle.astype(jnp.bfloat16)
    grad_out = general_rows(mixed, grad_middle_low)
    grad_bias_out = jnp.sum(grad_middle_low, 0, dtype=jnp.float32)
    grad_mixed = (
        general_cols(grad_middle_low, back_out).astype(jnp.bfloat16).reshape(-1, head_count, HEAD_DIM)
    )
    grad_mixed_small = grad_mixed[:small_rows].reshape(
        small_images, small_len, head_count, HEAD_DIM
    )
    grad_mixed_large = grad_mixed[small_rows:][None]
    gq_small, gk_small, gv_small = attend_back(
        query_small, key_small, value_small, valid_small, total_small, grad_mixed_small, factor
    )
    gq_large, gk_whole, gv_whole = attend_back(
        query_large, key_large, value_large, valid_large, total_large, grad_mixed_large, factor
    )
    gk_large, gv_large = (
        lax.psum_scatter(
            gk_whole[0].astype(jnp.bfloat16), "seq", scatter_dimension=0, tiled=True
        ).astype(jnp.float32),
        lax.psum_scatter(
            gv_whole[0].astype(jnp.bfloat16), "seq", scatter_dimension=0, tiled=True
        ).astype(jnp.float32),
    )
    grad_qkv_small = jnp.stack([gq_small, gk_small, gv_small], 2).reshape(small_rows, 3 * width_dim)
    grad_qkv_large = jnp.stack([gq_large[0], gk_large, gv_large], 1).reshape(
        half_len, 3 * width_dim
    )
    grad_qkv_low = jnp.concatenate([grad_qkv_small, grad_qkv_large]).astype(jnp.bfloat16)
    grad_qkv = general_rows(normed_one, grad_qkv_low)
    grad_bias_query = jnp.sum(grad_qkv_low[:, :width_dim], 0, dtype=jnp.float32)
    grad_bias_value = jnp.sum(grad_qkv_low[:, 2 * width_dim :], 0, dtype=jnp.float32)
    grad_normed_one = general_cols(grad_qkv_low, back_qkv)
    grad_in_norm, grad_gain_one, grad_shift_one = norm_one_back(grad_normed_one)
    grad_input = (grad_middle + grad_in_norm).astype(jnp.bfloat16)
    small_grad = grad_input[:small_rows].reshape(small_tokens.shape)
    large_grad = grad_input[small_rows:].reshape(large_tokens.shape)
    grad_norm_all = jnp.stack([grad_gain_one, grad_shift_one, grad_gain_two, grad_shift_two])
    grad_bias_all = jnp.stack([grad_bias_query, grad_bias_value, grad_bias_out, grad_bias_down])
    shard_qkv, shard_out, shard_up, shard_down, shard_norm, shard_bias, shard_up_bias = (
        lax.psum_scatter(grad_qkv, ("dp", "seq"), scatter_dimension=0, tiled=True),
        lax.psum_scatter(grad_out, ("dp", "seq"), scatter_dimension=0, tiled=True),
        lax.psum_scatter(grad_up, ("dp", "seq"), scatter_dimension=0, tiled=True),
        lax.psum_scatter(grad_down, ("dp", "seq"), scatter_dimension=0, tiled=True),
        lax.psum_scatter(grad_norm_all, ("dp", "seq"), scatter_dimension=1, tiled=True),
        lax.psum_scatter(grad_bias_all, ("dp", "seq"), scatter_dimension=1, tiled=True),
        lax.psum_scatter(grad_up_bias, ("dp", "seq"), scatter_dimension=0, tiled=True),
    )
    return (
        small_out,
        large_out,
        small_grad,
        large_grad,
        shard_qkv,
        shard_out,
        shard_up,
        shard_down,
        shard_norm,
        shard_bias,
        shard_up_bias,
    )


def solution(mesh):
    in_specs = (
        P(("dp", "seq"), None, None),
        P("dp", "seq", None),
        P(("dp", "seq")),
        P("dp"),
        P(("dp", "seq"), None, None),
        P("dp", "seq", None),
        P(("dp", "seq"), None),
        P(("dp", "seq"), None),
        P(("dp", "seq"), None),
        P(("dp", "seq"), None),
        P(None, ("dp", "seq")),
        P(None, ("dp", "seq")),
        P(("dp", "seq")),
    )
    out_specs = (
        P(("dp", "seq"), None, None),
        P("dp", "seq", None),
        P(("dp", "seq"), None, None),
        P("dp", "seq", None),
        P(("dp", "seq"), None),
        P(("dp", "seq"), None),
        P(("dp", "seq"), None),
        P(("dp", "seq"), None),
        P(None, ("dp", "seq")),
        P(None, ("dp", "seq")),
        P(("dp", "seq")),
    )
    body = shards if (mesh.shape["dp"], mesh.shape["seq"]) == (16, 2) else shards_general
    return jax.shard_map(body, mesh=mesh, in_specs=in_specs, out_specs=out_specs, check_vma=False)
```

```python
import functools

import jax
import jax.numpy as jnp
from jax import lax
from jax.experimental import pallas as pl
from jax.experimental.pallas import tpu as pltpu
from jax.sharding import PartitionSpec as P

HEAD_DIM = 64
MESH = pl.DeviceIdType.MESH
BF = jnp.bfloat16
F32 = jnp.float32


def dot(a, b):
    return lax.dot_general(a, b, (((1,), (0,)), ((), ())), preferred_element_type=F32)


def dot_rows(a, b):
    return lax.dot_general(a, b, (((0,), (0,)), ((), ())), preferred_element_type=F32)


def dot_cols(a, b):
    return lax.dot_general(a, b, (((1,), (1,)), ((), ())), preferred_element_type=F32)


def device(x, y, z, c):
    return ((z * 2 + y) * 2 + c, x)


def rcopy(src, dst, send, recv, dev):
    return pltpu.make_async_remote_copy(
        src_ref=src, dst_ref=dst, send_sem=send, recv_sem=recv, device_id=dev, device_id_type=MESH
    )


def shard_at(j):
    return j // 4, (j // 2) % 2, j % 2


def stack_halves(g):
    n = g.shape[1] // 2
    return jnp.concatenate([g[:, :n], g[:, n:]], axis=0)


def rows_of(i, size, base=0):
    return pl.ds(pl.multiple_of(base + i * size, 16), size)


def lanes_of(i, size, base=0):
    return pl.ds(pl.multiple_of(base + i * size, 128), size)


def normalize(v):
    centred = v - jnp.mean(v, -1, keepdims=True)
    scale = lax.rsqrt(jnp.mean(centred * centred, -1, keepdims=True) + 1e-06)
    return centred * scale, scale


def norm_back(v, gain, grad):
    unit, scale = normalize(v)
    lifted = grad * gain
    inner = jnp.mean(lifted * unit, -1, keepdims=True)
    return scale * (lifted - jnp.mean(lifted, -1, keepdims=True) - unit * inner), unit


def gelu_pair(h):
    p = 0.3275911 * 0.7071067811865476
    t = 1.0 / (1.0 + p * abs(h))
    e = jnp.exp(-0.5 * h * h)
    poly = ((((1.061405429 * t - 1.453152027) * t + 1.421413741) * t - 0.284496736) * t + 0.254829592) * t
    q = 0.5 * poly * e
    phi = jnp.where(h >= 0, 1.0 - q, q)
    return h * phi, phi + h * e * 0.3989422804014327


def total(v):
    return jnp.sum(v.astype(F32), 0, keepdims=True)


def heads_forward(Q, KV, MIX, LSE, bias, q0, nq, k0, nk, first, count, unroll=1):
    D = Q.shape[1]
    left = lax.broadcasted_iota(jnp.int32, (nq, 128), 1) < HEAD_DIM

    def pair(hp, _):
        q = Q[q0 : q0 + nq, lanes_of(hp, 128)] * jnp.asarray(HEAD_DIM**-0.5, BF)
        k = KV[k0 : k0 + nk, lanes_of(hp, 128)]
        v = KV[k0 : k0 + nk, lanes_of(hp, 128, D)]
        zero = jnp.zeros_like(q)
        outs = []
        for head in range(2):
            qm = jnp.where(left, q, zero) if head == 0 else jnp.where(left, zero, q)
            s = dot_cols(k, qm) + bias
            top = jnp.max(s, 0, keepdims=True)
            e = jnp.exp(s - top)
            tot = jnp.sum(e, 0, keepdims=True)
            outs.append(dot_rows(v, e.astype(BF)) * (1.0 / tot))
            LSE[pl.ds(2 * hp + head, 1), 0:nq] = top + jnp.log(tot)
        both = jnp.concatenate([outs[0][:HEAD_DIM], outs[1][HEAD_DIM:]], axis=0)
        MIX[q0 : q0 + nq, lanes_of(hp, 128)] = jnp.transpose(both).astype(BF)
        return 0

    lax.fori_loop(first, first + count, pair, 0, unroll=unroll)


def heads_backward(Q, KV, MIX, DMIX, LSE, bias, q0, nq, k0, nk, first, count, unroll=1):
    D = Q.shape[1]
    left = lax.broadcasted_iota(jnp.int32, (nq, 128), 1) < HEAD_DIM
    leftk = lax.broadcasted_iota(jnp.int32, (nk, 128), 1) < HEAD_DIM

    def pair(hp, _):
        q = Q[q0 : q0 + nq, lanes_of(hp, 128)] * jnp.asarray(HEAD_DIM**-0.5, BF)
        dm = DMIX[q0 : q0 + nq, lanes_of(hp, 128)]
        k = KV[k0 : k0 + nk, lanes_of(hp, 128)]
        v = KV[k0 : k0 + nk, lanes_of(hp, 128, D)]
        zero = jnp.zeros_like(q)
        weighted = jnp.transpose(dm.astype(F32) * MIX[q0 : q0 + nq, lanes_of(hp, 128)].astype(F32))
        dqs, dks, dvs = [], [], []
        for head in range(2):
            mask = lambda u: jnp.where(left, u, zero) if head == 0 else jnp.where(left, zero, u)
            delta = jnp.sum(weighted[head * HEAD_DIM : (head + 1) * HEAD_DIM], 0, keepdims=True)
            s = dot_cols(k, mask(q)) + bias
            pr = jnp.exp(s - LSE[pl.ds(2 * hp + head, 1), 0:nq])
            dvs.append(dot(pr.astype(BF), dm))
            ds = (pr * (dot_cols(v, mask(dm)) - delta)).astype(BF)
            dks.append(dot(ds, q))
            dqs.append(dot_rows(k, ds))
        both = jnp.concatenate([dqs[0][:HEAD_DIM], dqs[1][HEAD_DIM:]], axis=0) * HEAD_DIM**-0.5
        Q[q0 : q0 + nq, lanes_of(hp, 128)] = jnp.transpose(both).astype(BF)
        KV[k0 : k0 + nk, lanes_of(hp, 128)] = jnp.where(leftk, dks[0], dks[1]).astype(BF)
        KV[k0 : k0 + nk, lanes_of(hp, 128, D)] = jnp.where(leftk, dvs[0], dvs[1]).astype(BF)
        return 0

    lax.fori_loop(first, first + count, pair, 0, unroll=unroll)


def store_block(g, SP, w, h):
    for j in range(16):
        z, y, c = shard_at(j)
        for x in range(2):
            r = 48 * j + 24 * x
            SP[w, h, x, y, z, c] = stack_halves(g[r : r + 24]).astype(BF)


def store_down(g, SP, f):
    n = SP.shape[-1]
    for j in range(4):
        for x in range(2):
            for half in range(2):
                r = (2 * j + x) * 96 + 48 * half
                for h in range(2):
                    SP[2 + half, h, x, j // 2, f, j % 2] = g[r : r + 48, h * n : h * n + n].astype(BF)


def layer_kernel(
    xs, xl, cs, cl, count_s, count_l, wqkv, wout, wup, wdown, norm, bias, upbias,
    OUT, DX, gqkv, gout, gup, gdown, SGO,
    X, DY, H1, Q, KV, MIX, MID, H2, ACC, DH2, ACT, DHB, DH1P, LP, LSES, LSEL,
    WQKV, WOUT, WUP, WDOWN, SP, OWN, LC, T, LF, sp, sm, sml, SG, SGL,
    ss, rs, tsem, psem, sms, smr, gs, gr, s2, r2, credit, room,
):
    d = lax.axis_index("dp")
    x, y, z, c = lax.axis_index("seq"), (d // 2) % 2, d // 4, d % 2
    zs = [(z + k) % 4 for k in (1, 2, 3)]
    sib, xn, yn = device(x, y, z, 1 - c), device(1 - x, y, z, c), device(x, 1 - y, z, c)
    zn = [device(x, y, k, c) for k in zs]
    bar = pltpu.get_barrier_semaphore()
    for p in [sib, xn, yn] + zn:
        pl.semaphore_signal(bar, inc=1, device_id=p, device_id_type=MESH)

    D = xs.shape[1]
    n = D // 2
    ns, nl = xs.shape[0], xl.shape[0]
    r1 = -(-ns // 16) * 16
    rl = -(-nl // 16) * 16
    R = r1 + rl
    RK = R + rl
    RB = 32
    zero = functools.partial(jnp.zeros, dtype=BF)
    head = ns - ns % 16

    X[head:r1, :] = zero((r1 - head, D))
    X[R - 16 : R, :] = zero((16, D))
    X[0:ns, :] = xs[...]
    X[r1 : r1 + nl, :] = xl[...]

    blocks = [wqkv[:, k * D : (k + 1) * D] for k in range(3)] + [wout[...]]
    blocks = [stack_halves(g) for g in blocks]
    blocks += [wdown[48 * (b // 2) : 48 * (b // 2) + 48, (b % 2) * n : (b % 2) * n + n] for b in range(4)]
    blocks += [stack_halves(wup[:, k * D : (k + 1) * D]) for k in range(4)]
    for b, g in enumerate(blocks):
        OWN[b // 2, b % 2] = g.astype(BF)
    for w in range(6):
        SP[w, c, x, y, z, c] = OWN[w, c]
    pl.semaphore_wait(bar, 6)
    swaps = [rcopy(OWN.at[w, 1 - c], SP.at[w, 1 - c, x, y, z, c], ss.at[w, 0], rs.at[w, 0], sib) for w in range(6)]
    for cp in swaps:
        cp.start()
    tcp = rcopy(X.at[r1:R], X.at[R:RK], tsem.at[0], tsem.at[1], xn)
    tcp.start()

    me = d * 2 + x
    k, m = norm.shape[1], upbias.shape[1]

    def placed(v, start):
        wide = jnp.concatenate([v, jnp.zeros((v.shape[0], D - v.shape[1]), F32)], axis=1)
        return pltpu.roll(wide, start, 1)

    row = lax.broadcasted_iota(jnp.int32, (8, D), 0)
    both = jnp.concatenate([norm[...], bias[...]], axis=0).astype(BF).astype(F32)
    sm[0:8, :] = placed(both, me * k)
    ub = placed(jnp.broadcast_to(upbias[...].astype(BF).astype(F32), (8, m)), lax.rem(me * m, D))
    sm[8:16, :] = jnp.where(row == (me * m) // D, ub, 0.0)

    def join(buf, land, send, recv, ks, devs):
        cps = [rcopy(buf, land.at[i], send.at[i], recv.at[i], dev) for i, dev in zip(ks, devs)]

        def start():
            for cp in cps:
                cp.start()

        def finish():
            for cp in cps:
                cp.wait()
            tot = buf[...]
            for i in ks:
                tot = tot + land[i]
            buf[...] = tot

        return start, finish

    def joins(buf, land, send, recv):
        return [
            join(buf, land, send, recv, *a) for a in (([0], [sib]), ([1], [xn]), ([2], [yn]), ([3, 4, 5], zn))
        ]

    smalls = joins(sm, sml, sms, smr)

    def zsend(w, i):
        src = SP.at[w, c, x, y, z]
        return rcopy(src, src, ss.at[w, 1 + i], rs.at[w, 1 + i], zn[i])

    def zrecv(w, i):
        dst = SP.at[w, c, x, y, zs[i]]
        return rcopy(dst, dst, ss.at[w, 3 - i], rs.at[w, 3 - i], zn[i])

    def a1(w):
        swaps[w].wait()
        for i in range(3):
            zsend(w, i).start()

    def hop(w, sem, cases, start):
        for core, (dev, src, dst) in enumerate(cases):

            def go(dev=dev, src=src, dst=dst):
                if start:
                    rcopy(src, src, ss.at[w, sem], rs.at[w, sem], dev).start()
                else:
                    cp = rcopy(src, dst, ss.at[w, sem], rs.at[w, sem], dev)
                    cp.wait_send()
                    cp.wait_recv()

            pl.when(c == core)(go)

    def cases2(w):
        src = SP.at[w, c, x, y]
        return (xn, src, SP.at[w, c, 1 - x, y]), (yn, src, SP.at[w, c, x, 1 - y])

    def cases3(w):
        return (
            (yn, SP.at[w, c, :, y], SP.at[w, c, :, 1 - y]),
            (xn, SP.at[w, c, x], SP.at[w, c, 1 - x]),
        )

    def a2(w):
        for i in range(3):
            zsend(w, i).wait_send()
            zrecv(w, i).wait_recv()
        hop(w, 4, cases2(w), True)

    def a3(w):
        hop(w, 4, cases2(w), False)
        hop(w, 5, cases3(w), True)

    def a4(w):
        hop(w, 5, cases3(w), False)
        src = SP.at[w, c]
        rcopy(src, src, ss.at[w, 6], rs.at[w, 6], sib).start()

    def assemble(w, h, dst, col):
        def step(j, _):
            pz, py, pc = shard_at(j)
            a = SP[w, h, 0, py, pz, pc].astype(F32)
            e = SP[w, h, 1, py, pz, pc].astype(F32)
            dst[rows_of(j, 48), col : col + n] = jnp.concatenate([a[:24], e[:24]], axis=0).astype(BF)
            dst[rows_of(j, 48), col + n : col + D] = jnp.concatenate([a[24:], e[24:]], axis=0).astype(BF)
            return 0

        lax.fori_loop(0, 16, step, 0, unroll=4)

    def assemble_down(w, h):
        def step(j, _):
            pz, py, pc = shard_at(j)
            for px in range(2):
                rows = pl.ds(pl.multiple_of(96 * (2 * j + px) + 48 * (w - 2), 16), 48)
                WDOWN[rows, n * h : n * h + n] = SP[w, h, px, py, pz, pc]
            return 0

        lax.fori_loop(0, 16, step, 0, unroll=4)

    def a5(w):
        src, dst = SP.at[w, c], SP.at[w, 1 - c]
        rcopy(src, src, ss.at[w, 6], rs.at[w, 6], sib).wait_send()
        rcopy(dst, dst, ss.at[w, 6], rs.at[w, 6], sib).wait_recv()
        for h in range(2):
            b = 2 * w + h
            if b < 3:
                assemble(w, h, WQKV, b * D)
            elif b == 3:
                assemble(w, h, WOUT, 0)
            elif b < 8:
                assemble_down(w, h)
            else:
                assemble(w, h, WUP, (b - 8) * D)

    def credits(w):
        for i, dev in enumerate([xn, yn] + zn):
            pl.semaphore_signal(room.at[i], inc=1, device_id=dev, device_id_type=MESH)

    order = [4, 5, 2, 3, 1, 0]

    def add(w, dst, src, count):
        def step(i, _):
            at = (w, c) + dst(i)
            SP[at] = (SP[at].astype(F32) + src(i).astype(F32)).astype(BF)
            return 0

        lax.fori_loop(0, count, step, 0, unroll=4)

    def first_copy(i):
        w = order[i]
        return rcopy(SP.at[w, 1 - c], LC.at[i % 2], s2.at[w, 0], r2.at[w, 0], sib)

    def go(i):
        if i >= 2:
            pl.semaphore_wait(credit, 1)
        first_copy(i).start()

    def cases_b(w, stage):
        land = SP.at[w, 1 - c]
        if stage == 1:
            return (yn, SP.at[w, c, :, 1 - y], land.at[0]), (xn, SP.at[w, c, 1 - x], land.at[0])
        return (xn, SP.at[w, c, 1 - x, y], land.at[1, 0]), (yn, SP.at[w, c, x, 1 - y], land.at[1, 0])

    def back_hop(w, stage, start):
        for core, (dev, src, dst) in enumerate(cases_b(w, stage)):

            def run(dev=dev, src=src, dst=dst, core=core):
                cp = rcopy(src, dst, s2.at[w, stage], r2.at[w, stage], dev)
                if start:
                    pl.semaphore_wait(room.at[1 - core if stage == 1 else core], 1)
                    cp.start()
                    return
                cp.wait()
                if stage == 1:
                    place = (lambda i: (i // 8, y, (i // 2) % 4, i % 2)) if core == 0 else (
                        lambda i: (x, i // 8, (i // 2) % 4, i % 2)
                    )
                    add(w, place, lambda i: SP[w, 1 - c, 0, i // 8, (i // 2) % 4, i % 2], 16)
                else:
                    add(w, lambda i: (x, y, i // 2, i % 2), lambda i: SP[w, 1 - c, 1, 0, i // 2, i % 2], 8)

            pl.when(c == core)(run)

    def zback(w, i):
        return rcopy(SP.at[w, c, x, y, zs[i]], SP.at[w, 1 - c, 1, 1, i], s2.at[w, 3 + i], r2.at[w, 3 + i], zn[i])

    def last_copy(w):
        return rcopy(T.at[w, 1 - c], LF.at[w], s2.at[w, 6], r2.at[w, 6], sib)

    def deliver(w):
        mine, other = T[w, c], LF[w]
        for h in range(2):
            g = jnp.where(c == h, mine, other)
            b = 2 * w + h
            if 4 <= b < 8:
                half = (b - 4) // 2
                gdown[48 * half : 48 * half + 48, n * h : n * h + n] = g
                continue
            wide = jnp.concatenate([g[0:24], g[24:48]], axis=1)
            if b >= 8:
                gup[:, (b - 8) * D : (b - 7) * D] = wide
            elif b == 2:
                gout[...] = wide
            else:
                g0 = (3, 2, None, 1)[b] - 1
                third = D // 3
                for part in range(3):
                    lo = part * D + g0 * third
                    gqkv[:, lo : lo + third] = wide[:, part * third : (part + 1) * third]

    def back(i, stage):
        w = order[i]
        if stage == 0:
            first_copy(i).wait()
            idx = lambda j: (j // 16, (j // 8) % 2, (j // 2) % 4, j % 2)
            add(w, idx, lambda j: LC[(i % 2,) + idx(j)], 32)
            if i < 4:
                pl.semaphore_signal(credit, inc=1, device_id=sib, device_id_type=MESH)
            credits(w)
            back_hop(w, 1, True)
        elif stage == 1:
            back_hop(w, 1, False)
            back_hop(w, 2, True)
        elif stage == 2:
            back_hop(w, 2, False)
            for j in range(3):
                pl.semaphore_wait(room.at[2 + 2 - j], 1)
                zback(w, j).start()
        elif stage == 3:
            for j in range(3):
                zback(w, j).wait()
            for q in range(2):
                tot = SP[w, c, x, y, z, q].astype(F32)
                for j in range(3):
                    tot = tot + SP[w, 1 - c, 1, 1, j, q].astype(F32)
                T[w, q] = tot
            last_copy(w).start()
        else:
            last_copy(w).wait()
            deliver(w)

    def norm_one(base, count):
        def step(i, _):
            rows = rows_of(i, 16, base)
            unit, _ = normalize(X[rows, :].astype(F32))
            H1[rows, :] = (unit * sp[0:1, :] + sp[1:2, :]).astype(BF)
            return 0

        lax.fori_loop(0, count // 16, step, 0, unroll=2)

    small_count, large_count = count_s[0], count_l[0]
    kj = lax.broadcasted_iota(jnp.int32, (r1, 1), 0)
    bias_small = jnp.where(kj < small_count, 0.0, -1e30)
    kj = lax.broadcasted_iota(jnp.int32, (2 * rl, 1), 0)
    mine = kj < rl
    inside = jnp.where(mine, kj, kj - rl)
    where = inside + jnp.where(mine, x, 1 - x) * nl
    bias_large = jnp.where((inside < nl) & (where < large_count), 0.0, -1e30)
    small_part = (bias_small, 0, r1, 0, r1)
    large_part = (bias_large, r1, rl, r1, 2 * rl)

    a1(0)
    smalls[0][0]()
    DY[head:r1, :] = zero((r1 - head, D))
    DY[R - 16 : R, :] = zero((16, D))
    DY[0:ns, :] = cs[...]
    DY[r1 : r1 + nl, :] = cl[...]
    SG[...] = jnp.zeros(SG.shape, F32)
    smalls[0][1]()
    smalls[1][0]()
    a2(0)
    a1(1)
    smalls[1][1]()
    smalls[2][0]()
    a3(0)
    smalls[2][1]()
    smalls[3][0]()
    a2(1)
    a1(2)
    smalls[3][1]()
    sp[...] = sm[...]
    norm_one(0, R)
    a4(0)
    a3(1)
    a2(2)
    a1(3)
    tcp.wait()
    norm_one(R, rl)
    a5(0)
    Q[...] = (dot(H1[0:R, :], WQKV[:, 0:D]) + sp[4:5, :]).astype(BF)
    KV[:, 0:D] = dot(H1[...], WQKV[:, D : 2 * D]).astype(BF)
    a4(1)
    a3(2)
    a2(3)
    a1(4)
    a5(1)
    KV[:, D:] = (dot(H1[...], WQKV[:, 2 * D :]) + sp[5:6, :]).astype(BF)
    heads_forward(Q, KV, MIX, LSES, *small_part, 0, 6, unroll=2)
    heads_forward(Q, KV, MIX, LSEL, *large_part, 0, 2)
    a4(2)
    a3(3)
    a2(4)
    a1(5)
    heads_forward(Q, KV, MIX, LSEL, *large_part, 2, 2)
    a5(2)
    heads_forward(Q, KV, MIX, LSEL, *large_part, 4, 2)
    a4(3)
    a3(4)
    a2(5)

    MID[...] = dot(MIX[...], WOUT[...])

    def norm_two(i, _):
        rows = rows_of(i, RB)
        middle = X[rows, :].astype(F32) + MID[rows, :] + sp[6:7, :]
        MID[rows, :] = middle
        unit, _ = normalize(middle)
        H2[rows, :] = (unit * sp[2:3, :] + sp[3:4, :]).astype(BF)
        ACC[rows, :] = middle + sp[7:8, :]
        return 0

    lax.fori_loop(0, R // RB, norm_two, 0)
    DH2[...] = jnp.zeros(DH2.shape, F32)
    a5(3)
    a4(4)
    a3(5)
    a5(4)

    def quarter(f, between):
        fl, fr = slice(f * D, (f + 1) * D), slice(f * D, (f + 1) * D)
        hidden = dot(H2[...], WUP[:, fl]) + sp[8 + f : 9 + f, :]
        dact = dot_cols(DY[...], WDOWN[fr, :])
        act, slope = gelu_pair(hidden)
        ACT[...] = act.astype(BF)
        dh = (dact * slope).astype(BF)
        DHB[...] = dh
        SG[8 + f : 9 + f, :] = total(dh)
        between()
        store_block(dot_rows(H2[...], DHB[...]), SP, 4 + f // 2, f % 2)
        store_down(dot_rows(ACT[...], DY[...]), SP, f)
        ACC[...] += dot(ACT[...], WDOWN[fr, :])
        DH2[...] += dot_cols(DHB[...], WUP[:, fl])

    nothing = lambda: None
    quarter(0, nothing)
    a4(5)
    quarter(1, nothing)
    go(0)
    a5(5)
    quarter(2, lambda: back(0, 0))
    back(0, 1)
    quarter(3, lambda: back(0, 2))
    go(1)
    go(2)
    back(0, 3)
    OUT[...] = ACC[...].astype(BF)

    def back_two(i, sums):
        rows = rows_of(i, RB)
        grad = DH2[rows, :]
        dy = DY[rows, :].astype(F32)
        dv, unit = norm_back(MID[rows, :], sp[2:3, :], grad)
        dmid = dy + dv
        MID[rows, :] = dmid
        low = dmid.astype(BF)
        H2[rows, :] = low
        return sums[0] + total(grad * unit), sums[1] + total(grad), sums[2] + total(low), sums[3] + total(dy)

    z1 = jnp.zeros((1, D), F32)
    sums = lax.fori_loop(0, R // RB, back_two, (z1, z1, z1, z1))
    for i, at in enumerate((2, 3, 6, 7)):
        SG[at : at + 1, :] = sums[i]
    back(1, 0)
    back(2, 0)
    go(3)
    ACT[...] = dot_cols(H2[...], WOUT[...]).astype(BF)
    store_block(dot_rows(MIX[...], H2[...]), SP, 1, 0)
    back(0, 4)
    back(1, 1)
    back(3, 0)

    third = D // 3

    def group(g, w, h, between):
        heads_backward(Q, KV, MIX, ACT, LSES, *small_part, 2 * g, 2, unroll=2)
        heads_backward(Q, KV, MIX, ACT, LSEL, *large_part, 2 * g, 1)
        between()
        heads_backward(Q, KV, MIX, ACT, LSEL, *large_part, 2 * g + 1, 1)
        lo = slice(g * third, (g + 1) * third)
        lov = slice(D + g * third, D + (g + 1) * third)
        parts = [dot_rows(H1[0:R, :], Q[:, lo]), dot_rows(H1[...], KV[:, lo]), dot_rows(H1[...], KV[:, lov])]
        store_block(jnp.concatenate(parts, axis=1), SP, w, h)

    def mid0():
        back(1, 2)
        back(2, 1)

    group(0, 1, 1, mid0)
    go(4)
    back(1, 3)
    back(2, 2)
    back(3, 1)

    def mid1():
        back(4, 0)
        back(1, 4)
        back(2, 3)
        back(3, 2)

    group(1, 0, 1, mid1)
    back(4, 1)
    back(2, 4)
    back(3, 3)

    def mid2():
        back(4, 2)
        back(3, 4)

    group(2, 0, 0, mid2)
    go(5)
    back(4, 3)
    DH1P[...] = (dot_cols(KV[R:RK, 0:D], WQKV[:, D : 2 * D]) + dot_cols(KV[R:RK, D:], WQKV[:, 2 * D :])).astype(BF)
    pcp = rcopy(DH1P, LP, psem.at[0], psem.at[1], xn)
    pcp.start()
    back(5, 0)
    ACC[...] = dot_cols(Q[...], WQKV[:, 0:D]) + dot_cols(KV[0:R, 0:D], WQKV[:, D : 2 * D])
    ACC[...] += dot_cols(KV[0:R, D:], WQKV[:, 2 * D :])
    back(4, 4)
    back(5, 1)

    def back_one(base, partner):
        def step(i, _):
            rows = rows_of(i, 16, base)
            grad = ACC[rows, :]
            if partner:
                grad = grad + LP[rows_of(i, 16), :].astype(F32)
            dv, _ = norm_back(X[rows, :].astype(F32), sp[0:1, :], grad)
            DX[rows, :] = (MID[rows, :] + dv).astype(BF)
            return 0

        return step

    def norm_sums(base, grads, gbase):
        def step(i, sums):
            unit, _ = normalize(X[rows_of(i, 16, base), :].astype(F32))
            grad = grads[rows_of(i, 16, gbase), :].astype(F32)
            return sums[0] + total(grad * unit), sums[1] + total(grad)

        return step

    sums = lax.fori_loop(0, R // 16, norm_sums(0, ACC, 0), (z1, z1), unroll=2)
    sums = lax.fori_loop(0, rl // 16, norm_sums(R, DH1P, 0), sums)
    SG[0:1, :] = sums[0]
    SG[1:2, :] = sums[1]
    SG[4:5, :] = total(Q[...])
    SG[5:6, :] = total(KV[:, D:])
    ends = joins(SG, SGL, gs, gr)
    ends[0][0]()
    back(5, 2)
    ends[0][1]()
    ends[1][0]()
    lax.fori_loop(0, r1 // 16, back_one(0, False), 0)
    ends[1][1]()
    ends[2][0]()
    pcp.wait()
    lax.fori_loop(0, rl // 16, back_one(r1, True), 0)
    back(5, 3)
    ends[2][1]()
    ends[3][0]()
    back(5, 4)
    ends[3][1]()
    SGO[...] = SG[...]


def deliver_kernel(
    OUT, DX, gqkv, gout, gup, gdown, SG,
    outs, outl, dxs, dxl, oqkv, oout, oup, odown, onorm, obias, oub,
):
    ns, nl = outs.shape[0], outl.shape[0]
    r1 = -(-ns // 16) * 16
    outs[...] = OUT[0:ns, :]
    outl[...] = OUT[r1 : r1 + nl, :]
    dxs[...] = DX[0:ns, :]
    dxl[...] = DX[r1 : r1 + nl, :]
    oqkv[...] = gqkv[...]
    oout[...] = gout[...]
    oup[...] = gup[...]
    odown[...] = gdown[...]
    D = outs.shape[1]
    me = lax.axis_index("dp") * 2 + lax.axis_index("seq")
    k, m = onorm.shape[1], oub.shape[1]
    near = pltpu.roll(SG[0:8, :], lax.rem(D - me * k, D), 1)[:, 0:k]
    onorm[...] = near[0:4]
    obias[...] = near[4:8]
    row = lax.broadcasted_iota(jnp.int32, (8, D), 0)
    picked = total(jnp.where(row == (me * m) // D, SG[8:16, :], 0.0))
    near = pltpu.roll(jnp.broadcast_to(picked, (8, D)), lax.rem(D - lax.rem(me * m, D), D), 1)
    oub[...] = near[0:1, 0:m]


def vm():
    return pl.BlockSpec(memory_space=pltpu.VMEM)


def layer(xs, xl, cs, cl, count_s, count_l, wqkv, wout, wup, wdown, norm, bias, upbias):
    D = xs.shape[1]
    n = D // 2
    r1 = -(-xs.shape[0] // 16) * 16
    rl = -(-xl.shape[0] // 16) * 16
    R = r1 + rl
    RK = R + rl
    sds = jax.ShapeDtypeStruct
    smem = pl.BlockSpec(memory_space=pltpu.SMEM)
    dma, regular = pltpu.SemaphoreType.DMA, pltpu.SemaphoreType.REGULAR
    small = (16, D)
    return pl.pallas_call(
        layer_kernel,
        out_shape=(
            sds((R, D), BF), sds((R, D), BF),
            sds(wqkv.shape, F32), sds(wout.shape, F32), sds(wup.shape, F32), sds(wdown.shape, F32), sds(small, F32),
        ),
        in_specs=[vm()] * 4 + [smem] * 2 + [vm()] * 7,
        out_specs=(vm(),) * 7,
        scratch_shapes=[
            pltpu.VMEM((RK, D), BF),
            pltpu.VMEM((R, D), BF),
            pltpu.VMEM((RK, D), BF),
            pltpu.VMEM((R, D), BF),
            pltpu.VMEM((RK, 2 * D), BF),
            pltpu.VMEM((R, D), BF),
            pltpu.VMEM((R, D), F32),
            pltpu.VMEM((R, D), BF),
            pltpu.VMEM((R, D), F32),
            pltpu.VMEM((R, D), F32),
            pltpu.VMEM((R, D), BF),
            pltpu.VMEM((R, D), BF),
            pltpu.VMEM((rl, D), BF),
            pltpu.VMEM((rl, D), BF),
            pltpu.VMEM((16, r1), F32),
            pltpu.VMEM((16, rl), F32),
            pltpu.VMEM((D, 3 * D), BF),
            pltpu.VMEM((D, D), BF),
            pltpu.VMEM((D, 4 * D), BF),
            pltpu.VMEM((4 * D, D), BF),
            pltpu.VMEM((6, 2, 2, 2, 4, 2, 48, n), BF),
            pltpu.VMEM((6, 2, 48, n), BF),
            pltpu.VMEM((2, 2, 2, 4, 2, 48, n), BF),
            pltpu.VMEM((6, 2, 48, n), F32),
            pltpu.VMEM((6, 48, n), F32),
            pltpu.VMEM(small, F32),
            pltpu.VMEM(small, F32),
            pltpu.VMEM((6,) + small, F32),
            pltpu.VMEM(small, F32),
            pltpu.VMEM((6,) + small, F32),
            dma((6, 7)), dma((6, 7)), dma((2,)), dma((2,)), dma((6,)), dma((6,)), dma((6,)), dma((6,)),
            dma((6, 7)), dma((6, 7)), regular, regular((5,)),
        ],
        compiler_params=pltpu.CompilerParams(collective_id=1, has_side_effects=True, vmem_limit_bytes=63 << 20),
        name="layer",
    )(xs, xl, cs, cl, count_s, count_l, wqkv, wout, wup, wdown, norm, bias, upbias)


def shards(
    small_tokens, large_tokens, small_counts, large_counts, small_cot, large_cot,
    w_qkv, w_out, w_up, w_down, norm_params, proj_bias, up_bias,
):
    flat = lambda v: v.reshape(v.shape[1:])
    xs, xl, cs, cl = flat(small_tokens), flat(large_tokens), flat(small_cot), flat(large_cot)
    made = layer(
        xs, xl, cs, cl, small_counts, large_counts, w_qkv, w_out, w_up, w_down, norm_params, proj_bias, up_bias[None]
    )
    like = (xs, xl, xs, xl, w_qkv, w_out, w_up, w_down, norm_params, proj_bias, up_bias[None])
    outs, outl, dxs, dxl, gqkv, gout, gup, gdown, gnorm, gbias, gub = pl.pallas_call(
        deliver_kernel,
        out_shape=tuple(jax.ShapeDtypeStruct(v.shape, v.dtype) for v in like),
        in_specs=[vm()] * 7,
        out_specs=(vm(),) * 11,
        compiler_params=pltpu.CompilerParams(vmem_limit_bytes=32 << 20),
        name="deliver",
    )(*made)
    return outs[None], outl[None], dxs[None], dxl[None], gqkv, gout, gup, gdown, gnorm, gbias, gub[0]


def norm_rows(values, gain, shift):
    centre = jnp.mean(values, -1, keepdims=True)
    centered = values - centre
    spread = jnp.mean(centered * centered, -1, keepdims=True)
    return centered * lax.rsqrt(spread + 1e-06) * gain + shift


def gelu_exact(values):
    return jax.nn.gelu(values, approximate=False)


def general_rows(left, right):
    return lax.dot_general(
        left, right, (((0,), (0,)), ((), ())), preferred_element_type=jnp.float32
    )


def general_cols(left, right):
    return lax.dot_general(
        left, right, (((1,), (1,)), ((), ())), preferred_element_type=jnp.float32
    )


def attend(query, key_part, value, valid_keys, factor):
    raw_scores = jnp.einsum("bqhe,bkhe->bhqk", query, key_part, preferred_element_type=jnp.float32)
    scaled = jnp.where(valid_keys[:, None, None, :], raw_scores * factor, -1e30)
    row_top = jnp.max(scaled, -1, keepdims=True)
    expo_rows = jnp.exp(scaled - row_top)
    totals = jnp.sum(expo_rows, -1, keepdims=True)
    probs_full = expo_rows / totals
    mixed = jnp.einsum(
        "bhqk,bkhe->bqhe",
        probs_full.astype(jnp.bfloat16),
        value,
        preferred_element_type=jnp.float32,
    )
    return (mixed, row_top + jnp.log(totals))


def attend_back(query, key_part, value, valid_keys, log_total, grad_mixed, factor):
    raw_scores = jnp.einsum("bqhe,bkhe->bhqk", query, key_part, preferred_element_type=jnp.float32)
    scaled = jnp.where(valid_keys[:, None, None, :], raw_scores * factor, -1e30)
    probs_full = jnp.exp(scaled - log_total)
    grad_value = jnp.einsum(
        "bhqk,bqhe->bkhe",
        probs_full.astype(jnp.bfloat16),
        grad_mixed,
        preferred_element_type=jnp.float32,
    )
    grad_probs = jnp.einsum(
        "bqhe,bkhe->bhqk", grad_mixed, value, preferred_element_type=jnp.float32
    )
    row_delta = jnp.sum(probs_full * grad_probs, -1, keepdims=True)
    grad_raw = (probs_full * (grad_probs - row_delta) * factor).astype(jnp.bfloat16)
    grad_query = jnp.einsum(
        "bhqk,bkhe->bqhe", grad_raw, key_part, preferred_element_type=jnp.float32
    )
    grad_key = jnp.einsum("bhqk,bqhe->bkhe", grad_raw, query, preferred_element_type=jnp.float32)
    return (grad_query, grad_key, grad_value)


def shards_general(
    small_tokens,
    large_tokens,
    small_counts,
    large_counts,
    small_cot,
    large_cot,
    w_qkv,
    w_out,
    w_up,
    w_down,
    norm_params,
    proj_bias,
    up_bias,
):
    gathered = (
        lax.all_gather(w_qkv.astype(jnp.bfloat16), ("dp", "seq"), axis=0, tiled=True),
        lax.all_gather(w_out.astype(jnp.bfloat16), ("dp", "seq"), axis=0, tiled=True),
        lax.all_gather(w_up.astype(jnp.bfloat16), ("dp", "seq"), axis=0, tiled=True),
        lax.all_gather(w_down.astype(jnp.bfloat16), ("dp", "seq"), axis=0, tiled=True),
        lax.all_gather(norm_params.astype(jnp.bfloat16), ("dp", "seq"), axis=1, tiled=True),
        lax.all_gather(proj_bias.astype(jnp.bfloat16), ("dp", "seq"), axis=1, tiled=True),
        lax.all_gather(up_bias.astype(jnp.bfloat16), ("dp", "seq"), axis=0, tiled=True),
    )
    full_qkv, full_out, full_up, full_down, full_norm, full_bias, full_upbias = gathered
    norm_vals = full_norm.astype(jnp.float32)
    bias_vals = full_bias.astype(jnp.float32)
    upbias_vals = full_upbias.astype(jnp.float32)
    factor = HEAD_DIM ** (-0.5)
    small_images, small_len, width_dim = small_tokens.shape
    half_len = large_tokens.shape[1]
    small_rows = small_images * small_len
    head_count = width_dim // HEAD_DIM
    rows_in = jnp.concatenate(
        [small_tokens.reshape(small_rows, width_dim), large_tokens.reshape(half_len, width_dim)]
    ).astype(jnp.float32)
    normed_one, norm_one_back = jax.vjp(norm_rows, rows_in, norm_vals[0], norm_vals[1])
    normed_one = normed_one.astype(jnp.bfloat16)
    qkv_bias = jnp.concatenate([bias_vals[0], jnp.zeros((width_dim,), jnp.float32), bias_vals[1]])
    qkv_rows = (
        jnp.dot(normed_one, full_qkv, preferred_element_type=jnp.float32) + qkv_bias
    ).astype(jnp.bfloat16)
    qkv_heads = qkv_rows.reshape(-1, 3, head_count, HEAD_DIM)
    small_heads = qkv_heads[:small_rows].reshape(small_images, small_len, 3, head_count, HEAD_DIM)
    query_small = small_heads[:, :, 0]
    key_small = small_heads[:, :, 1]
    value_small = small_heads[:, :, 2]
    valid_small = jnp.arange(small_len, dtype=jnp.int32)[None, :] < small_counts[:, None]
    large_heads = qkv_heads[small_rows:]
    query_large = large_heads[:, 0][None]
    key_whole, value_whole = (
        lax.all_gather(large_heads[:, 1], "seq", axis=0, tiled=True),
        lax.all_gather(large_heads[:, 2], "seq", axis=0, tiled=True),
    )
    key_large = key_whole[None]
    value_large = value_whole[None]
    valid_large = jnp.arange(key_whole.shape[0], dtype=jnp.int32)[None, :] < large_counts[:, None]
    mixed_small, total_small = attend(query_small, key_small, value_small, valid_small, factor)
    mixed_large, total_large = attend(query_large, key_large, value_large, valid_large, factor)
    mixed = jnp.concatenate(
        [mixed_small.reshape(small_rows, width_dim), mixed_large.reshape(half_len, width_dim)]
    ).astype(jnp.bfloat16)
    middle = rows_in + jnp.dot(mixed, full_out, preferred_element_type=jnp.float32) + bias_vals[2]
    normed_two, norm_two_back = jax.vjp(norm_rows, middle, norm_vals[2], norm_vals[3])
    normed_two = normed_two.astype(jnp.bfloat16)
    up_proj = jnp.dot(normed_two, full_up, preferred_element_type=jnp.float32) + upbias_vals
    act_full, gelu_back = jax.vjp(gelu_exact, up_proj)
    act_low = act_full.astype(jnp.bfloat16)
    result = middle + jnp.dot(act_low, full_down, preferred_element_type=jnp.float32) + bias_vals[3]
    result_low = result.astype(jnp.bfloat16)
    small_out = result_low[:small_rows].reshape(small_tokens.shape)
    large_out = result_low[small_rows:].reshape(large_tokens.shape)
    back_qkv, back_out, back_up, back_down = (full_qkv, full_out, full_up, full_down)
    grad_rows = jnp.concatenate(
        [small_cot.reshape(small_rows, width_dim), large_cot.reshape(half_len, width_dim)]
    )
    grad_rows_full = grad_rows.astype(jnp.float32)
    grad_down = general_rows(act_low, grad_rows)
    grad_bias_down = jnp.sum(grad_rows, 0, dtype=jnp.float32)
    grad_act = general_cols(grad_rows, back_down)
    (grad_hidden,) = gelu_back(grad_act)
    grad_hidden_low = grad_hidden.astype(jnp.bfloat16)
    grad_up = general_rows(normed_two, grad_hidden_low)
    grad_up_bias = jnp.sum(grad_hidden_low, 0, dtype=jnp.float32)
    grad_normed_two = general_cols(grad_hidden_low, back_up)
    grad_mid_norm, grad_gain_two, grad_shift_two = norm_two_back(grad_normed_two)
    grad_middle = grad_rows_full + grad_mid_norm
    grad_middle_low = grad_middle.astype(jnp.bfloat16)
    grad_out = general_rows(mixed, grad_middle_low)
    grad_bias_out = jnp.sum(grad_middle_low, 0, dtype=jnp.float32)
    grad_mixed = (
        general_cols(grad_middle_low, back_out).astype(jnp.bfloat16).reshape(-1, head_count, HEAD_DIM)
    )
    grad_mixed_small = grad_mixed[:small_rows].reshape(
        small_images, small_len, head_count, HEAD_DIM
    )
    grad_mixed_large = grad_mixed[small_rows:][None]
    gq_small, gk_small, gv_small = attend_back(
        query_small, key_small, value_small, valid_small, total_small, grad_mixed_small, factor
    )
    gq_large, gk_whole, gv_whole = attend_back(
        query_large, key_large, value_large, valid_large, total_large, grad_mixed_large, factor
    )
    gk_large, gv_large = (
        lax.psum_scatter(
            gk_whole[0].astype(jnp.bfloat16), "seq", scatter_dimension=0, tiled=True
        ).astype(jnp.float32),
        lax.psum_scatter(
            gv_whole[0].astype(jnp.bfloat16), "seq", scatter_dimension=0, tiled=True
        ).astype(jnp.float32),
    )
    grad_qkv_small = jnp.stack([gq_small, gk_small, gv_small], 2).reshape(small_rows, 3 * width_dim)
    grad_qkv_large = jnp.stack([gq_large[0], gk_large, gv_large], 1).reshape(
        half_len, 3 * width_dim
    )
    grad_qkv_low = jnp.concatenate([grad_qkv_small, grad_qkv_large]).astype(jnp.bfloat16)
    grad_qkv = general_rows(normed_one, grad_qkv_low)
    grad_bias_query = jnp.sum(grad_qkv_low[:, :width_dim], 0, dtype=jnp.float32)
    grad_bias_value = jnp.sum(grad_qkv_low[:, 2 * width_dim :], 0, dtype=jnp.float32)
    grad_normed_one = general_cols(grad_qkv_low, back_qkv)
    grad_in_norm, grad_gain_one, grad_shift_one = norm_one_back(grad_normed_one)
    grad_input = (grad_middle + grad_in_norm).astype(jnp.bfloat16)
    small_grad = grad_input[:small_rows].reshape(small_tokens.shape)
    large_grad = grad_input[small_rows:].reshape(large_tokens.shape)
    grad_norm_all = jnp.stack([grad_gain_one, grad_shift_one, grad_gain_two, grad_shift_two])
    grad_bias_all = jnp.stack([grad_bias_query, grad_bias_value, grad_bias_out, grad_bias_down])
    shard_qkv, shard_out, shard_up, shard_down, shard_norm, shard_bias, shard_up_bias = (
        lax.psum_scatter(grad_qkv, ("dp", "seq"), scatter_dimension=0, tiled=True),
        lax.psum_scatter(grad_out, ("dp", "seq"), scatter_dimension=0, tiled=True),
        lax.psum_scatter(grad_up, ("dp", "seq"), scatter_dimension=0, tiled=True),
        lax.psum_scatter(grad_down, ("dp", "seq"), scatter_dimension=0, tiled=True),
        lax.psum_scatter(grad_norm_all, ("dp", "seq"), scatter_dimension=1, tiled=True),
        lax.psum_scatter(grad_bias_all, ("dp", "seq"), scatter_dimension=1, tiled=True),
        lax.psum_scatter(grad_up_bias, ("dp", "seq"), scatter_dimension=0, tiled=True),
    )
    return (
        small_out,
        large_out,
        small_grad,
        large_grad,
        shard_qkv,
        shard_out,
        shard_up,
        shard_down,
        shard_norm,
        shard_bias,
        shard_up_bias,
    )


def solution(mesh):
    in_specs = (
        P(("dp", "seq"), None, None),
        P("dp", "seq", None),
        P(("dp", "seq")),
        P("dp"),
        P(("dp", "seq"), None, None),
        P("dp", "seq", None),
        P(("dp", "seq"), None),
        P(("dp", "seq"), None),
        P(("dp", "seq"), None),
        P(("dp", "seq"), None),
        P(None, ("dp", "seq")),
        P(None, ("dp", "seq")),
        P(("dp", "seq")),
    )
    out_specs = (
        P(("dp", "seq"), None, None),
        P("dp", "seq", None),
        P(("dp", "seq"), None, None),
        P("dp", "seq", None),
        P(("dp", "seq"), None),
        P(("dp", "seq"), None),
        P(("dp", "seq"), None),
        P(("dp", "seq"), None),
        P(None, ("dp", "seq")),
        P(None, ("dp", "seq")),
        P(("dp", "seq")),
    )
    body = shards if (mesh.shape["dp"], mesh.shape["seq"]) == (16, 2) else shards_general
    return jax.shard_map(body, mesh=mesh, in_specs=in_specs, out_specs=out_specs, check_vma=False)
```

```python
import functools

import jax
import jax.numpy as jnp
from jax import lax
from jax.experimental import pallas as pl
from jax.experimental.pallas import tpu as pltpu
from jax.sharding import PartitionSpec as P

HEAD_DIM = 64
MESH = pl.DeviceIdType.MESH
BF = jnp.bfloat16
F32 = jnp.float32


def dot(a, b):
    return lax.dot_general(a, b, (((1,), (0,)), ((), ())), preferred_element_type=F32)


def dot_rows(a, b):
    return lax.dot_general(a, b, (((0,), (0,)), ((), ())), preferred_element_type=F32)


def dot_cols(a, b):
    return lax.dot_general(a, b, (((1,), (1,)), ((), ())), preferred_element_type=F32)


def device(x, y, z, c):
    return ((z * 2 + y) * 2 + c, x)


def rcopy(src, dst, send, recv, dev):
    return pltpu.make_async_remote_copy(
        src_ref=src, dst_ref=dst, send_sem=send, recv_sem=recv, device_id=dev, device_id_type=MESH
    )


def shard_at(j):
    return j // 4, (j // 2) % 2, j % 2


def stack_halves(g):
    n = g.shape[1] // 2
    return jnp.concatenate([g[:, :n], g[:, n:]], axis=0)


def rows_of(i, size, base=0):
    return pl.ds(pl.multiple_of(base + i * size, 16), size)


def lanes_of(i, size, base=0):
    return pl.ds(pl.multiple_of(base + i * size, 128), size)


def normalize(v):
    centred = v - jnp.mean(v, -1, keepdims=True)
    scale = lax.rsqrt(jnp.mean(centred * centred, -1, keepdims=True) + 1e-06)
    return centred * scale, scale


def norm_back(v, gain, grad):
    unit, scale = normalize(v)
    lifted = grad * gain
    inner = jnp.mean(lifted * unit, -1, keepdims=True)
    return scale * (lifted - jnp.mean(lifted, -1, keepdims=True) - unit * inner), unit


def gelu_pair(h):
    p = 0.3275911 * 0.7071067811865476
    t = 1.0 / (1.0 + p * abs(h))
    e = jnp.exp(-0.5 * h * h)
    poly = ((((1.061405429 * t - 1.453152027) * t + 1.421413741) * t - 0.284496736) * t + 0.254829592) * t
    q = 0.5 * poly * e
    phi = jnp.where(h >= 0, 1.0 - q, q)
    return h * phi, phi + h * e * 0.3989422804014327


def total(v):
    return jnp.sum(v.astype(F32), 0, keepdims=True)


def heads_forward(Q, KV, MIX, LSE, bias, q0, nq, k0, nk, first, count, unroll=1):
    D = Q.shape[1]
    left = lax.broadcasted_iota(jnp.int32, (nq, 128), 1) < HEAD_DIM

    def pair(hp, _):
        q = Q[q0 : q0 + nq, lanes_of(hp, 128)] * jnp.asarray(HEAD_DIM**-0.5, BF)
        k = KV[k0 : k0 + nk, lanes_of(hp, 128)]
        v = KV[k0 : k0 + nk, lanes_of(hp, 128, D)]
        zero = jnp.zeros_like(q)
        outs = []
        for head in range(2):
            qm = jnp.where(left, q, zero) if head == 0 else jnp.where(left, zero, q)
            s = dot_cols(k, qm) + bias
            top = jnp.max(s, 0, keepdims=True)
            e = jnp.exp(s - top)
            tot = jnp.sum(e, 0, keepdims=True)
            outs.append(dot_rows(v, e.astype(BF)) * (1.0 / tot))
            LSE[pl.ds(2 * hp + head, 1), 0:nq] = top + jnp.log(tot)
        both = jnp.concatenate([outs[0][:HEAD_DIM], outs[1][HEAD_DIM:]], axis=0)
        MIX[q0 : q0 + nq, lanes_of(hp, 128)] = jnp.transpose(both).astype(BF)
        return 0

    lax.fori_loop(first, first + count, pair, 0, unroll=unroll)


def heads_backward(Q, KV, MIX, DMIX, LSE, bias, q0, nq, k0, nk, first, count, unroll=1):
    D = Q.shape[1]
    left = lax.broadcasted_iota(jnp.int32, (nq, 128), 1) < HEAD_DIM
    leftk = lax.broadcasted_iota(jnp.int32, (nk, 128), 1) < HEAD_DIM

    def pair(hp, _):
        q = Q[q0 : q0 + nq, lanes_of(hp, 128)] * jnp.asarray(HEAD_DIM**-0.5, BF)
        dm = DMIX[q0 : q0 + nq, lanes_of(hp, 128)]
        k = KV[k0 : k0 + nk, lanes_of(hp, 128)]
        v = KV[k0 : k0 + nk, lanes_of(hp, 128, D)]
        zero = jnp.zeros_like(q)
        weighted = jnp.transpose(dm.astype(F32) * MIX[q0 : q0 + nq, lanes_of(hp, 128)].astype(F32))
        dqs, dks, dvs = [], [], []
        for head in range(2):
            mask = lambda u: jnp.where(left, u, zero) if head == 0 else jnp.where(left, zero, u)
            delta = jnp.sum(weighted[head * HEAD_DIM : (head + 1) * HEAD_DIM], 0, keepdims=True)
            s = dot_cols(k, mask(q)) + bias
            pr = jnp.exp(s - LSE[pl.ds(2 * hp + head, 1), 0:nq])
            dvs.append(dot(pr.astype(BF), dm))
            ds = (pr * (dot_cols(v, mask(dm)) - delta)).astype(BF)
            dks.append(dot(ds, q))
            dqs.append(dot_rows(k, ds))
        both = jnp.concatenate([dqs[0][:HEAD_DIM], dqs[1][HEAD_DIM:]], axis=0) * HEAD_DIM**-0.5
        Q[q0 : q0 + nq, lanes_of(hp, 128)] = jnp.transpose(both).astype(BF)
        KV[k0 : k0 + nk, lanes_of(hp, 128)] = jnp.where(leftk, dks[0], dks[1]).astype(BF)
        KV[k0 : k0 + nk, lanes_of(hp, 128, D)] = jnp.where(leftk, dvs[0], dvs[1]).astype(BF)
        return 0

    lax.fori_loop(first, first + count, pair, 0, unroll=unroll)


def store_block(g, SP, w, h):
    for j in range(16):
        z, y, c = shard_at(j)
        for x in range(2):
            r = 48 * j + 24 * x
            SP[w, h, x, y, z, c] = stack_halves(g[r : r + 24]).astype(BF)


def store_down(g, SP, f):
    n = SP.shape[-1]
    for j in range(4):
        for x in range(2):
            for half in range(2):
                r = (2 * j + x) * 96 + 48 * half
                for h in range(2):
                    SP[2 + half, h, x, j // 2, f, j % 2] = g[r : r + 48, h * n : h * n + n].astype(BF)


def layer_kernel(
    xs, xl, cs, cl, count_s, count_l, wqkv, wout, wup, wdown, norm, bias, upbias,
    OUT, DX, gqkv, gout, gup, gdown, SGO,
    X, DY, H1, Q, KV, MIX, MID, H2, ACC, DH2, ACT, DHB, DH1P, LP, LSES, LSEL,
    WQKV, WOUT, WUP, WDOWN, SP, OWN, LC, T, LF, sp, sm, sml, SG, SGL,
    ss, rs, tsem, psem, sms, smr, gs, gr, s2, r2, credit, room,
):
    d = lax.axis_index("dp")
    x, y, z, c = lax.axis_index("seq"), (d // 2) % 2, d // 4, d % 2
    zs = [z + 1 - 2 * (z % 2), 3 - z, (z + 2) % 4]
    sib, xn, yn = device(x, y, z, 1 - c), device(1 - x, y, z, c), device(x, 1 - y, z, c)
    zn = [device(x, y, k, c) for k in zs]
    bar = pltpu.get_barrier_semaphore()
    for p in [sib, xn, yn] + zn:
        pl.semaphore_signal(bar, inc=1, device_id=p, device_id_type=MESH)

    D = xs.shape[1]
    n = D // 2
    ns, nl = xs.shape[0], xl.shape[0]
    r1 = -(-ns // 16) * 16
    rl = -(-nl // 16) * 16
    R = r1 + rl
    RK = R + rl
    RB = 32
    zero = functools.partial(jnp.zeros, dtype=BF)
    head = ns - ns % 16

    X[head:r1, :] = zero((r1 - head, D))
    X[R - 16 : R, :] = zero((16, D))
    X[0:ns, :] = xs[...]
    X[r1 : r1 + nl, :] = xl[...]

    blocks = [wqkv[:, k * D : (k + 1) * D] for k in range(3)] + [wout[...]]
    blocks = [stack_halves(g) for g in blocks]
    blocks += [wdown[48 * (b // 2) : 48 * (b // 2) + 48, (b % 2) * n : (b % 2) * n + n] for b in range(4)]
    blocks += [stack_halves(wup[:, k * D : (k + 1) * D]) for k in range(4)]
    for b, g in enumerate(blocks):
        OWN[b // 2, b % 2] = g.astype(BF)
    for w in range(6):
        SP[w, c, x, y, z, c] = OWN[w, c]
    pl.semaphore_wait(bar, 6)
    swaps = [rcopy(OWN.at[w, 1 - c], SP.at[w, 1 - c, x, y, z, c], ss.at[w, 0], rs.at[w, 0], sib) for w in range(6)]
    for cp in swaps:
        cp.start()
    tcp = rcopy(X.at[r1:R], X.at[R:RK], tsem.at[0], tsem.at[1], xn)

    me = d * 2 + x
    k, m = norm.shape[1], upbias.shape[1]

    def placed(v, start):
        wide = jnp.concatenate([v, jnp.zeros((v.shape[0], D - v.shape[1]), F32)], axis=1)
        return pltpu.roll(wide, start, 1)

    row = lax.broadcasted_iota(jnp.int32, (8, D), 0)
    both = jnp.concatenate([norm[...], bias[...]], axis=0).astype(BF).astype(F32)
    sm[0:8, :] = placed(both, me * k)
    ub = placed(jnp.broadcast_to(upbias[...].astype(BF).astype(F32), (8, m)), lax.rem(me * m, D))
    sm[8:16, :] = jnp.where(row == (me * m) // D, ub, 0.0)

    def join(buf, land, send, recv, ks, devs):
        cps = [rcopy(buf, land.at[i], send.at[i], recv.at[i], dev) for i, dev in zip(ks, devs)]

        def start():
            for cp in cps:
                cp.start()

        def finish():
            for cp in cps:
                cp.wait()
            tot = buf[...]
            for i in ks:
                tot = tot + land[i]
            buf[...] = tot

        return start, finish

    def joins(buf, land, send, recv):
        return [
            join(buf, land, send, recv, *a) for a in (([0], [sib]), ([1], [xn]), ([2], [yn]), ([3, 4, 5], zn))
        ]

    smalls = joins(sm, sml, sms, smr)

    pieces = [z] + zs

    def by_core(run):
        for core in range(2):
            pl.when(c == core)(lambda core=core: run(core))

    def mail(w, sem, dev, out, back):
        sent, got = SP.at[(w, c) + out], SP.at[(w, c) + back]
        return (
            rcopy(sent, sent, ss.at[w, sem], rs.at[w, sem], dev),
            rcopy(got, got, ss.at[w, sem], rs.at[w, sem], dev),
        )

    def mails(w, core):
        if core == 0:
            one = [mail(w, 1 + i, zn[i], (x, y, z), (x, y, zs[i])) for i in range(3)]
            two = [mail(w, 4 + k, yn, (x, y, p), (x, 1 - y, p)) for k, p in enumerate(pieces)]
            three = [mail(w, 8 + k, xn, (x, y, p), (1 - x, y, p)) for k, p in enumerate(pieces)]
            three += [mail(w, 12 + k, xn, (x, 1 - y, p), (1 - x, 1 - y, p)) for k, p in enumerate(pieces)]
        else:
            one = [mail(w, 1, xn, (x, y, z), (1 - x, y, z))]
            two = [mail(w, 2 + i, zn[i], (x, y, z), (x, y, zs[i])) for i in range(3)]
            two += [mail(w, 5 + i, zn[i], (1 - x, y, z), (1 - x, y, zs[i])) for i in range(3)]
            three = [mail(w, 8 + k, yn, (x, y, p), (x, 1 - y, p)) for k, p in enumerate(pieces)]
            three += [mail(w, 12 + k, yn, (1 - x, y, p), (1 - x, 1 - y, p)) for k, p in enumerate(pieces)]
        return one, two, three

    def a1(w):
        swaps[w].wait()

        def run(core):
            one, two, three = mails(w, core)
            first = one + (two[0:1] + three[0:1] if core == 0 else two[0:3] + three[0:1])
            for sent, _ in first:
                sent.start()

        by_core(run)

    def a2(w):
        def run(core):
            one, two, three = mails(w, core)
            for i, (_, got) in enumerate(one):
                got.wait_recv()
                onward = [two[1 + i], three[1 + i]] if core == 0 else two[3:6] + three[4:5]
                for sent, _ in onward:
                    sent.start()

        by_core(run)

    def a3(w):
        def run(core):
            _, two, three = mails(w, core)
            if core == 0:
                for k in range(4):
                    two[k][1].wait_recv()
                    three[4 + k][0].start()
            else:
                for part in range(2):
                    for i in range(3):
                        two[3 * part + i][1].wait_recv()
                        three[4 * part + 1 + i][0].start()

        by_core(run)

    def a4(w):
        def run(core):
            one, two, three = mails(w, core)
            for _, got in three:
                got.wait_recv()
            for sent, _ in one + two + three:
                sent.wait_send()

        by_core(run)
        src = SP.at[w, c]
        rcopy(src, src, ss.at[w, 16], rs.at[w, 16], sib).start()

    def assemble(w, h, dst, col):
        def step(j, _):
            pz, py, pc = shard_at(j)
            a = SP[w, h, 0, py, pz, pc].astype(F32)
            e = SP[w, h, 1, py, pz, pc].astype(F32)
            dst[rows_of(j, 48), col : col + n] = jnp.concatenate([a[:24], e[:24]], axis=0).astype(BF)
            dst[rows_of(j, 48), col + n : col + D] = jnp.concatenate([a[24:], e[24:]], axis=0).astype(BF)
            return 0

        lax.fori_loop(0, 16, step, 0, unroll=4)

    def assemble_down(w, h):
        def step(j, _):
            pz, py, pc = shard_at(j)
            for px in range(2):
                rows = pl.ds(pl.multiple_of(96 * (2 * j + px) + 48 * (w - 2), 16), 48)
                WDOWN[rows, n * h : n * h + n] = SP[w, h, px, py, pz, pc]
            return 0

        lax.fori_loop(0, 16, step, 0, unroll=4)

    def a5(w):
        src, dst = SP.at[w, c], SP.at[w, 1 - c]
        rcopy(src, src, ss.at[w, 16], rs.at[w, 16], sib).wait_send()
        rcopy(dst, dst, ss.at[w, 16], rs.at[w, 16], sib).wait_recv()
        for h in range(2):
            b = 2 * w + h
            if b < 3:
                assemble(w, h, WQKV, b * D)
            elif b == 3:
                assemble(w, h, WOUT, 0)
            elif b < 8:
                assemble_down(w, h)
            else:
                assemble(w, h, WUP, (b - 8) * D)

    def credits(w):
        for i, dev in enumerate([xn, yn] + zn):
            pl.semaphore_signal(room.at[i], inc=1, device_id=dev, device_id_type=MESH)

    order = [4, 5, 2, 3, 1, 0]
    backs = [zs[2], zs[1], zs[0], z]

    def add(w, dst, src, count):
        def step(i, _):
            at = (w, c) + dst(i)
            SP[at] = (SP[at].astype(F32) + src(i).astype(F32)).astype(BF)
            return 0

        lax.fori_loop(0, count, step, 0, unroll=min(count, 4))

    def first_copy(i, k):
        w = order[i]
        return rcopy(SP.at[w, 1 - c, :, :, k], LC.at[i % 2, :, :, k], s2.at[w, k], r2.at[w, k], sib)

    def go(i):
        if i >= 2:
            pl.semaphore_wait(credit, 1)
        for k in range(4):
            first_copy(i, k).start()

    def second_copy(w, k, core):
        pz = backs[k]
        dev = (xn, yn)[core]
        src = (SP.at[w, c, 1 - x, :, pz], SP.at[w, c, :, 1 - y, pz])[core]
        return rcopy(src, SP.at[w, 1 - c, 0, :, k], s2.at[w, 4 + k], r2.at[w, 4 + k], dev)

    def third_copy(w, k, core):
        pz = backs[k]
        if core == 0:
            return rcopy(SP.at[w, c, x, 1 - y, pz], SP.at[w, 1 - c, 1, 0, k], s2.at[w, 8 + k], r2.at[w, 8 + k], yn)
        return rcopy(SP.at[w, c, :, y, pz], SP.at[w, 1 - c, 1, :, k], s2.at[w, 8 + k], r2.at[w, 8 + k], zn[2 - k])

    def fourth_copy(w, k, core):
        if core == 0:
            return rcopy(
                SP.at[w, c, x, y, backs[k]], SP.at[w, 1 - c, 1, 1, k], s2.at[w, 12 + k], r2.at[w, 12 + k], zn[2 - k]
            )
        return rcopy(SP.at[w, c, 1 - x, y, z], SP.at[w, 1 - c, 1, 0, 3], s2.at[w, 12], r2.at[w, 12], xn)

    def last_copy(w):
        return rcopy(T.at[w, 1 - c], LF.at[w], s2.at[w, 15], r2.at[w, 15], sib)

    def deliver(w):
        mine, other = T[w, c], LF[w]
        for h in range(2):
            g = jnp.where(c == h, mine, other)
            b = 2 * w + h
            if 4 <= b < 8:
                half = (b - 4) // 2
                gdown[48 * half : 48 * half + 48, n * h : n * h + n] = g
                continue
            wide = jnp.concatenate([g[0:24], g[24:48]], axis=1)
            if b >= 8:
                gup[:, (b - 8) * D : (b - 7) * D] = wide
            elif b == 2:
                gout[...] = wide
            else:
                g0 = (3, 2, None, 1)[b] - 1
                third = D // 3
                for part in range(3):
                    lo = part * D + g0 * third
                    gqkv[:, lo : lo + third] = wide[:, part * third : (part + 1) * third]

    def back(i, stage):
        w = order[i]
        if stage == 0:
            for k in range(4):
                first_copy(i, k).wait()
                idx = lambda j: (j // 4, (j // 2) % 2, k, j % 2)
                add(w, idx, lambda j: LC[(i % 2,) + idx(j)], 8)
            if i < 4:
                pl.semaphore_signal(credit, inc=1, device_id=sib, device_id_type=MESH)
            credits(w)
        elif stage == 1:

            def run(core):
                pl.semaphore_wait(room.at[core], 1)
                for k in range(4):
                    second_copy(w, k, core).start()

            by_core(run)
        elif stage == 2:

            def run(core):
                if core == 0:
                    pl.semaphore_wait(room.at[1], 1)
                for k in range(4):
                    second_copy(w, k, core).wait()
                    place = ((lambda j: (x, j // 2, backs[k], j % 2)), (lambda j: (j // 2, y, backs[k], j % 2)))[core]
                    add(w, place, lambda j: SP[w, 1 - c, 0, j // 2, k, j % 2], 4)
                    if core == 1 and k < 3:
                        pl.semaphore_wait(room.at[2 + 2 - k], 1)
                    if core == 0 or k < 3:
                        third_copy(w, k, core).start()

            by_core(run)
        elif stage == 3:

            def run(core):
                if core == 0:
                    for k in range(4):
                        third_copy(w, k, core).wait()
                        add(w, lambda j: (x, y, backs[k], j), lambda j: SP[w, 1 - c, 1, 0, k, j], 2)
                        if k < 3:
                            pl.semaphore_wait(room.at[2 + 2 - k], 1)
                            fourth_copy(w, k, core).start()
                    return
                for k in range(3):
                    third_copy(w, k, core).wait()
                three = lambda j: sum(SP[w, 1 - c, 1, j // 2, k, j % 2].astype(F32) for k in range(3))
                add(w, lambda j: (j // 2, y, z, j % 2), three, 4)
                pl.semaphore_wait(room.at[0], 1)
                fourth_copy(w, 0, core).start()

            by_core(run)
        elif stage == 4:

            def run(core):
                count = 3 if core == 0 else 1
                for k in range(count):
                    fourth_copy(w, k, core).wait()
                for q in range(2):
                    tot = SP[w, c, x, y, z, q].astype(F32)
                    for k in range(count):
                        at = (1, 1, k, q) if core == 0 else (1, 0, 3, q)
                        tot = tot + SP[(w, 1 - c) + at].astype(F32)
                    T[w, q] = tot

            by_core(run)
            last_copy(w).start()
        else:
            last_copy(w).wait()
            deliver(w)

    def norm_one(base, count):
        def step(i, _):
            rows = rows_of(i, 16, base)
            unit, _ = normalize(X[rows, :].astype(F32))
            H1[rows, :] = (unit * sp[0:1, :] + sp[1:2, :]).astype(BF)
            return 0

        lax.fori_loop(0, count // 16, step, 0, unroll=2)

    small_count, large_count = count_s[0], count_l[0]
    kj = lax.broadcasted_iota(jnp.int32, (r1, 1), 0)
    bias_small = jnp.where(kj < small_count, 0.0, -1e30)
    kj = lax.broadcasted_iota(jnp.int32, (2 * rl, 1), 0)
    mine = kj < rl
    inside = jnp.where(mine, kj, kj - rl)
    where = inside + jnp.where(mine, x, 1 - x) * nl
    bias_large = jnp.where((inside < nl) & (where < large_count), 0.0, -1e30)
    small_part = (bias_small, 0, r1, 0, r1)
    large_part = (bias_large, r1, rl, r1, 2 * rl)

    def take_cotangents():
        DY[head:r1, :] = zero((r1 - head, D))
        DY[R - 16 : R, :] = zero((16, D))
        DY[0:ns, :] = cs[...]
        DY[r1 : r1 + nl, :] = cl[...]

    def know_smalls():
        smalls[3][1]()
        sp[...] = sm[...]

    def query():
        Q[...] = (dot(H1[0:R, :], WQKV[:, 0:D]) + sp[4:5, :]).astype(BF)

    def key():
        KV[:, 0:D] = dot(H1[...], WQKV[:, D : 2 * D]).astype(BF)

    def value():
        KV[:, D:] = (dot(H1[...], WQKV[:, 2 * D :]) + sp[5:6, :]).astype(BF)

    def attend_small():
        heads_forward(Q, KV, MIX, LSES, *small_part, 0, 6, unroll=2)

    def attend_large(hp):
        heads_forward(Q, KV, MIX, LSEL, *large_part, hp, 1)

    def project_out():
        MID[...] = dot(MIX[...], WOUT[...])

    def second_norm():
        def step(i, _):
            rows = rows_of(i, RB)
            middle = X[rows, :].astype(F32) + MID[rows, :] + sp[6:7, :]
            MID[rows, :] = middle
            unit, _ = normalize(middle)
            H2[rows, :] = (unit * sp[2:3, :] + sp[3:4, :]).astype(BF)
            ACC[rows, :] = middle + sp[7:8, :]
            return 0

        lax.fori_loop(0, R // RB, step, 0)

    def part(f):
        return slice(f * D, (f + 1) * D)

    def hidden_units(f):
        hidden = dot(H2[...], WUP[:, part(f)]) + sp[8 + f : 9 + f, :]
        dact = dot_cols(DY[...], WDOWN[part(f), :])
        act, slope = gelu_pair(hidden)
        ACT[...] = act.astype(BF)
        dh = (dact * slope).astype(BF)
        DHB[...] = dh
        SG[8 + f : 9 + f, :] = total(dh)

    def grad_up(f):
        store_block(dot_rows(H2[...], DHB[...]), SP, 4 + f // 2, f % 2)

    def grad_down(f):
        store_down(dot_rows(ACT[...], DY[...]), SP, f)

    def forward_down(f):
        ACC[...] += dot(ACT[...], WDOWN[part(f), :])

    def backward_up(f):
        g = dot_cols(DHB[...], WUP[:, part(f)])
        DH2[...] = g if f == 0 else DH2[...] + g

    def give_out():
        OUT[...] = ACC[...].astype(BF)

    z1 = jnp.zeros((1, D), F32)

    def second_norm_back():
        def step(i, sums):
            rows = rows_of(i, RB)
            grad = DH2[rows, :]
            dy = DY[rows, :].astype(F32)
            dv, unit = norm_back(MID[rows, :], sp[2:3, :], grad)
            dmid = dy + dv
            MID[rows, :] = dmid
            low = dmid.astype(BF)
            H2[rows, :] = low
            return sums[0] + total(grad * unit), sums[1] + total(grad), sums[2] + total(low), sums[3] + total(dy)

        sums = lax.fori_loop(0, R // RB, step, (z1, z1, z1, z1))
        for i, at in enumerate((2, 3, 6, 7)):
            SG[at : at + 1, :] = sums[i]

    def grad_mixed():
        ACT[...] = dot_cols(H2[...], WOUT[...]).astype(BF)

    def grad_out():
        store_block(dot_rows(MIX[...], H2[...]), SP, 1, 0)

    third = D // 3

    def back_small(g):
        heads_backward(Q, KV, MIX, ACT, LSES, *small_part, 2 * g, 2, unroll=2)

    def back_large(hp):
        heads_backward(Q, KV, MIX, ACT, LSEL, *large_part, hp, 1)

    def grad_heads(g):
        lo = slice(g * third, (g + 1) * third)
        lov = slice(D + g * third, D + (g + 1) * third)
        grads = [dot_rows(H1[0:R, :], Q[:, lo]), dot_rows(H1[...], KV[:, lo]), dot_rows(H1[...], KV[:, lov])]
        w, h = ((1, 1), (0, 1), (0, 0))[g]
        store_block(jnp.concatenate(grads, axis=1), SP, w, h)

    pcp = rcopy(DH1P, LP, psem.at[0], psem.at[1], xn)

    def grad_partner():
        g = dot_cols(KV[R:RK, 0:D], WQKV[:, D : 2 * D]) + dot_cols(KV[R:RK, D:], WQKV[:, 2 * D :])
        DH1P[...] = g.astype(BF)

    def grad_normed():
        ACC[...] = dot_cols(Q[...], WQKV[:, 0:D]) + dot_cols(KV[0:R, 0:D], WQKV[:, D : 2 * D])
        ACC[...] += dot_cols(KV[0:R, D:], WQKV[:, 2 * D :])

    def first_norm_back(base, count, partner):
        def step(i, _):
            rows = rows_of(i, 16, base)
            grad = ACC[rows, :]
            if partner:
                grad = grad + LP[rows_of(i, 16), :].astype(F32)
            dv, _ = norm_back(X[rows, :].astype(F32), sp[0:1, :], grad)
            DX[rows, :] = (MID[rows, :] + dv).astype(BF)
            return 0

        lax.fori_loop(0, count // 16, step, 0)

    ends = joins(SG, SGL, gs, gr)

    def first_norm_sums():
        def part_of(base, grads, gbase):
            def step(i, sums):
                unit, _ = normalize(X[rows_of(i, 16, base), :].astype(F32))
                grad = grads[rows_of(i, 16, gbase), :].astype(F32)
                return sums[0] + total(grad * unit), sums[1] + total(grad)

            return step

        sums = lax.fori_loop(0, R // 16, part_of(0, ACC, 0), (z1, z1), unroll=2)
        sums = lax.fori_loop(0, rl // 16, part_of(R, DH1P, 0), sums)
        SG[0:1, :] = sums[0]
        SG[1:2, :] = sums[1]
        SG[4:5, :] = total(Q[...])
        SG[5:6, :] = total(KV[:, D:])

    SG[...] = jnp.zeros(SG.shape, F32)

    a1(0)
    smalls[0][0]()
    smalls[0][1]()
    smalls[1][0]()
    a2(0)
    a1(1)
    smalls[1][1]()
    a3(0)
    tcp.start()
    smalls[2][0]()
    a4(0)
    a2(1)
    a1(2)
    smalls[2][1]()
    a3(1)
    tcp.wait()
    take_cotangents()
    smalls[3][0]()
    a2(2)
    a5(0)
    know_smalls()
    norm_one(0, R)
    a1(3)
    a4(1)
    a3(2)
    query()
    norm_one(R, rl)
    key()
    a5(1)
    a2(3)
    a1(4)
    value()
    attend_large(0)
    a4(2)
    a2(4)
    attend_large(1)
    a3(3)
    a1(5)
    attend_large(2)
    attend_large(3)
    attend_large(4)
    a3(4)
    attend_small()
    a4(3)
    attend_large(5)
    a2(5)
    a5(2)
    a4(4)
    project_out()
    second_norm()
    a5(3)
    a3(5)
    a5(4)
    hidden_units(0)
    grad_up(0)
    forward_down(0)
    grad_down(0)
    backward_up(0)
    a4(5)
    hidden_units(1)
    backward_up(1)
    forward_down(1)
    grad_down(1)
    grad_up(1)
    go(0)
    a5(5)
    hidden_units(2)
    back(0, 0)
    grad_up(2)
    backward_up(2)
    forward_down(2)
    back(0, 1)
    grad_down(2)
    hidden_units(3)
    grad_up(3)
    go(1)
    backward_up(3)
    grad_down(3)
    second_norm_back()
    back(1, 0)
    back(0, 2)
    forward_down(3)
    back(1, 1)
    grad_mixed()
    go(2)
    back_large(0)
    go(3)
    grad_out()
    back(2, 0)
    back(0, 3)
    back_small(0)
    back(1, 2)
    back(2, 1)
    back(3, 0)
    back_large(1)
    grad_heads(0)
    back(3, 1)
    go(4)
    back_large(5)
    back(1, 3)
    back_small(1)
    back(2, 2)
    give_out()
    back(4, 0)
    back_small(2)
    back_large(4)
    back(4, 1)
    back(3, 2)
    back(0, 4)
    back_large(2)
    back_large(3)
    back(2, 3)
    grad_partner()
    pcp.start()
    grad_heads(2)
    back(3, 3)
    grad_heads(1)
    back(4, 2)
    back(0, 5)
    back(1, 4)
    go(5)
    grad_normed()
    back(5, 0)
    first_norm_sums()
    ends[0][0]()
    back(5, 1)
    back(4, 3)
    back(1, 5)
    back(2, 4)
    ends[0][1]()
    ends[1][0]()
    back(5, 2)
    back(3, 4)
    back(4, 4)
    ends[1][1]()
    back(2, 5)
    ends[2][0]()
    back(5, 3)
    first_norm_back(0, r1, False)
    pcp.wait()
    ends[2][1]()
    back(3, 5)
    ends[3][0]()
    back(5, 4)
    first_norm_back(r1, rl, True)
    back(4, 5)
    back(5, 5)
    ends[3][1]()
    SGO[...] = SG[...]


def deliver_kernel(
    OUT, DX, gqkv, gout, gup, gdown, SG,
    outs, outl, dxs, dxl, oqkv, oout, oup, odown, onorm, obias, oub,
):
    ns, nl = outs.shape[0], outl.shape[0]
    r1 = -(-ns // 16) * 16
    outs[...] = OUT[0:ns, :]
    outl[...] = OUT[r1 : r1 + nl, :]
    dxs[...] = DX[0:ns, :]
    dxl[...] = DX[r1 : r1 + nl, :]
    oqkv[...] = gqkv[...]
    oout[...] = gout[...]
    oup[...] = gup[...]
    odown[...] = gdown[...]
    D = outs.shape[1]
    me = lax.axis_index("dp") * 2 + lax.axis_index("seq")
    k, m = onorm.shape[1], oub.shape[1]
    near = pltpu.roll(SG[0:8, :], lax.rem(D - me * k, D), 1)[:, 0:k]
    onorm[...] = near[0:4]
    obias[...] = near[4:8]
    row = lax.broadcasted_iota(jnp.int32, (8, D), 0)
    picked = total(jnp.where(row == (me * m) // D, SG[8:16, :], 0.0))
    near = pltpu.roll(jnp.broadcast_to(picked, (8, D)), lax.rem(D - lax.rem(me * m, D), D), 1)
    oub[...] = near[0:1, 0:m]


def vm():
    return pl.BlockSpec(memory_space=pltpu.VMEM)


def layer(xs, xl, cs, cl, count_s, count_l, wqkv, wout, wup, wdown, norm, bias, upbias):
    D = xs.shape[1]
    n = D // 2
    r1 = -(-xs.shape[0] // 16) * 16
    rl = -(-xl.shape[0] // 16) * 16
    R = r1 + rl
    RK = R + rl
    sds = jax.ShapeDtypeStruct
    smem = pl.BlockSpec(memory_space=pltpu.SMEM)
    dma, regular = pltpu.SemaphoreType.DMA, pltpu.SemaphoreType.REGULAR
    small = (16, D)
    return pl.pallas_call(
        layer_kernel,
        out_shape=(
            sds((R, D), BF), sds((R, D), BF),
            sds(wqkv.shape, F32), sds(wout.shape, F32), sds(wup.shape, F32), sds(wdown.shape, F32), sds(small, F32),
        ),
        in_specs=[vm()] * 4 + [smem] * 2 + [vm()] * 7,
        out_specs=(vm(),) * 7,
        scratch_shapes=[
            pltpu.VMEM((RK, D), BF),
            pltpu.VMEM((R, D), BF),
            pltpu.VMEM((RK, D), BF),
            pltpu.VMEM((R, D), BF),
            pltpu.VMEM((RK, 2 * D), BF),
            pltpu.VMEM((R, D), BF),
            pltpu.VMEM((R, D), F32),
            pltpu.VMEM((R, D), BF),
            pltpu.VMEM((R, D), F32),
            pltpu.VMEM((R, D), F32),
            pltpu.VMEM((R, D), BF),
            pltpu.VMEM((R, D), BF),
            pltpu.VMEM((rl, D), BF),
            pltpu.VMEM((rl, D), BF),
            pltpu.VMEM((16, r1), F32),
            pltpu.VMEM((16, rl), F32),
            pltpu.VMEM((D, 3 * D), BF),
            pltpu.VMEM((D, D), BF),
            pltpu.VMEM((D, 4 * D), BF),
            pltpu.VMEM((4 * D, D), BF),
            pltpu.VMEM((6, 2, 2, 2, 4, 2, 48, n), BF),
            pltpu.VMEM((6, 2, 48, n), BF),
            pltpu.VMEM((2, 2, 2, 4, 2, 48, n), BF),
            pltpu.VMEM((6, 2, 48, n), F32),
            pltpu.VMEM((6, 48, n), F32),
            pltpu.VMEM(small, F32),
            pltpu.VMEM(small, F32),
            pltpu.VMEM((6,) + small, F32),
            pltpu.VMEM(small, F32),
            pltpu.VMEM((6,) + small, F32),
            dma((6, 17)), dma((6, 17)), dma((2,)), dma((2,)), dma((6,)), dma((6,)), dma((6,)), dma((6,)),
            dma((6, 16)), dma((6, 16)), regular, regular((5,)),
        ],
        compiler_params=pltpu.CompilerParams(collective_id=1, has_side_effects=True, vmem_limit_bytes=63 << 20),
        name="layer",
    )(xs, xl, cs, cl, count_s, count_l, wqkv, wout, wup, wdown, norm, bias, upbias)


def shards(
    small_tokens, large_tokens, small_counts, large_counts, small_cot, large_cot,
    w_qkv, w_out, w_up, w_down, norm_params, proj_bias, up_bias,
):
    flat = lambda v: v.reshape(v.shape[1:])
    xs, xl, cs, cl = flat(small_tokens), flat(large_tokens), flat(small_cot), flat(large_cot)
    made = layer(
        xs, xl, cs, cl, small_counts, large_counts, w_qkv, w_out, w_up, w_down, norm_params, proj_bias, up_bias[None]
    )
    like = (xs, xl, xs, xl, w_qkv, w_out, w_up, w_down, norm_params, proj_bias, up_bias[None])
    outs, outl, dxs, dxl, gqkv, gout, gup, gdown, gnorm, gbias, gub = pl.pallas_call(
        deliver_kernel,
        out_shape=tuple(jax.ShapeDtypeStruct(v.shape, v.dtype) for v in like),
        in_specs=[vm()] * 7,
        out_specs=(vm(),) * 11,
        compiler_params=pltpu.CompilerParams(vmem_limit_bytes=62 << 20),
        name="deliver",
    )(*made)
    return outs[None], outl[None], dxs[None], dxl[None], gqkv, gout, gup, gdown, gnorm, gbias, gub[0]


def norm_rows(values, gain, shift):
    centre = jnp.mean(values, -1, keepdims=True)
    centered = values - centre
    spread = jnp.mean(centered * centered, -1, keepdims=True)
    return centered * lax.rsqrt(spread + 1e-06) * gain + shift


def gelu_exact(values):
    return jax.nn.gelu(values, approximate=False)


def general_rows(left, right):
    return lax.dot_general(
        left, right, (((0,), (0,)), ((), ())), preferred_element_type=jnp.float32
    )


def general_cols(left, right):
    return lax.dot_general(
        left, right, (((1,), (1,)), ((), ())), preferred_element_type=jnp.float32
    )


def attend(query, key_part, value, valid_keys, factor):
    raw_scores = jnp.einsum("bqhe,bkhe->bhqk", query, key_part, preferred_element_type=jnp.float32)
    scaled = jnp.where(valid_keys[:, None, None, :], raw_scores * factor, -1e30)
    row_top = jnp.max(scaled, -1, keepdims=True)
    expo_rows = jnp.exp(scaled - row_top)
    totals = jnp.sum(expo_rows, -1, keepdims=True)
    probs_full = expo_rows / totals
    mixed = jnp.einsum(
        "bhqk,bkhe->bqhe",
        probs_full.astype(jnp.bfloat16),
        value,
        preferred_element_type=jnp.float32,
    )
    return (mixed, row_top + jnp.log(totals))


def attend_back(query, key_part, value, valid_keys, log_total, grad_mixed, factor):
    raw_scores = jnp.einsum("bqhe,bkhe->bhqk", query, key_part, preferred_element_type=jnp.float32)
    scaled = jnp.where(valid_keys[:, None, None, :], raw_scores * factor, -1e30)
    probs_full = jnp.exp(scaled - log_total)
    grad_value = jnp.einsum(
        "bhqk,bqhe->bkhe",
        probs_full.astype(jnp.bfloat16),
        grad_mixed,
        preferred_element_type=jnp.float32,
    )
    grad_probs = jnp.einsum(
        "bqhe,bkhe->bhqk", grad_mixed, value, preferred_element_type=jnp.float32
    )
    row_delta = jnp.sum(probs_full * grad_probs, -1, keepdims=True)
    grad_raw = (probs_full * (grad_probs - row_delta) * factor).astype(jnp.bfloat16)
    grad_query = jnp.einsum(
        "bhqk,bkhe->bqhe", grad_raw, key_part, preferred_element_type=jnp.float32
    )
    grad_key = jnp.einsum("bhqk,bqhe->bkhe", grad_raw, query, preferred_element_type=jnp.float32)
    return (grad_query, grad_key, grad_value)


def shards_general(
    small_tokens,
    large_tokens,
    small_counts,
    large_counts,
    small_cot,
    large_cot,
    w_qkv,
    w_out,
    w_up,
    w_down,
    norm_params,
    proj_bias,
    up_bias,
):
    gathered = (
        lax.all_gather(w_qkv.astype(jnp.bfloat16), ("dp", "seq"), axis=0, tiled=True),
        lax.all_gather(w_out.astype(jnp.bfloat16), ("dp", "seq"), axis=0, tiled=True),
        lax.all_gather(w_up.astype(jnp.bfloat16), ("dp", "seq"), axis=0, tiled=True),
        lax.all_gather(w_down.astype(jnp.bfloat16), ("dp", "seq"), axis=0, tiled=True),
        lax.all_gather(norm_params.astype(jnp.bfloat16), ("dp", "seq"), axis=1, tiled=True),
        lax.all_gather(proj_bias.astype(jnp.bfloat16), ("dp", "seq"), axis=1, tiled=True),
        lax.all_gather(up_bias.astype(jnp.bfloat16), ("dp", "seq"), axis=0, tiled=True),
    )
    full_qkv, full_out, full_up, full_down, full_norm, full_bias, full_upbias = gathered
    norm_vals = full_norm.astype(jnp.float32)
    bias_vals = full_bias.astype(jnp.float32)
    upbias_vals = full_upbias.astype(jnp.float32)
    factor = HEAD_DIM ** (-0.5)
    small_images, small_len, width_dim = small_tokens.shape
    half_len = large_tokens.shape[1]
    small_rows = small_images * small_len
    head_count = width_dim // HEAD_DIM
    rows_in = jnp.concatenate(
        [small_tokens.reshape(small_rows, width_dim), large_tokens.reshape(half_len, width_dim)]
    ).astype(jnp.float32)
    normed_one, norm_one_back = jax.vjp(norm_rows, rows_in, norm_vals[0], norm_vals[1])
    normed_one = normed_one.astype(jnp.bfloat16)
    qkv_bias = jnp.concatenate([bias_vals[0], jnp.zeros((width_dim,), jnp.float32), bias_vals[1]])
    qkv_rows = (
        jnp.dot(normed_one, full_qkv, preferred_element_type=jnp.float32) + qkv_bias
    ).astype(jnp.bfloat16)
    qkv_heads = qkv_rows.reshape(-1, 3, head_count, HEAD_DIM)
    small_heads = qkv_heads[:small_rows].reshape(small_images, small_len, 3, head_count, HEAD_DIM)
    query_small = small_heads[:, :, 0]
    key_small = small_heads[:, :, 1]
    value_small = small_heads[:, :, 2]
    valid_small = jnp.arange(small_len, dtype=jnp.int32)[None, :] < small_counts[:, None]
    large_heads = qkv_heads[small_rows:]
    query_large = large_heads[:, 0][None]
    key_whole, value_whole = (
        lax.all_gather(large_heads[:, 1], "seq", axis=0, tiled=True),
        lax.all_gather(large_heads[:, 2], "seq", axis=0, tiled=True),
    )
    key_large = key_whole[None]
    value_large = value_whole[None]
    valid_large = jnp.arange(key_whole.shape[0], dtype=jnp.int32)[None, :] < large_counts[:, None]
    mixed_small, total_small = attend(query_small, key_small, value_small, valid_small, factor)
    mixed_large, total_large = attend(query_large, key_large, value_large, valid_large, factor)
    mixed = jnp.concatenate(
        [mixed_small.reshape(small_rows, width_dim), mixed_large.reshape(half_len, width_dim)]
    ).astype(jnp.bfloat16)
    middle = rows_in + jnp.dot(mixed, full_out, preferred_element_type=jnp.float32) + bias_vals[2]
    normed_two, norm_two_back = jax.vjp(norm_rows, middle, norm_vals[2], norm_vals[3])
    normed_two = normed_two.astype(jnp.bfloat16)
    up_proj = jnp.dot(normed_two, full_up, preferred_element_type=jnp.float32) + upbias_vals
    act_full, gelu_back = jax.vjp(gelu_exact, up_proj)
    act_low = act_full.astype(jnp.bfloat16)
    result = middle + jnp.dot(act_low, full_down, preferred_element_type=jnp.float32) + bias_vals[3]
    result_low = result.astype(jnp.bfloat16)
    small_out = result_low[:small_rows].reshape(small_tokens.shape)
    large_out = result_low[small_rows:].reshape(large_tokens.shape)
    back_qkv, back_out, back_up, back_down = (full_qkv, full_out, full_up, full_down)
    grad_rows = jnp.concatenate(
        [small_cot.reshape(small_rows, width_dim), large_cot.reshape(half_len, width_dim)]
    )
    grad_rows_full = grad_rows.astype(jnp.float32)
    grad_down = general_rows(act_low, grad_rows)
    grad_bias_down = jnp.sum(grad_rows, 0, dtype=jnp.float32)
    grad_act = general_cols(grad_rows, back_down)
    (grad_hidden,) = gelu_back(grad_act)
    grad_hidden_low = grad_hidden.astype(jnp.bfloat16)
    grad_up = general_rows(normed_two, grad_hidden_low)
    grad_up_bias = jnp.sum(grad_hidden_low, 0, dtype=jnp.float32)
    grad_normed_two = general_cols(grad_hidden_low, back_up)
    grad_mid_norm, grad_gain_two, grad_shift_two = norm_two_back(grad_normed_two)
    grad_middle = grad_rows_full + grad_mid_norm
    grad_middle_low = grad_middle.astype(jnp.bfloat16)
    grad_out = general_rows(mixed, grad_middle_low)
    grad_bias_out = jnp.sum(grad_middle_low, 0, dtype=jnp.float32)
    grad_mixed = (
        general_cols(grad_middle_low, back_out).astype(jnp.bfloat16).reshape(-1, head_count, HEAD_DIM)
    )
    grad_mixed_small = grad_mixed[:small_rows].reshape(
        small_images, small_len, head_count, HEAD_DIM
    )
    grad_mixed_large = grad_mixed[small_rows:][None]
    gq_small, gk_small, gv_small = attend_back(
        query_small, key_small, value_small, valid_small, total_small, grad_mixed_small, factor
    )
    gq_large, gk_whole, gv_whole = attend_back(
        query_large, key_large, value_large, valid_large, total_large, grad_mixed_large, factor
    )
    gk_large, gv_large = (
        lax.psum_scatter(
            gk_whole[0].astype(jnp.bfloat16), "seq", scatter_dimension=0, tiled=True
        ).astype(jnp.float32),
        lax.psum_scatter(
            gv_whole[0].astype(jnp.bfloat16), "seq", scatter_dimension=0, tiled=True
        ).astype(jnp.float32),
    )
    grad_qkv_small = jnp.stack([gq_small, gk_small, gv_small], 2).reshape(small_rows, 3 * width_dim)
    grad_qkv_large = jnp.stack([gq_large[0], gk_large, gv_large], 1).reshape(
        half_len, 3 * width_dim
    )
    grad_qkv_low = jnp.concatenate([grad_qkv_small, grad_qkv_large]).astype(jnp.bfloat16)
    grad_qkv = general_rows(normed_one, grad_qkv_low)
    grad_bias_query = jnp.sum(grad_qkv_low[:, :width_dim], 0, dtype=jnp.float32)
    grad_bias_value = jnp.sum(grad_qkv_low[:, 2 * width_dim :], 0, dtype=jnp.float32)
    grad_normed_one = general_cols(grad_qkv_low, back_qkv)
    grad_in_norm, grad_gain_one, grad_shift_one = norm_one_back(grad_normed_one)
    grad_input = (grad_middle + grad_in_norm).astype(jnp.bfloat16)
    small_grad = grad_input[:small_rows].reshape(small_tokens.shape)
    large_grad = grad_input[small_rows:].reshape(large_tokens.shape)
    grad_norm_all = jnp.stack([grad_gain_one, grad_shift_one, grad_gain_two, grad_shift_two])
    grad_bias_all = jnp.stack([grad_bias_query, grad_bias_value, grad_bias_out, grad_bias_down])
    shard_qkv, shard_out, shard_up, shard_down, shard_norm, shard_bias, shard_up_bias = (
        lax.psum_scatter(grad_qkv, ("dp", "seq"), scatter_dimension=0, tiled=True),
        lax.psum_scatter(grad_out, ("dp", "seq"), scatter_dimension=0, tiled=True),
        lax.psum_scatter(grad_up, ("dp", "seq"), scatter_dimension=0, tiled=True),
        lax.psum_scatter(grad_down, ("dp", "seq"), scatter_dimension=0, tiled=True),
        lax.psum_scatter(grad_norm_all, ("dp", "seq"), scatter_dimension=1, tiled=True),
        lax.psum_scatter(grad_bias_all, ("dp", "seq"), scatter_dimension=1, tiled=True),
        lax.psum_scatter(grad_up_bias, ("dp", "seq"), scatter_dimension=0, tiled=True),
    )
    return (
        small_out,
        large_out,
        small_grad,
        large_grad,
        shard_qkv,
        shard_out,
        shard_up,
        shard_down,
        shard_norm,
        shard_bias,
        shard_up_bias,
    )


def solution(mesh):
    in_specs = (
        P(("dp", "seq"), None, None),
        P("dp", "seq", None),
        P(("dp", "seq")),
        P("dp"),
        P(("dp", "seq"), None, None),
        P("dp", "seq", None),
        P(("dp", "seq"), None),
        P(("dp", "seq"), None),
        P(("dp", "seq"), None),
        P(("dp", "seq"), None),
        P(None, ("dp", "seq")),
        P(None, ("dp", "seq")),
        P(("dp", "seq")),
    )
    out_specs = (
        P(("dp", "seq"), None, None),
        P("dp", "seq", None),
        P(("dp", "seq"), None, None),
        P("dp", "seq", None),
        P(("dp", "seq"), None),
        P(("dp", "seq"), None),
        P(("dp", "seq"), None),
        P(("dp", "seq"), None),
        P(None, ("dp", "seq")),
        P(None, ("dp", "seq")),
        P(("dp", "seq")),
    )
    body = shards if (mesh.shape["dp"], mesh.shape["seq"]) == (16, 2) else shards_general
    return jax.shard_map(body, mesh=mesh, in_specs=in_specs, out_specs=out_specs, check_vma=False)
```

```python
import functools

import jax
import jax.numpy as jnp
from jax import lax
from jax.experimental import pallas as pl
from jax.experimental.pallas import tpu as pltpu
from jax.sharding import PartitionSpec as P

HEAD_DIM = 64
MESH = pl.DeviceIdType.MESH
BF = jnp.bfloat16
F32 = jnp.float32


def dot(a, b):
    return lax.dot_general(a, b, (((1,), (0,)), ((), ())), preferred_element_type=F32)


def dot_rows(a, b):
    return lax.dot_general(a, b, (((0,), (0,)), ((), ())), preferred_element_type=F32)


def dot_cols(a, b):
    return lax.dot_general(a, b, (((1,), (1,)), ((), ())), preferred_element_type=F32)


def device(x, y, z, c):
    return ((z * 2 + y) * 2 + c, x)


def rcopy(src, dst, send, recv, dev):
    return pltpu.make_async_remote_copy(
        src_ref=src, dst_ref=dst, send_sem=send, recv_sem=recv, device_id=dev, device_id_type=MESH
    )


def shard_at(j):
    return j // 4, (j // 2) % 2, j % 2


def stack_halves(g):
    n = g.shape[1] // 2
    return jnp.concatenate([g[:, :n], g[:, n:]], axis=0)


def rows_of(i, size, base=0):
    return pl.ds(pl.multiple_of(base + i * size, 16), size)


def lanes_of(i, size, base=0):
    return pl.ds(pl.multiple_of(base + i * size, 128), size)


def normalize(v):
    centred = v - jnp.mean(v, -1, keepdims=True)
    scale = lax.rsqrt(jnp.mean(centred * centred, -1, keepdims=True) + 1e-06)
    return centred * scale, scale


def norm_back(v, gain, grad):
    unit, scale = normalize(v)
    lifted = grad * gain
    inner = jnp.mean(lifted * unit, -1, keepdims=True)
    return scale * (lifted - jnp.mean(lifted, -1, keepdims=True) - unit * inner), unit


def gelu_pair(h):
    p = 0.3275911 * 0.7071067811865476
    t = 1.0 / (1.0 + p * abs(h))
    e = jnp.exp(-0.5 * h * h)
    poly = ((((1.061405429 * t - 1.453152027) * t + 1.421413741) * t - 0.284496736) * t + 0.254829592) * t
    q = 0.5 * poly * e
    phi = jnp.where(h >= 0, 1.0 - q, q)
    return h * phi, phi + h * e * 0.3989422804014327


def total(v):
    return jnp.sum(v.astype(F32), 0, keepdims=True)


def heads_forward(Q, KV, MIX, LSE, bias, q0, nq, k0, nk, first, count, unroll=1):
    D = Q.shape[1]
    left = lax.broadcasted_iota(jnp.int32, (nq, 128), 1) < HEAD_DIM

    def pair(hp, _):
        q = Q[q0 : q0 + nq, lanes_of(hp, 128)] * jnp.asarray(HEAD_DIM**-0.5, BF)
        k = KV[k0 : k0 + nk, lanes_of(hp, 128)]
        v = KV[k0 : k0 + nk, lanes_of(hp, 128, D)]
        zero = jnp.zeros_like(q)
        outs = []
        for head in range(2):
            qm = jnp.where(left, q, zero) if head == 0 else jnp.where(left, zero, q)
            s = dot_cols(k, qm) + bias
            top = jnp.max(s, 0, keepdims=True)
            e = jnp.exp(s - top)
            tot = jnp.sum(e, 0, keepdims=True)
            outs.append(dot_rows(v, e.astype(BF)) * (1.0 / tot))
            LSE[pl.ds(2 * hp + head, 1), 0:nq] = top + jnp.log(tot)
        both = jnp.concatenate([outs[0][:HEAD_DIM], outs[1][HEAD_DIM:]], axis=0)
        MIX[q0 : q0 + nq, lanes_of(hp, 128)] = jnp.transpose(both).astype(BF)
        return 0

    lax.fori_loop(0, count, lambda i, _: pair(first + i, _), 0, unroll=unroll)


def heads_backward(Q, KV, MIX, DMIX, LSE, bias, q0, nq, k0, nk, first, count, unroll=1):
    D = Q.shape[1]
    left = lax.broadcasted_iota(jnp.int32, (nq, 128), 1) < HEAD_DIM
    leftk = lax.broadcasted_iota(jnp.int32, (nk, 128), 1) < HEAD_DIM

    def pair(hp, _):
        q = Q[q0 : q0 + nq, lanes_of(hp, 128)] * jnp.asarray(HEAD_DIM**-0.5, BF)
        dm = DMIX[q0 : q0 + nq, lanes_of(hp, 128)]
        k = KV[k0 : k0 + nk, lanes_of(hp, 128)]
        v = KV[k0 : k0 + nk, lanes_of(hp, 128, D)]
        zero = jnp.zeros_like(q)
        weighted = jnp.transpose(dm.astype(F32) * MIX[q0 : q0 + nq, lanes_of(hp, 128)].astype(F32))
        dqs, dks, dvs = [], [], []
        for head in range(2):
            mask = lambda u: jnp.where(left, u, zero) if head == 0 else jnp.where(left, zero, u)
            delta = jnp.sum(weighted[head * HEAD_DIM : (head + 1) * HEAD_DIM], 0, keepdims=True)
            s = dot_cols(k, mask(q)) + bias
            pr = jnp.exp(s - LSE[pl.ds(2 * hp + head, 1), 0:nq])
            dvs.append(dot(pr.astype(BF), dm))
            ds = (pr * (dot_cols(v, mask(dm)) - delta)).astype(BF)
            dks.append(dot(ds, q))
            dqs.append(dot_rows(k, ds))
        both = jnp.concatenate([dqs[0][:HEAD_DIM], dqs[1][HEAD_DIM:]], axis=0) * HEAD_DIM**-0.5
        Q[q0 : q0 + nq, lanes_of(hp, 128)] = jnp.transpose(both).astype(BF)
        KV[k0 : k0 + nk, lanes_of(hp, 128)] = jnp.where(leftk, dks[0], dks[1]).astype(BF)
        KV[k0 : k0 + nk, lanes_of(hp, 128, D)] = jnp.where(leftk, dvs[0], dvs[1]).astype(BF)
        return 0

    lax.fori_loop(0, count, lambda i, _: pair(first + i, _), 0, unroll=unroll)


def store_block(g, SP, w, h):
    for j in range(16):
        z, y, c = shard_at(j)
        for x in range(2):
            r = 48 * j + 24 * x
            SP[w, h, x, y, z, c] = stack_halves(g[r : r + 24]).astype(BF)


def store_down(g, SP, f):
    n = SP.shape[-1]
    for j in range(4):
        for x in range(2):
            for half in range(2):
                r = (2 * j + x) * 96 + 48 * half
                for h in range(2):
                    SP[2 + half, h, x, j // 2, f, j % 2] = g[r : r + 48, h * n : h * n + n].astype(BF)


def layer_kernel(
    xs, xl, cs, cl, count_s, count_l, wqkv, wout, wup, wdown, norm, bias, upbias,
    OUT, DX, gqkv, gout, gup, gdown, SGO,
    X, DY, H1, Q, KV, MIX, MID, H2, ACC, DH2, ACT, DHB, DH1P, LP, LSES, LSEL,
    WQKV, WOUT, WUP, WDOWN, SP, OWN, LC, T, LF, sp, sm, sml, SG, SGL,
    ss, rs, tsem, psem, sms, smr, gs, gr, s2, r2, credit, room,
):
    d = lax.axis_index("dp")
    x, y, z, c = lax.axis_index("seq"), (d // 2) % 2, d // 4, d % 2
    zs = [z + 1 - 2 * (z % 2), 3 - z, (z + 2) % 4]
    sib, xn, yn = device(x, y, z, 1 - c), device(1 - x, y, z, c), device(x, 1 - y, z, c)
    zn = [device(x, y, k, c) for k in zs]
    bar = pltpu.get_barrier_semaphore()
    for p in [sib, xn, yn] + zn:
        pl.semaphore_signal(bar, inc=1, device_id=p, device_id_type=MESH)

    D = xs.shape[1]
    n = D // 2
    ns, nl = xs.shape[0], xl.shape[0]
    r1 = -(-ns // 16) * 16
    rl = -(-nl // 16) * 16
    R = r1 + rl
    RK = R + rl
    RB = R // 2
    zero = functools.partial(jnp.zeros, dtype=BF)
    head = ns - ns % 16

    X[head:r1, :] = zero((r1 - head, D))
    X[R - 16 : R, :] = zero((16, D))
    X[0:ns, :] = xs[...]
    X[r1 : r1 + nl, :] = xl[...]

    blocks = [wqkv[:, k * D : (k + 1) * D] for k in range(3)] + [wout[...]]
    blocks = [stack_halves(g) for g in blocks]
    blocks += [wdown[48 * (b // 2) : 48 * (b // 2) + 48, (b % 2) * n : (b % 2) * n + n] for b in range(4)]
    blocks += [stack_halves(wup[:, k * D : (k + 1) * D]) for k in range(4)]
    for b, g in enumerate(blocks):
        OWN[b // 2, b % 2] = g.astype(BF)
    for w in range(6):
        SP[w, c, x, y, z, c] = OWN[w, c]
    pl.semaphore_wait(bar, 6)
    swaps = [rcopy(OWN.at[w, 1 - c], SP.at[w, 1 - c, x, y, z, c], ss.at[w, 0], rs.at[w, 0], sib) for w in range(6)]
    for cp in swaps:
        cp.start()
    tcp = rcopy(X.at[r1:R], X.at[R:RK], tsem.at[0], tsem.at[1], xn)

    me = d * 2 + x
    k, m = norm.shape[1], upbias.shape[1]

    def placed(v, start):
        wide = jnp.concatenate([v, jnp.zeros((v.shape[0], D - v.shape[1]), F32)], axis=1)
        return pltpu.roll(wide, start, 1)

    row = lax.broadcasted_iota(jnp.int32, (8, D), 0)
    both = jnp.concatenate([norm[...], bias[...]], axis=0).astype(BF).astype(F32)
    sm[0:8, :] = placed(both, me * k)
    ub = placed(jnp.broadcast_to(upbias[...].astype(BF).astype(F32), (8, m)), lax.rem(me * m, D))
    sm[8:16, :] = jnp.where(row == (me * m) // D, ub, 0.0)

    def join(buf, land, send, recv, ks, devs):
        cps = [rcopy(buf, land.at[i], send.at[i], recv.at[i], dev) for i, dev in zip(ks, devs)]

        def start():
            for cp in cps:
                cp.start()

        def finish():
            for cp in cps:
                cp.wait()
            tot = buf[...]
            for i in ks:
                tot = tot + land[i]
            buf[...] = tot

        return start, finish

    def joins(buf, land, send, recv):
        return [
            join(buf, land, send, recv, *a) for a in (([0], [sib]), ([1], [xn]), ([2], [yn]), ([3, 4, 5], zn))
        ]

    smalls = joins(sm, sml, sms, smr)

    pieces = [z] + zs

    def by_core(run):
        for core in range(2):
            pl.when(c == core)(lambda core=core: run(core))

    def mail(w, sem, dev, out, back):
        sent, got = SP.at[(w, c) + out], SP.at[(w, c) + back]
        return (
            rcopy(sent, sent, ss.at[w, sem], rs.at[w, sem], dev),
            rcopy(got, got, ss.at[w, sem], rs.at[w, sem], dev),
        )

    def mails(w, core):
        if core == 0:
            one = [mail(w, 1 + i, zn[i], (x, y, z), (x, y, zs[i])) for i in range(3)]
            two = [mail(w, 4 + k, yn, (x, y, p), (x, 1 - y, p)) for k, p in enumerate(pieces)]
            three = [mail(w, 8 + k, xn, (x, y, p), (1 - x, y, p)) for k, p in enumerate(pieces)]
            three += [mail(w, 12 + k, xn, (x, 1 - y, p), (1 - x, 1 - y, p)) for k, p in enumerate(pieces)]
        else:
            one = [mail(w, 1, xn, (x, y, z), (1 - x, y, z))]
            two = [mail(w, 2 + i, zn[i], (x, y, z), (x, y, zs[i])) for i in range(3)]
            two += [mail(w, 5 + i, zn[i], (1 - x, y, z), (1 - x, y, zs[i])) for i in range(3)]
            three = [mail(w, 8 + k, yn, (x, y, p), (x, 1 - y, p)) for k, p in enumerate(pieces)]
            three += [mail(w, 12 + k, yn, (1 - x, y, p), (1 - x, 1 - y, p)) for k, p in enumerate(pieces)]
        return one, two, three

    def a1(w):
        swaps[w].wait()

        def run(core):
            one, two, three = mails(w, core)
            first = one + (two[0:1] + three[0:1] if core == 0 else two[0:3] + three[0:1])
            for sent, _ in first:
                sent.start()

        by_core(run)

    def a2(w):
        def run(core):
            one, two, three = mails(w, core)
            for i, (_, got) in enumerate(one):
                got.wait_recv()
                onward = [two[1 + i], three[1 + i]] if core == 0 else two[3:6] + three[4:5]
                for sent, _ in onward:
                    sent.start()

        by_core(run)

    def a3(w):
        def run(core):
            _, two, three = mails(w, core)
            if core == 0:
                for k in range(4):
                    two[k][1].wait_recv()
                    three[4 + k][0].start()
            else:
                for part in range(2):
                    for i in range(3):
                        two[3 * part + i][1].wait_recv()
                        three[4 * part + 1 + i][0].start()

        by_core(run)

    def a4(w):
        def run(core):
            one, two, three = mails(w, core)
            for _, got in three:
                got.wait_recv()
            for sent, _ in one + two + three:
                sent.wait_send()

        by_core(run)
        src = SP.at[w, c]
        rcopy(src, src, ss.at[w, 16], rs.at[w, 16], sib).start()

    def assemble(w, h, dst, col):
        def step(j, _):
            pz, py, pc = shard_at(j)
            a = SP[w, h, 0, py, pz, pc].astype(F32)
            e = SP[w, h, 1, py, pz, pc].astype(F32)
            dst[rows_of(j, 48), col : col + n] = jnp.concatenate([a[:24], e[:24]], axis=0).astype(BF)
            dst[rows_of(j, 48), col + n : col + D] = jnp.concatenate([a[24:], e[24:]], axis=0).astype(BF)
            return 0

        lax.fori_loop(0, 16, step, 0, unroll=4)

    def assemble_down(w, h):
        def step(j, _):
            pz, py, pc = shard_at(j)
            for px in range(2):
                rows = pl.ds(pl.multiple_of(96 * (2 * j + px) + 48 * (w - 2), 16), 48)
                WDOWN[rows, n * h : n * h + n] = SP[w, h, px, py, pz, pc]
            return 0

        lax.fori_loop(0, 16, step, 0, unroll=4)

    def a5(w):
        src, dst = SP.at[w, c], SP.at[w, 1 - c]
        rcopy(src, src, ss.at[w, 16], rs.at[w, 16], sib).wait_send()
        rcopy(dst, dst, ss.at[w, 16], rs.at[w, 16], sib).wait_recv()
        for h in range(2):
            b = 2 * w + h
            if b < 3:
                assemble(w, h, WQKV, b * D)
            elif b == 3:
                assemble(w, h, WOUT, 0)
            elif b < 8:
                assemble_down(w, h)
            else:
                assemble(w, h, WUP, (b - 8) * D)

    def credits(w):
        for i, dev in enumerate([xn, yn] + zn):
            pl.semaphore_signal(room.at[i], inc=1, device_id=dev, device_id_type=MESH)

    order = [4, 5, 2, 3, 1, 0]
    backs = [zs[2], zs[1], zs[0], z]

    def add(w, dst, src, count):
        def step(i, _):
            at = (w, c) + dst(i)
            SP[at] = (SP[at].astype(F32) + src(i).astype(F32)).astype(BF)
            return 0

        lax.fori_loop(0, count, step, 0, unroll=min(count, 4))

    def first_copy(i, k):
        w = order[i]
        return rcopy(SP.at[w, 1 - c, :, :, k], LC.at[i % 2, :, :, k], s2.at[w, k], r2.at[w, k], sib)

    def go(i):
        if i >= 2:
            pl.semaphore_wait(credit, 1)
        for k in range(4):
            first_copy(i, k).start()

    def second_copy(w, k, core):
        pz = backs[k]
        dev = (xn, yn)[core]
        src = (SP.at[w, c, 1 - x, :, pz], SP.at[w, c, :, 1 - y, pz])[core]
        return rcopy(src, SP.at[w, 1 - c, 0, :, k], s2.at[w, 4 + k], r2.at[w, 4 + k], dev)

    def third_copy(w, k, core):
        pz = backs[k]
        if core == 0:
            return rcopy(SP.at[w, c, x, 1 - y, pz], SP.at[w, 1 - c, 1, 0, k], s2.at[w, 8 + k], r2.at[w, 8 + k], yn)
        return rcopy(SP.at[w, c, :, y, pz], SP.at[w, 1 - c, 1, :, k], s2.at[w, 8 + k], r2.at[w, 8 + k], zn[2 - k])

    def fourth_copy(w, k, core):
        if core == 0:
            return rcopy(
                SP.at[w, c, x, y, backs[k]], SP.at[w, 1 - c, 1, 1, k], s2.at[w, 12 + k], r2.at[w, 12 + k], zn[2 - k]
            )
        return rcopy(SP.at[w, c, 1 - x, y, z], SP.at[w, 1 - c, 1, 0, 3], s2.at[w, 12], r2.at[w, 12], xn)

    def last_copy(w):
        return rcopy(T.at[w, 1 - c], LF.at[w], s2.at[w, 15], r2.at[w, 15], sib)

    def deliver(w):
        mine, other = T[w, c], LF[w]
        for h in range(2):
            g = jnp.where(c == h, mine, other)
            b = 2 * w + h
            if 4 <= b < 8:
                half = (b - 4) // 2
                gdown[48 * half : 48 * half + 48, n * h : n * h + n] = g
                continue
            wide = jnp.concatenate([g[0:24], g[24:48]], axis=1)
            if b >= 8:
                gup[:, (b - 8) * D : (b - 7) * D] = wide
            elif b == 2:
                gout[...] = wide
            else:
                g0 = (3, 2, None, 1)[b] - 1
                third = D // 3
                for part in range(3):
                    lo = part * D + g0 * third
                    gqkv[:, lo : lo + third] = wide[:, part * third : (part + 1) * third]

    def back(i, stage):
        w = order[i]
        if stage == 0:
            for k in range(4):
                first_copy(i, k).wait()
                idx = lambda j: (j // 4, (j // 2) % 2, k, j % 2)
                add(w, idx, lambda j: LC[(i % 2,) + idx(j)], 8)
            if i < 4:
                pl.semaphore_signal(credit, inc=1, device_id=sib, device_id_type=MESH)
            credits(w)
        elif stage == 1:

            def run(core):
                pl.semaphore_wait(room.at[core], 1)
                for k in range(4):
                    second_copy(w, k, core).start()

            by_core(run)
        elif stage == 2:

            def run(core):
                if core == 0:
                    pl.semaphore_wait(room.at[1], 1)
                for k in range(4):
                    second_copy(w, k, core).wait()
                    place = ((lambda j: (x, j // 2, backs[k], j % 2)), (lambda j: (j // 2, y, backs[k], j % 2)))[core]
                    add(w, place, lambda j: SP[w, 1 - c, 0, j // 2, k, j % 2], 4)
                    if core == 1 and k < 3:
                        pl.semaphore_wait(room.at[2 + 2 - k], 1)
                    if core == 0 or k < 3:
                        third_copy(w, k, core).start()

            by_core(run)
        elif stage == 3:

            def run(core):
                if core == 0:
                    for k in range(4):
                        third_copy(w, k, core).wait()
                        add(w, lambda j: (x, y, backs[k], j), lambda j: SP[w, 1 - c, 1, 0, k, j], 2)
                        if k < 3:
                            pl.semaphore_wait(room.at[2 + 2 - k], 1)
                            fourth_copy(w, k, core).start()
                    return
                for k in range(3):
                    third_copy(w, k, core).wait()
                three = lambda j: sum(SP[w, 1 - c, 1, j // 2, k, j % 2].astype(F32) for k in range(3))
                add(w, lambda j: (j // 2, y, z, j % 2), three, 4)
                pl.semaphore_wait(room.at[0], 1)
                fourth_copy(w, 0, core).start()

            by_core(run)
        elif stage == 4:

            def run(core):
                count = 3 if core == 0 else 1
                for k in range(count):
                    fourth_copy(w, k, core).wait()
                for q in range(2):
                    tot = SP[w, c, x, y, z, q].astype(F32)
                    for k in range(count):
                        at = (1, 1, k, q) if core == 0 else (1, 0, 3, q)
                        tot = tot + SP[(w, 1 - c) + at].astype(F32)
                    T[w, q] = tot

            by_core(run)
            last_copy(w).start()
        else:
            last_copy(w).wait()
            deliver(w)

    def norm_one(base, count):
        def step(i, _):
            rows = rows_of(i, size, base)
            unit, _ = normalize(X[rows, :].astype(F32))
            H1[rows, :] = (unit * sp[0:1, :] + sp[1:2, :]).astype(BF)
            return 0

        size = RB if count % RB == 0 else count
        lax.fori_loop(0, count // size, step, 0)

    small_count, large_count = count_s[0], count_l[0]
    kj = lax.broadcasted_iota(jnp.int32, (r1, 1), 0)
    bias_small = jnp.where(kj < small_count, 0.0, -1e30)
    kj = lax.broadcasted_iota(jnp.int32, (2 * rl, 1), 0)
    mine = kj < rl
    inside = jnp.where(mine, kj, kj - rl)
    where = inside + jnp.where(mine, x, 1 - x) * nl
    bias_large = jnp.where((inside < nl) & (where < large_count), 0.0, -1e30)
    small_part = (bias_small, 0, r1, 0, r1)
    large_part = (bias_large, r1, rl, r1, 2 * rl)

    def take_cotangents():
        DY[head:r1, :] = zero((r1 - head, D))
        DY[R - 16 : R, :] = zero((16, D))
        DY[0:ns, :] = cs[...]
        DY[r1 : r1 + nl, :] = cl[...]

    def know_smalls():
        smalls[3][1]()
        sp[...] = sm[...]

    def query():
        Q[...] = (dot(H1[0:R, :], WQKV[:, 0:D]) + sp[4:5, :]).astype(BF)

    def key():
        KV[:, 0:D] = dot(H1[...], WQKV[:, D : 2 * D]).astype(BF)

    def value():
        KV[:, D:] = (dot(H1[...], WQKV[:, 2 * D :]) + sp[5:6, :]).astype(BF)

    def attend_small():
        heads_forward(Q, KV, MIX, LSES, *small_part, 0, 6, unroll=2)

    def attend_large(hp):
        heads_forward(Q, KV, MIX, LSEL, *large_part, hp, 1)

    def project_out():
        MID[...] = dot(MIX[...], WOUT[...])

    def second_norm():
        def step(i, _):
            rows = rows_of(i, RB)
            middle = X[rows, :].astype(F32) + MID[rows, :] + sp[6:7, :]
            MID[rows, :] = middle
            unit, _ = normalize(middle)
            H2[rows, :] = (unit * sp[2:3, :] + sp[3:4, :]).astype(BF)
            ACC[rows, :] = middle + sp[7:8, :]
            return 0

        lax.fori_loop(0, R // RB, step, 0)

    def hidden_units(f):
        hidden = dot(H2[...], WUP[:, lanes_of(f, D)]) + sp[pl.ds(8 + f, 1), :]
        dact = dot_cols(DY[...], WDOWN[rows_of(f, D), :])
        act, slope = gelu_pair(hidden)
        ACT[...] = act.astype(BF)
        dh = (dact * slope).astype(BF)
        DHB[...] = dh
        SG[pl.ds(8 + f, 1), :] = total(dh)

    def grad_up(f):
        store_block(dot_rows(H2[...], DHB[...]), SP, 4 + f // 2, f % 2)

    def grad_down(f):
        store_down(dot_rows(ACT[...], DY[...]), SP, f)

    def forward_down(f):
        ACC[...] += dot(ACT[...], WDOWN[rows_of(f, D), :])

    def backward_up(f):
        DH2[...] += dot_cols(DHB[...], WUP[:, lanes_of(f, D)])

    def give_out():
        OUT[...] = ACC[...].astype(BF)

    z1 = jnp.zeros((1, D), F32)

    def second_norm_back():
        def step(i, sums):
            rows = rows_of(i, RB)
            grad = DH2[rows, :]
            dy = DY[rows, :].astype(F32)
            dv, unit = norm_back(MID[rows, :], sp[2:3, :], grad)
            dmid = dy + dv
            MID[rows, :] = dmid
            low = dmid.astype(BF)
            H2[rows, :] = low
            return sums[0] + total(grad * unit), sums[1] + total(grad), sums[2] + total(low), sums[3] + total(dy)

        sums = lax.fori_loop(0, R // RB, step, (z1, z1, z1, z1))
        for i, at in enumerate((2, 3, 6, 7)):
            SG[at : at + 1, :] = sums[i]

    def grad_mixed():
        ACT[...] = dot_cols(H2[...], WOUT[...]).astype(BF)

    def grad_out():
        store_block(dot_rows(MIX[...], H2[...]), SP, 1, 0)

    third = D // 3

    def back_small(g):
        heads_backward(Q, KV, MIX, ACT, LSES, *small_part, 2 * g, 2, unroll=2)

    def back_large(hp):
        heads_backward(Q, KV, MIX, ACT, LSEL, *large_part, hp, 1)

    def grad_heads(g):
        lo, lov = lanes_of(g, third), lanes_of(g, third, D)
        grads = [dot_rows(H1[0:R, :], Q[:, lo]), dot_rows(H1[...], KV[:, lo]), dot_rows(H1[...], KV[:, lov])]
        store_block(jnp.concatenate(grads, axis=1), SP, (2 - g) // 2, 1 - g // 2)

    pcp = rcopy(DH1P, LP, psem.at[0], psem.at[1], xn)

    def grad_partner():
        g = dot_cols(KV[R:RK, 0:D], WQKV[:, D : 2 * D]) + dot_cols(KV[R:RK, D:], WQKV[:, 2 * D :])
        DH1P[...] = g.astype(BF)

    def grad_normed():
        ACC[...] = dot_cols(Q[...], WQKV[:, 0:D]) + dot_cols(KV[0:R, 0:D], WQKV[:, D : 2 * D])
        ACC[...] += dot_cols(KV[0:R, D:], WQKV[:, 2 * D :])

    def first_norm_back(base, count, partner):
        rows = slice(base, base + count)
        grad = ACC[rows, :]
        if partner:
            grad = grad + LP[...].astype(F32)
        dv, _ = norm_back(X[rows, :].astype(F32), sp[0:1, :], grad)
        DX[rows, :] = (MID[rows, :] + dv).astype(BF)

    ends = joins(SG, SGL, gs, gr)

    def first_norm_sums():
        def step(i, sums):
            unit, _ = normalize(X[rows_of(i, RB), :].astype(F32))
            grad = ACC[rows_of(i, RB), :]
            return sums[0] + total(grad * unit), sums[1] + total(grad)

        sums = lax.fori_loop(0, R // RB, step, (z1, z1))
        unit, _ = normalize(X[R:RK, :].astype(F32))
        grad = DH1P[...].astype(F32)
        SG[0:1, :] = sums[0] + total(grad * unit)
        SG[1:2, :] = sums[1] + total(grad)
        SG[4:5, :] = total(Q[...])
        SG[5:6, :] = total(KV[:, D:])

    def clear():
        SG[...] = jnp.zeros(SG.shape, F32)
        DH2[...] = jnp.zeros(DH2.shape, F32)

    def repeat(count, body, after):
        def step(i, _):
            for k, do in enumerate(body):
                do(i)
                for j in range(count):
                    if after[j][k]:
                        pl.when(i == j)(after[j][k])
            return 0

        lax.fori_loop(0, count, step, 0)

    clear()
    a1(0)
    smalls[0][0]()
    a1(1)
    smalls[0][1]()
    take_cotangents()
    smalls[1][0]()
    a2(0)
    a3(0)
    smalls[1][1]()
    tcp.start()
    smalls[2][0]()
    smalls[2][1]()
    a2(1)
    a4(0)
    smalls[3][0]()
    a3(1)
    a1(2)
    know_smalls()
    a4(1)
    a5(0)
    norm_one(0, R)
    tcp.wait()
    norm_one(R, rl)
    a2(2)
    a1(3)
    a1(4)
    query()
    key()
    a5(1)
    value()
    a2(3)
    a2(4)

    def then_0():
        a3(2)
        a1(5)

    def then_1():
        a3(3)

    repeat(6, (attend_large,), ((None,), (then_0,), (None,), (None,), (then_1,), (None,),))
    a3(4)
    a4(2)
    attend_small()
    a2(5)
    a5(2)
    a4(3)
    project_out()
    a4(4)
    second_norm()
    a5(3)
    a5(4)

    def then_2():
        a3(5)

    def then_3():
        a4(5)
        go(0)

    def then_4():
        a5(5)
        back(0, 0)

    def then_5():
        back(0, 1)

    def then_6():
        go(1)

    def then_7():
        go(2)

    repeat(4, (hidden_units, grad_up, grad_down, backward_up, forward_down,), ((then_2, None, None, None, None), (None, then_3, None, None, then_4), (None, then_5, None, None, None), (None, then_6, None, then_7, None),))
    back(1, 0)
    give_out()
    back(0, 2)
    back(2, 0)
    back(1, 1)
    second_norm_back()
    grad_mixed()
    grad_out()
    back(2, 1)

    def then_8():
        go(3)

    def then_9():
        back(0, 3)
        back(3, 0)
        back(1, 2)

    def then_10():
        go(4)
        back(2, 2)
        back(0, 4)

    def then_11():
        back(4, 0)
        back(1, 3)
        back(3, 1)

    def then_12():
        back(2, 3)

    def then_13():
        back(4, 1)

    def then_14():
        back(3, 2)

    repeat(3, (back_small, lambda g: back_large(2 * g), lambda g: back_large(2 * g + 1), grad_heads,), ((then_8, then_9, None, None), (then_10, then_11, None, then_12), (then_13, then_14, None, None),))
    go(5)
    back(4, 2)
    back(1, 4)
    back(5, 0)
    grad_partner()
    back(3, 3)
    back(2, 4)
    back(5, 1)
    grad_normed()
    first_norm_sums()
    ends[0][0]()
    first_norm_back(0, r1, False)
    back(4, 3)
    ends[0][1]()
    ends[1][0]()
    back(0, 5)
    back(1, 5)
    back(5, 2)
    pcp.start()
    back(3, 4)
    back(2, 5)
    back(5, 3)
    ends[1][1]()
    ends[2][0]()
    ends[2][1]()
    ends[3][0]()
    pcp.wait()
    back(4, 4)
    back(5, 4)
    first_norm_back(r1, rl, True)
    back(3, 5)
    back(4, 5)
    ends[3][1]()
    back(5, 5)
    SGO[...] = SG[...]


def deliver_kernel(
    OUT, DX, gqkv, gout, gup, gdown, SG,
    outs, outl, dxs, dxl, oqkv, oout, oup, odown, onorm, obias, oub,
):
    ns, nl = outs.shape[0], outl.shape[0]
    r1 = -(-ns // 16) * 16
    outs[...] = OUT[0:ns, :]
    outl[...] = OUT[r1 : r1 + nl, :]
    dxs[...] = DX[0:ns, :]
    dxl[...] = DX[r1 : r1 + nl, :]
    oqkv[...] = gqkv[...]
    oout[...] = gout[...]
    oup[...] = gup[...]
    odown[...] = gdown[...]
    D = outs.shape[1]
    me = lax.axis_index("dp") * 2 + lax.axis_index("seq")
    k, m = onorm.shape[1], oub.shape[1]
    near = pltpu.roll(SG[0:8, :], lax.rem(D - me * k, D), 1)[:, 0:k]
    onorm[...] = near[0:4]
    obias[...] = near[4:8]
    row = lax.broadcasted_iota(jnp.int32, (8, D), 0)
    picked = total(jnp.where(row == (me * m) // D, SG[8:16, :], 0.0))
    near = pltpu.roll(jnp.broadcast_to(picked, (8, D)), lax.rem(D - lax.rem(me * m, D), D), 1)
    oub[...] = near[0:1, 0:m]


def vm():
    return pl.BlockSpec(memory_space=pltpu.VMEM)


def layer(xs, xl, cs, cl, count_s, count_l, wqkv, wout, wup, wdown, norm, bias, upbias):
    D = xs.shape[1]
    n = D // 2
    r1 = -(-xs.shape[0] // 16) * 16
    rl = -(-xl.shape[0] // 16) * 16
    R = r1 + rl
    RK = R + rl
    sds = jax.ShapeDtypeStruct
    smem = pl.BlockSpec(memory_space=pltpu.SMEM)
    dma, regular = pltpu.SemaphoreType.DMA, pltpu.SemaphoreType.REGULAR
    small = (16, D)
    return pl.pallas_call(
        layer_kernel,
        out_shape=(
            sds((R, D), BF), sds((R, D), BF),
            sds(wqkv.shape, F32), sds(wout.shape, F32), sds(wup.shape, F32), sds(wdown.shape, F32), sds(small, F32),
        ),
        in_specs=[vm()] * 4 + [smem] * 2 + [vm()] * 7,
        out_specs=(vm(),) * 7,
        scratch_shapes=[
            pltpu.VMEM((RK, D), BF),
            pltpu.VMEM((R, D), BF),
            pltpu.VMEM((RK, D), BF),
            pltpu.VMEM((R, D), BF),
            pltpu.VMEM((RK, 2 * D), BF),
            pltpu.VMEM((R, D), BF),
            pltpu.VMEM((R, D), F32),
            pltpu.VMEM((R, D), BF),
            pltpu.VMEM((R, D), F32),
            pltpu.VMEM((R, D), F32),
            pltpu.VMEM((R, D), BF),
            pltpu.VMEM((R, D), BF),
            pltpu.VMEM((rl, D), BF),
            pltpu.VMEM((rl, D), BF),
            pltpu.VMEM((16, r1), F32),
            pltpu.VMEM((16, rl), F32),
            pltpu.VMEM((D, 3 * D), BF),
            pltpu.VMEM((D, D), BF),
            pltpu.VMEM((D, 4 * D), BF),
            pltpu.VMEM((4 * D, D), BF),
            pltpu.VMEM((6, 2, 2, 2, 4, 2, 48, n), BF),
            pltpu.VMEM((6, 2, 48, n), BF),
            pltpu.VMEM((2, 2, 2, 4, 2, 48, n), BF),
            pltpu.VMEM((6, 2, 48, n), F32),
            pltpu.VMEM((6, 48, n), F32),
            pltpu.VMEM(small, F32),
            pltpu.VMEM(small, F32),
            pltpu.VMEM((6,) + small, F32),
            pltpu.VMEM(small, F32),
            pltpu.VMEM((6,) + small, F32),
            dma((6, 17)), dma((6, 17)), dma((2,)), dma((2,)), dma((6,)), dma((6,)), dma((6,)), dma((6,)),
            dma((6, 16)), dma((6, 16)), regular, regular((5,)),
        ],
        compiler_params=pltpu.CompilerParams(collective_id=1, has_side_effects=True, vmem_limit_bytes=63 << 20),
        name="layer",
    )(xs, xl, cs, cl, count_s, count_l, wqkv, wout, wup, wdown, norm, bias, upbias)


def shards(
    small_tokens, large_tokens, small_counts, large_counts, small_cot, large_cot,
    w_qkv, w_out, w_up, w_down, norm_params, proj_bias, up_bias,
):
    flat = lambda v: v.reshape(v.shape[1:])
    xs, xl, cs, cl = flat(small_tokens), flat(large_tokens), flat(small_cot), flat(large_cot)
    made = layer(
        xs, xl, cs, cl, small_counts, large_counts, w_qkv, w_out, w_up, w_down, norm_params, proj_bias, up_bias[None]
    )
    like = (xs, xl, xs, xl, w_qkv, w_out, w_up, w_down, norm_params, proj_bias, up_bias[None])
    outs, outl, dxs, dxl, gqkv, gout, gup, gdown, gnorm, gbias, gub = pl.pallas_call(
        deliver_kernel,
        out_shape=tuple(jax.ShapeDtypeStruct(v.shape, v.dtype) for v in like),
        in_specs=[vm()] * 7,
        out_specs=(vm(),) * 11,
        compiler_params=pltpu.CompilerParams(vmem_limit_bytes=62 << 20),
        name="deliver",
    )(*made)
    return outs[None], outl[None], dxs[None], dxl[None], gqkv, gout, gup, gdown, gnorm, gbias, gub[0]


def norm_rows(values, gain, shift):
    centre = jnp.mean(values, -1, keepdims=True)
    centered = values - centre
    spread = jnp.mean(centered * centered, -1, keepdims=True)
    return centered * lax.rsqrt(spread + 1e-06) * gain + shift


def gelu_exact(values):
    return jax.nn.gelu(values, approximate=False)


def general_rows(left, right):
    return lax.dot_general(
        left, right, (((0,), (0,)), ((), ())), preferred_element_type=jnp.float32
    )


def general_cols(left, right):
    return lax.dot_general(
        left, right, (((1,), (1,)), ((), ())), preferred_element_type=jnp.float32
    )


def attend(query, key_part, value, valid_keys, factor):
    raw_scores = jnp.einsum("bqhe,bkhe->bhqk", query, key_part, preferred_element_type=jnp.float32)
    scaled = jnp.where(valid_keys[:, None, None, :], raw_scores * factor, -1e30)
    row_top = jnp.max(scaled, -1, keepdims=True)
    expo_rows = jnp.exp(scaled - row_top)
    totals = jnp.sum(expo_rows, -1, keepdims=True)
    probs_full = expo_rows / totals
    mixed = jnp.einsum(
        "bhqk,bkhe->bqhe",
        probs_full.astype(jnp.bfloat16),
        value,
        preferred_element_type=jnp.float32,
    )
    return (mixed, row_top + jnp.log(totals))


def attend_back(query, key_part, value, valid_keys, log_total, grad_mixed, factor):
    raw_scores = jnp.einsum("bqhe,bkhe->bhqk", query, key_part, preferred_element_type=jnp.float32)
    scaled = jnp.where(valid_keys[:, None, None, :], raw_scores * factor, -1e30)
    probs_full = jnp.exp(scaled - log_total)
    grad_value = jnp.einsum(
        "bhqk,bqhe->bkhe",
        probs_full.astype(jnp.bfloat16),
        grad_mixed,
        preferred_element_type=jnp.float32,
    )
    grad_probs = jnp.einsum(
        "bqhe,bkhe->bhqk", grad_mixed, value, preferred_element_type=jnp.float32
    )
    row_delta = jnp.sum(probs_full * grad_probs, -1, keepdims=True)
    grad_raw = (probs_full * (grad_probs - row_delta) * factor).astype(jnp.bfloat16)
    grad_query = jnp.einsum(
        "bhqk,bkhe->bqhe", grad_raw, key_part, preferred_element_type=jnp.float32
    )
    grad_key = jnp.einsum("bhqk,bqhe->bkhe", grad_raw, query, preferred_element_type=jnp.float32)
    return (grad_query, grad_key, grad_value)


def shards_general(
    small_tokens,
    large_tokens,
    small_counts,
    large_counts,
    small_cot,
    large_cot,
    w_qkv,
    w_out,
    w_up,
    w_down,
    norm_params,
    proj_bias,
    up_bias,
):
    gathered = (
        lax.all_gather(w_qkv.astype(jnp.bfloat16), ("dp", "seq"), axis=0, tiled=True),
        lax.all_gather(w_out.astype(jnp.bfloat16), ("dp", "seq"), axis=0, tiled=True),
        lax.all_gather(w_up.astype(jnp.bfloat16), ("dp", "seq"), axis=0, tiled=True),
        lax.all_gather(w_down.astype(jnp.bfloat16), ("dp", "seq"), axis=0, tiled=True),
        lax.all_gather(norm_params.astype(jnp.bfloat16), ("dp", "seq"), axis=1, tiled=True),
        lax.all_gather(proj_bias.astype(jnp.bfloat16), ("dp", "seq"), axis=1, tiled=True),
        lax.all_gather(up_bias.astype(jnp.bfloat16), ("dp", "seq"), axis=0, tiled=True),
    )
    full_qkv, full_out, full_up, full_down, full_norm, full_bias, full_upbias = gathered
    norm_vals = full_norm.astype(jnp.float32)
    bias_vals = full_bias.astype(jnp.float32)
    upbias_vals = full_upbias.astype(jnp.float32)
    factor = HEAD_DIM ** (-0.5)
    small_images, small_len, width_dim = small_tokens.shape
    half_len = large_tokens.shape[1]
    small_rows = small_images * small_len
    head_count = width_dim // HEAD_DIM
    rows_in = jnp.concatenate(
        [small_tokens.reshape(small_rows, width_dim), large_tokens.reshape(half_len, width_dim)]
    ).astype(jnp.float32)
    normed_one, norm_one_back = jax.vjp(norm_rows, rows_in, norm_vals[0], norm_vals[1])
    normed_one = normed_one.astype(jnp.bfloat16)
    qkv_bias = jnp.concatenate([bias_vals[0], jnp.zeros((width_dim,), jnp.float32), bias_vals[1]])
    qkv_rows = (
        jnp.dot(normed_one, full_qkv, preferred_element_type=jnp.float32) + qkv_bias
    ).astype(jnp.bfloat16)
    qkv_heads = qkv_rows.reshape(-1, 3, head_count, HEAD_DIM)
    small_heads = qkv_heads[:small_rows].reshape(small_images, small_len, 3, head_count, HEAD_DIM)
    query_small = small_heads[:, :, 0]
    key_small = small_heads[:, :, 1]
    value_small = small_heads[:, :, 2]
    valid_small = jnp.arange(small_len, dtype=jnp.int32)[None, :] < small_counts[:, None]
    large_heads = qkv_heads[small_rows:]
    query_large = large_heads[:, 0][None]
    key_whole, value_whole = (
        lax.all_gather(large_heads[:, 1], "seq", axis=0, tiled=True),
        lax.all_gather(large_heads[:, 2], "seq", axis=0, tiled=True),
    )
    key_large = key_whole[None]
    value_large = value_whole[None]
    valid_large = jnp.arange(key_whole.shape[0], dtype=jnp.int32)[None, :] < large_counts[:, None]
    mixed_small, total_small = attend(query_small, key_small, value_small, valid_small, factor)
    mixed_large, total_large = attend(query_large, key_large, value_large, valid_large, factor)
    mixed = jnp.concatenate(
        [mixed_small.reshape(small_rows, width_dim), mixed_large.reshape(half_len, width_dim)]
    ).astype(jnp.bfloat16)
    middle = rows_in + jnp.dot(mixed, full_out, preferred_element_type=jnp.float32) + bias_vals[2]
    normed_two, norm_two_back = jax.vjp(norm_rows, middle, norm_vals[2], norm_vals[3])
    normed_two = normed_two.astype(jnp.bfloat16)
    up_proj = jnp.dot(normed_two, full_up, preferred_element_type=jnp.float32) + upbias_vals
    act_full, gelu_back = jax.vjp(gelu_exact, up_proj)
    act_low = act_full.astype(jnp.bfloat16)
    result = middle + jnp.dot(act_low, full_down, preferred_element_type=jnp.float32) + bias_vals[3]
    result_low = result.astype(jnp.bfloat16)
    small_out = result_low[:small_rows].reshape(small_tokens.shape)
    large_out = result_low[small_rows:].reshape(large_tokens.shape)
    back_qkv, back_out, back_up, back_down = (full_qkv, full_out, full_up, full_down)
    grad_rows = jnp.concatenate(
        [small_cot.reshape(small_rows, width_dim), large_cot.reshape(half_len, width_dim)]
    )
    grad_rows_full = grad_rows.astype(jnp.float32)
    grad_down = general_rows(act_low, grad_rows)
    grad_bias_down = jnp.sum(grad_rows, 0, dtype=jnp.float32)
    grad_act = general_cols(grad_rows, back_down)
    (grad_hidden,) = gelu_back(grad_act)
    grad_hidden_low = grad_hidden.astype(jnp.bfloat16)
    grad_up = general_rows(normed_two, grad_hidden_low)
    grad_up_bias = jnp.sum(grad_hidden_low, 0, dtype=jnp.float32)
    grad_normed_two = general_cols(grad_hidden_low, back_up)
    grad_mid_norm, grad_gain_two, grad_shift_two = norm_two_back(grad_normed_two)
    grad_middle = grad_rows_full + grad_mid_norm
    grad_middle_low = grad_middle.astype(jnp.bfloat16)
    grad_out = general_rows(mixed, grad_middle_low)
    grad_bias_out = jnp.sum(grad_middle_low, 0, dtype=jnp.float32)
    grad_mixed = (
        general_cols(grad_middle_low, back_out).astype(jnp.bfloat16).reshape(-1, head_count, HEAD_DIM)
    )
    grad_mixed_small = grad_mixed[:small_rows].reshape(
        small_images, small_len, head_count, HEAD_DIM
    )
    grad_mixed_large = grad_mixed[small_rows:][None]
    gq_small, gk_small, gv_small = attend_back(
        query_small, key_small, value_small, valid_small, total_small, grad_mixed_small, factor
    )
    gq_large, gk_whole, gv_whole = attend_back(
        query_large, key_large, value_large, valid_large, total_large, grad_mixed_large, factor
    )
    gk_large, gv_large = (
        lax.psum_scatter(
            gk_whole[0].astype(jnp.bfloat16), "seq", scatter_dimension=0, tiled=True
        ).astype(jnp.float32),
        lax.psum_scatter(
            gv_whole[0].astype(jnp.bfloat16), "seq", scatter_dimension=0, tiled=True
        ).astype(jnp.float32),
    )
    grad_qkv_small = jnp.stack([gq_small, gk_small, gv_small], 2).reshape(small_rows, 3 * width_dim)
    grad_qkv_large = jnp.stack([gq_large[0], gk_large, gv_large], 1).reshape(
        half_len, 3 * width_dim
    )
    grad_qkv_low = jnp.concatenate([grad_qkv_small, grad_qkv_large]).astype(jnp.bfloat16)
    grad_qkv = general_rows(normed_one, grad_qkv_low)
    grad_bias_query = jnp.sum(grad_qkv_low[:, :width_dim], 0, dtype=jnp.float32)
    grad_bias_value = jnp.sum(grad_qkv_low[:, 2 * width_dim :], 0, dtype=jnp.float32)
    grad_normed_one = general_cols(grad_qkv_low, back_qkv)
    grad_in_norm, grad_gain_one, grad_shift_one = norm_one_back(grad_normed_one)
    grad_input = (grad_middle + grad_in_norm).astype(jnp.bfloat16)
    small_grad = grad_input[:small_rows].reshape(small_tokens.shape)
    large_grad = grad_input[small_rows:].reshape(large_tokens.shape)
    grad_norm_all = jnp.stack([grad_gain_one, grad_shift_one, grad_gain_two, grad_shift_two])
    grad_bias_all = jnp.stack([grad_bias_query, grad_bias_value, grad_bias_out, grad_bias_down])
    shard_qkv, shard_out, shard_up, shard_down, shard_norm, shard_bias, shard_up_bias = (
        lax.psum_scatter(grad_qkv, ("dp", "seq"), scatter_dimension=0, tiled=True),
        lax.psum_scatter(grad_out, ("dp", "seq"), scatter_dimension=0, tiled=True),
        lax.psum_scatter(grad_up, ("dp", "seq"), scatter_dimension=0, tiled=True),
        lax.psum_scatter(grad_down, ("dp", "seq"), scatter_dimension=0, tiled=True),
        lax.psum_scatter(grad_norm_all, ("dp", "seq"), scatter_dimension=1, tiled=True),
        lax.psum_scatter(grad_bias_all, ("dp", "seq"), scatter_dimension=1, tiled=True),
        lax.psum_scatter(grad_up_bias, ("dp", "seq"), scatter_dimension=0, tiled=True),
    )
    return (
        small_out,
        large_out,
        small_grad,
        large_grad,
        shard_qkv,
        shard_out,
        shard_up,
        shard_down,
        shard_norm,
        shard_bias,
        shard_up_bias,
    )


def solution(mesh):
    in_specs = (
        P(("dp", "seq"), None, None),
        P("dp", "seq", None),
        P(("dp", "seq")),
        P("dp"),
        P(("dp", "seq"), None, None),
        P("dp", "seq", None),
        P(("dp", "seq"), None),
        P(("dp", "seq"), None),
        P(("dp", "seq"), None),
        P(("dp", "seq"), None),
        P(None, ("dp", "seq")),
        P(None, ("dp", "seq")),
        P(("dp", "seq")),
    )
    out_specs = (
        P(("dp", "seq"), None, None),
        P("dp", "seq", None),
        P(("dp", "seq"), None, None),
        P("dp", "seq", None),
        P(("dp", "seq"), None),
        P(("dp", "seq"), None),
        P(("dp", "seq"), None),
        P(("dp", "seq"), None),
        P(None, ("dp", "seq")),
        P(None, ("dp", "seq")),
        P(("dp", "seq")),
    )
    body = shards if (mesh.shape["dp"], mesh.shape["seq"]) == (16, 2) else shards_general
    return jax.shard_map(body, mesh=mesh, in_specs=in_specs, out_specs=out_specs, check_vma=False)
```

```python
import functools

import jax
import jax.numpy as jnp
from jax import lax
from jax.experimental import pallas as pl
from jax.experimental.pallas import tpu as pltpu
from jax.sharding import PartitionSpec as P

HEAD_DIM = 64
MESH = pl.DeviceIdType.MESH
BF = jnp.bfloat16
F32 = jnp.float32


def dot(a, b):
    return lax.dot_general(a, b, (((1,), (0,)), ((), ())), preferred_element_type=F32)


def dot_rows(a, b):
    return lax.dot_general(a, b, (((0,), (0,)), ((), ())), preferred_element_type=F32)


def dot_cols(a, b):
    return lax.dot_general(a, b, (((1,), (1,)), ((), ())), preferred_element_type=F32)


def device(x, y, z, c):
    return ((z * 2 + y) * 2 + c, x)


def rcopy(src, dst, send, recv, dev):
    return pltpu.make_async_remote_copy(
        src_ref=src, dst_ref=dst, send_sem=send, recv_sem=recv, device_id=dev, device_id_type=MESH
    )


def shard_at(j):
    return j // 4, (j // 2) % 2, j % 2


def stack_halves(g):
    n = g.shape[1] // 2
    return jnp.concatenate([g[:, :n], g[:, n:]], axis=0)


def rows_of(i, size, base=0):
    return pl.ds(pl.multiple_of(base + i * size, 16), size)


def lanes_of(i, size, base=0):
    return pl.ds(pl.multiple_of(base + i * size, 128), size)


def normalize(v):
    centred = v - jnp.mean(v, -1, keepdims=True)
    scale = lax.rsqrt(jnp.mean(centred * centred, -1, keepdims=True) + 1e-06)
    return centred * scale, scale


def norm_back(v, gain, grad):
    unit, scale = normalize(v)
    lifted = grad * gain
    inner = jnp.mean(lifted * unit, -1, keepdims=True)
    return scale * (lifted - jnp.mean(lifted, -1, keepdims=True) - unit * inner), unit


def gelu_pair(h):
    p = 0.3275911 * 0.7071067811865476
    t = 1.0 / (1.0 + p * abs(h))
    e = jnp.exp(-0.5 * h * h)
    poly = ((((1.061405429 * t - 1.453152027) * t + 1.421413741) * t - 0.284496736) * t + 0.254829592) * t
    q = 0.5 * poly * e
    phi = jnp.where(h >= 0, 1.0 - q, q)
    return h * phi, phi + h * e * 0.3989422804014327


def total(v):
    return jnp.sum(v.astype(F32), 0, keepdims=True)


def heads_forward(Q, KV, MIX, LSE, bias, q0, nq, k0, nk, first, count, unroll=1):
    D = Q.shape[1]
    left = lax.broadcasted_iota(jnp.int32, (nq, 128), 1) < HEAD_DIM

    def pair(hp, _):
        q = Q[q0 : q0 + nq, lanes_of(hp, 128)] * jnp.asarray(HEAD_DIM**-0.5, BF)
        k = KV[k0 : k0 + nk, lanes_of(hp, 128)]
        v = KV[k0 : k0 + nk, lanes_of(hp, 128, D)]
        zero = jnp.zeros_like(q)
        outs = []
        for head in range(2):
            qm = jnp.where(left, q, zero) if head == 0 else jnp.where(left, zero, q)
            s = dot_cols(k, qm) + bias
            top = jnp.max(s, 0, keepdims=True)
            e = jnp.exp(s - top)
            tot = jnp.sum(e, 0, keepdims=True)
            outs.append(dot_rows(v, e.astype(BF)) * (1.0 / tot))
            LSE[pl.ds(2 * hp + head, 1), 0:nq] = top + jnp.log(tot)
        both = jnp.concatenate([outs[0][:HEAD_DIM], outs[1][HEAD_DIM:]], axis=0)
        MIX[q0 : q0 + nq, lanes_of(hp, 128)] = jnp.transpose(both).astype(BF)
        return 0

    lax.fori_loop(0, count, lambda i, _: pair(first + i, _), 0, unroll=unroll)


def heads_backward(Q, KV, MIX, DMIX, LSE, bias, q0, nq, k0, nk, first, count, unroll=1):
    D = Q.shape[1]
    left = lax.broadcasted_iota(jnp.int32, (nq, 128), 1) < HEAD_DIM
    leftk = lax.broadcasted_iota(jnp.int32, (nk, 128), 1) < HEAD_DIM

    def pair(hp, _):
        q = Q[q0 : q0 + nq, lanes_of(hp, 128)] * jnp.asarray(HEAD_DIM**-0.5, BF)
        dm = DMIX[q0 : q0 + nq, lanes_of(hp, 128)]
        k = KV[k0 : k0 + nk, lanes_of(hp, 128)]
        v = KV[k0 : k0 + nk, lanes_of(hp, 128, D)]
        zero = jnp.zeros_like(q)
        weighted = jnp.transpose(dm.astype(F32) * MIX[q0 : q0 + nq, lanes_of(hp, 128)].astype(F32))
        dqs, dks, dvs = [], [], []
        for head in range(2):
            mask = lambda u: jnp.where(left, u, zero) if head == 0 else jnp.where(left, zero, u)
            delta = jnp.sum(weighted[head * HEAD_DIM : (head + 1) * HEAD_DIM], 0, keepdims=True)
            s = dot_cols(k, mask(q)) + bias
            pr = jnp.exp(s - LSE[pl.ds(2 * hp + head, 1), 0:nq])
            dvs.append(dot(pr.astype(BF), dm))
            ds = (pr * (dot_cols(v, mask(dm)) - delta)).astype(BF)
            dks.append(dot(ds, q))
            dqs.append(dot_rows(k, ds))
        both = jnp.concatenate([dqs[0][:HEAD_DIM], dqs[1][HEAD_DIM:]], axis=0) * HEAD_DIM**-0.5
        Q[q0 : q0 + nq, lanes_of(hp, 128)] = jnp.transpose(both).astype(BF)
        KV[k0 : k0 + nk, lanes_of(hp, 128)] = jnp.where(leftk, dks[0], dks[1]).astype(BF)
        KV[k0 : k0 + nk, lanes_of(hp, 128, D)] = jnp.where(leftk, dvs[0], dvs[1]).astype(BF)
        return 0

    lax.fori_loop(0, count, lambda i, _: pair(first + i, _), 0, unroll=unroll)


def store_block(g, SP, w, h):
    for j in range(16):
        z, y, c = shard_at(j)
        for x in range(2):
            r = 48 * j + 24 * x
            SP[w, h, x, y, z, c] = stack_halves(g[r : r + 24]).astype(BF)


def store_down(g, SP, f):
    n = SP.shape[-1]
    for j in range(4):
        for x in range(2):
            for half in range(2):
                r = (2 * j + x) * 96 + 48 * half
                for h in range(2):
                    SP[2 + half, h, x, j // 2, f, j % 2] = g[r : r + 48, h * n : h * n + n].astype(BF)


def layer_kernel(
    xs, xl, cs, cl, count_s, count_l, wqkv, wout, wup, wdown, norm, bias, upbias,
    OUT, DX, gqkv, gout, gup, gdown, SGO,
    X, DY, H1, Q, KV, MIX, MID, H2, ACC, DH2, ACT, DHB, DH1P, LP, LSES, LSEL,
    WQKV, WOUT, WUP, WDOWN, SP, OWN, LC, T, LF, sp, sm, sml, SG, SGL,
    ss, rs, tsem, psem, sms, smr, gs, gr, s2, r2, credit, room,
):
    d = lax.axis_index("dp")
    x, y, z, c = lax.axis_index("seq"), (d // 2) % 2, d // 4, d % 2
    zs = [z + 1 - 2 * (z % 2), 3 - z, (z + 2) % 4]
    sib, xn, yn = device(x, y, z, 1 - c), device(1 - x, y, z, c), device(x, 1 - y, z, c)
    zn = [device(x, y, k, c) for k in zs]
    bar = pltpu.get_barrier_semaphore()
    for p in [sib, xn, yn] + zn:
        pl.semaphore_signal(bar, inc=1, device_id=p, device_id_type=MESH)

    D = xs.shape[1]
    n = D // 2
    ns, nl = xs.shape[0], xl.shape[0]
    r1 = -(-ns // 16) * 16
    rl = -(-nl // 16) * 16
    R = r1 + rl
    RK = R + rl
    RB = R // 2
    zero = functools.partial(jnp.zeros, dtype=BF)
    head = ns - ns % 16

    blocks = [wqkv[:, k * D : (k + 1) * D] for k in range(3)] + [wout[...]]
    blocks = [stack_halves(g) for g in blocks]
    blocks += [wdown[48 * (b // 2) : 48 * (b // 2) + 48, (b % 2) * n : (b % 2) * n + n] for b in range(4)]
    blocks += [stack_halves(wup[:, k * D : (k + 1) * D]) for k in range(4)]
    for b, g in enumerate(blocks):
        OWN[b // 2, b % 2] = g.astype(BF)
    for w in range(6):
        SP[w, c, x, y, z, c] = OWN[w, c]
    pl.semaphore_wait(bar, 6)
    swaps = [rcopy(OWN.at[w, 1 - c], SP.at[w, 1 - c, x, y, z, c], ss.at[w, 0], rs.at[w, 0], sib) for w in range(6)]
    for cp in swaps:
        cp.start()

    X[head:r1, :] = zero((r1 - head, D))
    X[R - 16 : R, :] = zero((16, D))
    X[0:ns, :] = xs[...]
    X[r1 : r1 + nl, :] = xl[...]

    tcp = rcopy(X.at[r1:R], X.at[R:RK], tsem.at[0], tsem.at[1], xn)

    me = d * 2 + x
    k, m = norm.shape[1], upbias.shape[1]

    def placed(v, start):
        wide = jnp.concatenate([v, jnp.zeros((v.shape[0], D - v.shape[1]), F32)], axis=1)
        return pltpu.roll(wide, start, 1)

    row = lax.broadcasted_iota(jnp.int32, (8, D), 0)
    both = jnp.concatenate([norm[...], bias[...]], axis=0).astype(BF).astype(F32)
    top = placed(both, me * k)
    ub = placed(jnp.broadcast_to(upbias[...].astype(BF).astype(F32), (8, m)), lax.rem(me * m, D))
    low = jnp.where(row == (me * m) // D, ub, 0.0)
    sm[...] = jnp.concatenate([top, low], axis=0).astype(BF)

    def join(buf, land, send, recv, ks, devs):
        cps = [rcopy(buf, land.at[i], send.at[i], recv.at[i], dev) for i, dev in zip(ks, devs)]

        def start():
            for cp in cps:
                cp.start()

        def finish():
            for cp in cps:
                cp.wait()
            tot = buf[...].astype(F32)
            for i in ks:
                tot = tot + land[i].astype(F32)
            buf[...] = tot.astype(buf.dtype)

        return start, finish

    def joins(buf, land, send, recv):
        return [
            join(buf, land, send, recv, *a) for a in (([0], [sib]), ([1], [xn]), ([2], [yn]), ([3, 4, 5], zn))
        ]

    smalls = joins(sm, sml, sms, smr)

    pieces = [z] + zs

    def by_core(run):
        for core in range(2):
            pl.when(c == core)(lambda core=core: run(core))

    swapped_gather, swapped_scatter = (3,), (5, 3, 0)

    def roles(swapped):
        return (y, x, yn, xn) if swapped else (x, y, xn, yn)

    def spot(swapped, u, v, *rest):
        return ((v, u) if swapped else (u, v)) + rest

    def mail(w, sem, dev, out, back):
        sw = w in swapped_gather
        sent, got = SP.at[(w, c) + spot(sw, *out)], SP.at[(w, c) + spot(sw, *back)]
        return (
            rcopy(sent, sent, ss.at[w, sem], rs.at[w, sem], dev),
            rcopy(got, got, ss.at[w, sem], rs.at[w, sem], dev),
        )

    def mails(w, core):
        u, v, un, vn = roles(w in swapped_gather)
        if core == 0:
            one = [mail(w, 1 + i, zn[i], (u, v, z), (u, v, zs[i])) for i in range(3)]
            two = [mail(w, 4 + k, vn, (u, v, p), (u, 1 - v, p)) for k, p in enumerate(pieces)]
            three = [mail(w, 8 + k, un, (u, v, p), (1 - u, v, p)) for k, p in enumerate(pieces)]
            three += [mail(w, 12 + k, un, (u, 1 - v, p), (1 - u, 1 - v, p)) for k, p in enumerate(pieces)]
        else:
            one = [mail(w, 1, un, (u, v, z), (1 - u, v, z))]
            two = [mail(w, 2 + i, zn[i], (u, v, z), (u, v, zs[i])) for i in range(3)]
            two += [mail(w, 5 + i, zn[i], (1 - u, v, z), (1 - u, v, zs[i])) for i in range(3)]
            three = [mail(w, 8 + k, vn, (u, v, p), (u, 1 - v, p)) for k, p in enumerate(pieces)]
            three += [mail(w, 12 + k, vn, (1 - u, v, p), (1 - u, 1 - v, p)) for k, p in enumerate(pieces)]
        return one, two, three

    def a1(w):
        swaps[w].wait()

        def run(core):
            one, two, three = mails(w, core)
            first = one + (two[0:1] + three[0:1] if core == 0 else two[0:3] + three[0:1])
            for sent, _ in first:
                sent.start()

        by_core(run)

    def a2(w):
        def run(core):
            one, two, three = mails(w, core)
            for i, (_, got) in enumerate(one):
                got.wait_recv()
                onward = [two[1 + i], three[1 + i]] if core == 0 else two[3:6] + three[4:5]
                for sent, _ in onward:
                    sent.start()

        by_core(run)

    def a3(w):
        def run(core):
            _, two, three = mails(w, core)
            if core == 0:
                for k in range(4):
                    two[k][1].wait_recv()
                    three[4 + k][0].start()
            else:
                for part in range(2):
                    for i in range(3):
                        two[3 * part + i][1].wait_recv()
                        three[4 * part + 1 + i][0].start()

        by_core(run)

    def a4(w):
        def run(core):
            one, two, three = mails(w, core)
            for _, got in three:
                got.wait_recv()
            for sent, _ in one + two + three:
                sent.wait_send()

        by_core(run)
        src = SP.at[w, c]
        rcopy(src, src, ss.at[w, 16], rs.at[w, 16], sib).start()

    def assemble(w, h, dst, col):
        def step(j, _):
            pz, py, pc = shard_at(j)
            a = SP[w, h, 0, py, pz, pc].astype(F32)
            e = SP[w, h, 1, py, pz, pc].astype(F32)
            dst[rows_of(j, 48), col : col + n] = jnp.concatenate([a[:24], e[:24]], axis=0).astype(BF)
            dst[rows_of(j, 48), col + n : col + D] = jnp.concatenate([a[24:], e[24:]], axis=0).astype(BF)
            return 0

        lax.fori_loop(0, 16, step, 0, unroll=4)

    def assemble_down(w, h):
        def step(j, _):
            pz, py, pc = shard_at(j)
            for px in range(2):
                rows = pl.ds(pl.multiple_of(96 * (2 * j + px) + 48 * (w - 2), 16), 48)
                WDOWN[rows, n * h : n * h + n] = SP[w, h, px, py, pz, pc]
            return 0

        lax.fori_loop(0, 16, step, 0, unroll=4)

    def a5(w):
        src, dst = SP.at[w, c], SP.at[w, 1 - c]
        rcopy(src, src, ss.at[w, 16], rs.at[w, 16], sib).wait_send()
        rcopy(dst, dst, ss.at[w, 16], rs.at[w, 16], sib).wait_recv()
        for h in range(2):
            b = 2 * w + h
            if b < 3:
                assemble(w, h, WQKV, b * D)
            elif b == 3:
                assemble(w, h, WOUT, 0)
            elif b < 8:
                assemble_down(w, h)
            else:
                assemble(w, h, WUP, (b - 8) * D)

    def credits(w):
        for i, dev in enumerate([xn, yn] + zn):
            pl.semaphore_signal(room.at[w, i], inc=1, device_id=dev, device_id_type=MESH)

    order = [4, 5, 2, 3, 1, 0]
    backs = [zs[2], zs[1], zs[0], z]

    def add(w, dst, src, count):
        def step(i, _):
            at = (w, c) + dst(i)
            SP[at] = (SP[at].astype(F32) + src(i).astype(F32)).astype(BF)
            return 0

        lax.fori_loop(0, count, step, 0, unroll=min(count, 4))

    def first_copy(i, k):
        w = order[i]
        return rcopy(SP.at[w, 1 - c, :, :, k], LC.at[i % 2, :, :, k], s2.at[w, k], r2.at[w, k], sib)

    def go(i):
        if i >= 2:
            pl.semaphore_wait(credit, 1)
        for k in range(4):
            first_copy(i, k).start()

    def held(w, u, v, *rest):
        return SP.at[(w, c) + spot(w in swapped_scatter, u, v, *rest)]

    def second_copy(w, k, core):
        pz = backs[k]
        u, v, un, vn = roles(w in swapped_scatter)
        every = slice(None)
        dev = (un, vn)[core]
        src = held(w, 1 - u, every, pz) if core == 0 else held(w, every, 1 - v, pz)
        return rcopy(src, SP.at[w, 1 - c, 0, :, k], s2.at[w, 4 + k], r2.at[w, 4 + k], dev)

    def third_copy(w, k, core):
        pz = backs[k]
        u, v, un, vn = roles(w in swapped_scatter)
        sems = (s2.at[w, 8 + k], r2.at[w, 8 + k])
        if core == 0:
            return rcopy(held(w, u, 1 - v, pz), SP.at[w, 1 - c, 1, 0, k], *sems, vn)
        return rcopy(held(w, slice(None), v, pz), SP.at[w, 1 - c, 1, :, k], *sems, zn[2 - k])

    def fourth_copy(w, k, core):
        u, v, un, vn = roles(w in swapped_scatter)
        sems = (s2.at[w, 12 + k], r2.at[w, 12 + k])
        if core == 0:
            return rcopy(SP.at[w, c, x, y, backs[k]], SP.at[w, 1 - c, 1, 1, k], *sems, zn[2 - k])
        return rcopy(held(w, 1 - u, v, z), SP.at[w, 1 - c, 1, 0, 3], *sems, un)

    def last_copy(w):
        return rcopy(T.at[w, 1 - c], LF.at[w], s2.at[w, 15], r2.at[w, 15], sib)

    def deliver(w):
        mine, other = T[w, c], LF[w]
        for h in range(2):
            g = jnp.where(c == h, mine, other)
            b = 2 * w + h
            if 4 <= b < 8:
                half = (b - 4) // 2
                gdown[48 * half : 48 * half + 48, n * h : n * h + n] = g
                continue
            wide = jnp.concatenate([g[0:24], g[24:48]], axis=1)
            if b >= 8:
                gup[:, (b - 8) * D : (b - 7) * D] = wide
            elif b == 2:
                gout[...] = wide
            else:
                g0 = (3, 2, None, 1)[b] - 1
                third = D // 3
                for part in range(3):
                    lo = part * D + g0 * third
                    gqkv[:, lo : lo + third] = wide[:, part * third : (part + 1) * third]

    def back(i, stage):
        w = order[i]
        sw = w in swapped_scatter
        u, v, _, _ = roles(sw)
        side = (1, 0) if sw else (0, 1)
        if stage == 0:
            for k in range(4):
                first_copy(i, k).wait()
                idx = lambda j: (j // 4, (j // 2) % 2, k, j % 2)
                add(w, idx, lambda j: LC[(i % 2,) + idx(j)], 8)
            if i < 4:
                pl.semaphore_signal(credit, inc=1, device_id=sib, device_id_type=MESH)
            credits(w)
        elif stage == 1:

            def run(core):
                pl.semaphore_wait(room.at[w, side[core]], 1)
                for k in range(4):
                    second_copy(w, k, core).start()

            by_core(run)
        elif stage == 2:

            def run(core):
                if core == 0:
                    pl.semaphore_wait(room.at[w, side[1]], 1)
                for k in range(4):
                    second_copy(w, k, core).wait()
                    place = (
                        (lambda j: spot(sw, u, j // 2, backs[k], j % 2)),
                        (lambda j: spot(sw, j // 2, v, backs[k], j % 2)),
                    )[core]
                    add(w, place, lambda j: SP[w, 1 - c, 0, j // 2, k, j % 2], 4)
                    if core == 1 and k < 3:
                        pl.semaphore_wait(room.at[w, 2 + 2 - k], 1)
                    if core == 0 or k < 3:
                        third_copy(w, k, core).start()

            by_core(run)
        elif stage == 3:

            def run(core):
                if core == 0:
                    for k in range(4):
                        third_copy(w, k, core).wait()
                        add(w, lambda j: (x, y, backs[k], j), lambda j: SP[w, 1 - c, 1, 0, k, j], 2)
                        if k < 3:
                            pl.semaphore_wait(room.at[w, 2 + 2 - k], 1)
                            fourth_copy(w, k, core).start()
                    return
                for k in range(3):
                    third_copy(w, k, core).wait()
                three = lambda j: sum(SP[w, 1 - c, 1, j // 2, k, j % 2].astype(F32) for k in range(3))
                add(w, lambda j: spot(sw, j // 2, v, z, j % 2), three, 4)
                pl.semaphore_wait(room.at[w, side[0]], 1)
                fourth_copy(w, 0, core).start()

            by_core(run)
        elif stage == 4:

            def run(core):
                count = 3 if core == 0 else 1
                for k in range(count):
                    fourth_copy(w, k, core).wait()
                for q in range(2):
                    tot = SP[w, c, x, y, z, q].astype(F32)
                    for k in range(count):
                        at = (1, 1, k, q) if core == 0 else (1, 0, 3, q)
                        tot = tot + SP[(w, 1 - c) + at].astype(F32)
                    T[w, q] = tot

            by_core(run)
            last_copy(w).start()
        else:
            last_copy(w).wait()
            deliver(w)

    def norm_one(base, count):
        def step(i, _):
            rows = rows_of(i, size, base)
            unit, _ = normalize(X[rows, :].astype(F32))
            H1[rows, :] = (unit * sp[0:1, :] + sp[1:2, :]).astype(BF)
            return 0

        size = RB if count % RB == 0 else count
        lax.fori_loop(0, count // size, step, 0)

    small_count, large_count = count_s[0], count_l[0]
    kj = lax.broadcasted_iota(jnp.int32, (r1, 1), 0)
    bias_small = jnp.where(kj < small_count, 0.0, -1e30)
    kj = lax.broadcasted_iota(jnp.int32, (2 * rl, 1), 0)
    mine = kj < rl
    inside = jnp.where(mine, kj, kj - rl)
    where = inside + jnp.where(mine, x, 1 - x) * nl
    bias_large = jnp.where((inside < nl) & (where < large_count), 0.0, -1e30)
    small_part = (bias_small, 0, r1, 0, r1)
    large_part = (bias_large, r1, rl, r1, 2 * rl)

    def take_cotangents():
        DY[head:r1, :] = zero((r1 - head, D))
        DY[R - 16 : R, :] = zero((16, D))
        DY[0:ns, :] = cs[...]
        DY[r1 : r1 + nl, :] = cl[...]

    def know_smalls():
        smalls[3][1]()
        sp[...] = sm[...].astype(F32)

    def query():
        Q[...] = (dot(H1[0:R, :], WQKV[:, 0:D]) + sp[4:5, :]).astype(BF)

    def key():
        KV[:, 0:D] = dot(H1[...], WQKV[:, D : 2 * D]).astype(BF)

    def value():
        KV[:, D:] = (dot(H1[...], WQKV[:, 2 * D :]) + sp[5:6, :]).astype(BF)

    def attend_small():
        heads_forward(Q, KV, MIX, LSES, *small_part, 0, 6, unroll=2)

    def attend_large(hp):
        heads_forward(Q, KV, MIX, LSEL, *large_part, hp, 1)

    def project_out():
        MID[...] = dot(MIX[...], WOUT[...])

    def second_norm():
        def step(i, _):
            rows = rows_of(i, RB)
            middle = X[rows, :].astype(F32) + MID[rows, :] + sp[6:7, :]
            MID[rows, :] = middle
            unit, _ = normalize(middle)
            H2[rows, :] = (unit * sp[2:3, :] + sp[3:4, :]).astype(BF)
            ACC[rows, :] = middle + sp[7:8, :]
            return 0

        lax.fori_loop(0, R // RB, step, 0)

    def hidden_units(f):
        hidden = dot(H2[...], WUP[:, lanes_of(f, D)]) + sp[pl.ds(8 + f, 1), :]
        dact = dot_cols(DY[...], WDOWN[rows_of(f, D), :])
        act, slope = gelu_pair(hidden)
        ACT[f] = act.astype(BF)
        dh = (dact * slope).astype(BF)
        DHB[...] = dh
        SG[pl.ds(8 + f, 1), :] = total(dh)

    def grad_up(f):
        store_block(dot_rows(H2[...], DHB[...]), SP, 4 + f // 2, f % 2)

    def grad_down(f):
        store_down(dot_rows(ACT[f], DY[...]), SP, f)

    def forward_down():
        for f in range(4):
            ACC[...] += dot(ACT[f], WDOWN[f * D : (f + 1) * D, :])

    def backward_up(f):
        DH2[...] += dot_cols(DHB[...], WUP[:, lanes_of(f, D)])

    def give_out():
        OUT[...] = ACC[...].astype(BF)

    z1 = jnp.zeros((1, D), F32)

    def second_norm_back():
        def step(i, sums):
            rows = rows_of(i, RB)
            grad = DH2[rows, :]
            dy = DY[rows, :].astype(F32)
            dv, unit = norm_back(MID[rows, :], sp[2:3, :], grad)
            dmid = dy + dv
            MID[rows, :] = dmid
            low = dmid.astype(BF)
            H2[rows, :] = low
            return sums[0] + total(grad * unit), sums[1] + total(grad), sums[2] + total(low), sums[3] + total(dy)

        sums = lax.fori_loop(0, R // RB, step, (z1, z1, z1, z1))
        for i, at in enumerate((2, 3, 6, 7)):
            SG[at : at + 1, :] = sums[i]

    def grad_mixed():
        DHB[...] = dot_cols(H2[...], WOUT[...]).astype(BF)

    def grad_out():
        store_block(dot_rows(MIX[...], H2[...]), SP, 1, 0)

    third = D // 3

    def back_small(g):
        heads_backward(Q, KV, MIX, DHB, LSES, *small_part, 2 * g, 2, unroll=2)

    def back_large(hp):
        heads_backward(Q, KV, MIX, DHB, LSEL, *large_part, hp, 1)

    def grad_heads(g):
        lo, lov = lanes_of(g, third), lanes_of(g, third, D)
        grads = [dot_rows(H1[0:R, :], Q[:, lo]), dot_rows(H1[...], KV[:, lo]), dot_rows(H1[...], KV[:, lov])]
        store_block(jnp.concatenate(grads, axis=1), SP, (2 - g) // 2, 1 - g // 2)

    pcp = rcopy(DH1P, LP, psem.at[0], psem.at[1], xn)

    def grad_partner():
        g = dot_cols(KV[R:RK, 0:D], WQKV[:, D : 2 * D]) + dot_cols(KV[R:RK, D:], WQKV[:, 2 * D :])
        DH1P[...] = g.astype(BF)

    def grad_normed():
        g = dot_cols(Q[...], WQKV[:, 0:D]) + dot_cols(KV[0:R, 0:D], WQKV[:, D : 2 * D])
        DH2[...] = g + dot_cols(KV[0:R, D:], WQKV[:, 2 * D :])

    def first_norm_back(base, count, partner):
        rows = slice(base, base + count)
        grad = DH2[rows, :]
        if partner:
            grad = grad + LP[...].astype(F32)
        dv, _ = norm_back(X[rows, :].astype(F32), sp[0:1, :], grad)
        DX[rows, :] = (MID[rows, :] + dv).astype(BF)

    ends = joins(SG, SGL, gs, gr)

    def first_norm_sums():
        def step(i, sums):
            unit, _ = normalize(X[rows_of(i, RB), :].astype(F32))
            grad = DH2[rows_of(i, RB), :]
            return sums[0] + total(grad * unit), sums[1] + total(grad)

        sums = lax.fori_loop(0, R // RB, step, (z1, z1))
        unit, _ = normalize(X[R:RK, :].astype(F32))
        grad = DH1P[...].astype(F32)
        SG[0:1, :] = sums[0] + total(grad * unit)
        SG[1:2, :] = sums[1] + total(grad)
        SG[4:5, :] = total(Q[...])
        SG[5:6, :] = total(KV[:, D:])

    def clear():
        SG[...] = jnp.zeros(SG.shape, F32)
        DH2[...] = jnp.zeros(DH2.shape, F32)

    def repeat(count, body, after):
        def step(i, _):
            for k, do in enumerate(body):
                do(i)
                for j in range(count):
                    if after[j][k]:
                        pl.when(i == j)(after[j][k])
            return 0

        lax.fori_loop(0, count, step, 0)

    clear()
    a1(0)
    smalls[0][0]()
    smalls[0][1]()
    smalls[1][0]()
    a1(1)
    smalls[1][1]()
    a2(0)
    tcp.start()
    smalls[2][0]()
    a3(0)
    a2(1)
    smalls[2][1]()
    a1(2)
    take_cotangents()
    smalls[3][0]()
    a4(0)
    a3(1)
    a2(2)
    know_smalls()
    norm_one(0, R)
    a1(3)
    a4(1)
    a5(0)
    a2(3)
    tcp.wait()
    a1(4)
    norm_one(R, rl)
    query()
    a3(2)
    key()
    a5(1)
    value()
    a3(3)
    a2(4)

    def then_0():
        a1(5)

    def then_1():
        a4(2)
        a3(4)
        a4(3)

    repeat(6, (attend_large,), ((None,), (None,), (then_0,), (then_1,), (None,), (None,),))
    attend_small()
    a2(5)
    project_out()
    a4(4)
    a5(2)
    second_norm()
    a5(3)
    a3(5)
    a5(4)

    def then_2():
        a4(5)

    def then_3():
        a5(5)

    def then_4():
        go(0)

    def then_5():
        back(0, 0)

    def then_6():
        go(1)

    def then_7():
        back(0, 1)

    repeat(4, (hidden_units, grad_up, grad_down, backward_up,), ((None, None, None, then_2), (None, then_3, None, then_4), (None, then_5, None, None), (None, then_6, then_7, None),))
    go(2)
    second_norm_back()
    back(1, 0)
    grad_mixed()
    grad_out()
    back(1, 1)

    def then_8():
        go(3)
        back(2, 0)

    def then_9():
        back(3, 0)
        back(2, 1)
        back(0, 2)

    def then_10():
        go(4)
        back(1, 2)

    def then_11():
        back(3, 1)

    def then_12():
        back(0, 3)
        back(4, 0)

    def then_13():
        back(2, 2)
        back(4, 1)

    def then_14():
        back(3, 2)

    repeat(3, (back_small, lambda g: back_large(2 * g), lambda g: back_large(2 * g + 1), grad_heads,), ((then_8, then_9, None, then_10), (None, then_11, then_12, then_13), (then_14, None, None, None),))
    go(5)
    back(1, 3)
    back(2, 3)
    grad_partner()
    pcp.start()
    back(0, 4)
    back(4, 2)
    back(5, 0)
    back(5, 1)
    grad_normed()
    back(0, 5)
    back(3, 3)
    back(1, 4)
    first_norm_sums()
    ends[0][0]()
    back(1, 5)
    ends[0][1]()
    back(2, 4)
    ends[1][0]()
    first_norm_back(0, r1, False)
    back(4, 3)
    back(5, 2)
    back(2, 5)
    back(3, 4)
    ends[1][1]()
    ends[2][0]()
    forward_down()
    back(4, 4)
    ends[2][1]()
    back(3, 5)
    back(5, 3)
    back(4, 5)
    ends[3][0]()
    back(5, 4)
    pcp.wait()
    give_out()
    back(5, 5)
    first_norm_back(r1, rl, True)
    ends[3][1]()
    SGO[...] = SG[...]


def deliver_kernel(
    OUT, DX, gqkv, gout, gup, gdown, SG,
    outs, outl, dxs, dxl, oqkv, oout, oup, odown, onorm, obias, oub,
):
    ns, nl = outs.shape[0], outl.shape[0]
    r1 = -(-ns // 16) * 16
    outs[...] = OUT[0:ns, :]
    outl[...] = OUT[r1 : r1 + nl, :]
    dxs[...] = DX[0:ns, :]
    dxl[...] = DX[r1 : r1 + nl, :]
    oqkv[...] = gqkv[...]
    oout[...] = gout[...]
    oup[...] = gup[...]
    odown[...] = gdown[...]
    D = outs.shape[1]
    me = lax.axis_index("dp") * 2 + lax.axis_index("seq")
    k, m = onorm.shape[1], oub.shape[1]
    near = pltpu.roll(SG[0:8, :], lax.rem(D - me * k, D), 1)[:, 0:k]
    onorm[...] = near[0:4]
    obias[...] = near[4:8]
    row = lax.broadcasted_iota(jnp.int32, (8, D), 0)
    picked = total(jnp.where(row == (me * m) // D, SG[8:16, :], 0.0))
    near = pltpu.roll(jnp.broadcast_to(picked, (8, D)), lax.rem(D - lax.rem(me * m, D), D), 1)
    oub[...] = near[0:1, 0:m]


def vm():
    return pl.BlockSpec(memory_space=pltpu.VMEM)


def layer(xs, xl, cs, cl, count_s, count_l, wqkv, wout, wup, wdown, norm, bias, upbias):
    D = xs.shape[1]
    n = D // 2
    r1 = -(-xs.shape[0] // 16) * 16
    rl = -(-xl.shape[0] // 16) * 16
    R = r1 + rl
    RK = R + rl
    sds = jax.ShapeDtypeStruct
    smem = pl.BlockSpec(memory_space=pltpu.SMEM)
    dma, regular = pltpu.SemaphoreType.DMA, pltpu.SemaphoreType.REGULAR
    small = (16, D)
    return pl.pallas_call(
        layer_kernel,
        out_shape=(
            sds((R, D), BF), sds((R, D), BF),
            sds(wqkv.shape, F32), sds(wout.shape, F32), sds(wup.shape, F32), sds(wdown.shape, F32), sds(small, F32),
        ),
        in_specs=[vm()] * 4 + [smem] * 2 + [vm()] * 7,
        out_specs=(vm(),) * 7,
        scratch_shapes=[
            pltpu.VMEM((RK, D), BF),
            pltpu.VMEM((R, D), BF),
            pltpu.VMEM((RK, D), BF),
            pltpu.VMEM((R, D), BF),
            pltpu.VMEM((RK, 2 * D), BF),
            pltpu.VMEM((R, D), BF),
            pltpu.VMEM((R, D), F32),
            pltpu.VMEM((R, D), BF),
            pltpu.VMEM((R, D), F32),
            pltpu.VMEM((R, D), F32),
            pltpu.VMEM((4, R, D), BF),
            pltpu.VMEM((R, D), BF),
            pltpu.VMEM((rl, D), BF),
            pltpu.VMEM((rl, D), BF),
            pltpu.VMEM((16, r1), F32),
            pltpu.VMEM((16, rl), F32),
            pltpu.VMEM((D, 3 * D), BF),
            pltpu.VMEM((D, D), BF),
            pltpu.VMEM((D, 4 * D), BF),
            pltpu.VMEM((4 * D, D), BF),
            pltpu.VMEM((6, 2, 2, 2, 4, 2, 48, n), BF),
            pltpu.VMEM((6, 2, 48, n), BF),
            pltpu.VMEM((2, 2, 2, 4, 2, 48, n), BF),
            pltpu.VMEM((6, 2, 48, n), F32),
            pltpu.VMEM((6, 48, n), F32),
            pltpu.VMEM(small, F32),
            pltpu.VMEM(small, BF),
            pltpu.VMEM((6,) + small, BF),
            pltpu.VMEM(small, F32),
            pltpu.VMEM((6,) + small, F32),
            dma((6, 17)), dma((6, 17)), dma((2,)), dma((2,)), dma((6,)), dma((6,)), dma((6,)), dma((6,)),
            dma((6, 16)), dma((6, 16)), regular, regular((6, 5)),
        ],
        compiler_params=pltpu.CompilerParams(collective_id=1, has_side_effects=True, vmem_limit_bytes=63 << 20),
        name="layer",
    )(xs, xl, cs, cl, count_s, count_l, wqkv, wout, wup, wdown, norm, bias, upbias)


def shards(
    small_tokens, large_tokens, small_counts, large_counts, small_cot, large_cot,
    w_qkv, w_out, w_up, w_down, norm_params, proj_bias, up_bias,
):
    flat = lambda v: v.reshape(v.shape[1:])
    xs, xl, cs, cl = flat(small_tokens), flat(large_tokens), flat(small_cot), flat(large_cot)
    made = layer(
        xs, xl, cs, cl, small_counts, large_counts, w_qkv, w_out, w_up, w_down, norm_params, proj_bias, up_bias[None]
    )
    like = (xs, xl, xs, xl, w_qkv, w_out, w_up, w_down, norm_params, proj_bias, up_bias[None])
    outs, outl, dxs, dxl, gqkv, gout, gup, gdown, gnorm, gbias, gub = pl.pallas_call(
        deliver_kernel,
        out_shape=tuple(jax.ShapeDtypeStruct(v.shape, v.dtype) for v in like),
        in_specs=[vm()] * 7,
        out_specs=(vm(),) * 11,
        compiler_params=pltpu.CompilerParams(vmem_limit_bytes=62 << 20),
        name="deliver",
    )(*made)
    return outs[None], outl[None], dxs[None], dxl[None], gqkv, gout, gup, gdown, gnorm, gbias, gub[0]


def norm_rows(values, gain, shift):
    centre = jnp.mean(values, -1, keepdims=True)
    centered = values - centre
    spread = jnp.mean(centered * centered, -1, keepdims=True)
    return centered * lax.rsqrt(spread + 1e-06) * gain + shift


def gelu_exact(values):
    return jax.nn.gelu(values, approximate=False)


def general_rows(left, right):
    return lax.dot_general(
        left, right, (((0,), (0,)), ((), ())), preferred_element_type=jnp.float32
    )


def general_cols(left, right):
    return lax.dot_general(
        left, right, (((1,), (1,)), ((), ())), preferred_element_type=jnp.float32
    )


def attend(query, key_part, value, valid_keys, factor):
    raw_scores = jnp.einsum("bqhe,bkhe->bhqk", query, key_part, preferred_element_type=jnp.float32)
    scaled = jnp.where(valid_keys[:, None, None, :], raw_scores * factor, -1e30)
    row_top = jnp.max(scaled, -1, keepdims=True)
    expo_rows = jnp.exp(scaled - row_top)
    totals = jnp.sum(expo_rows, -1, keepdims=True)
    probs_full = expo_rows / totals
    mixed = jnp.einsum(
        "bhqk,bkhe->bqhe",
        probs_full.astype(jnp.bfloat16),
        value,
        preferred_element_type=jnp.float32,
    )
    return (mixed, row_top + jnp.log(totals))


def attend_back(query, key_part, value, valid_keys, log_total, grad_mixed, factor):
    raw_scores = jnp.einsum("bqhe,bkhe->bhqk", query, key_part, preferred_element_type=jnp.float32)
    scaled = jnp.where(valid_keys[:, None, None, :], raw_scores * factor, -1e30)
    probs_full = jnp.exp(scaled - log_total)
    grad_value = jnp.einsum(
        "bhqk,bqhe->bkhe",
        probs_full.astype(jnp.bfloat16),
        grad_mixed,
        preferred_element_type=jnp.float32,
    )
    grad_probs = jnp.einsum(
        "bqhe,bkhe->bhqk", grad_mixed, value, preferred_element_type=jnp.float32
    )
    row_delta = jnp.sum(probs_full * grad_probs, -1, keepdims=True)
    grad_raw = (probs_full * (grad_probs - row_delta) * factor).astype(jnp.bfloat16)
    grad_query = jnp.einsum(
        "bhqk,bkhe->bqhe", grad_raw, key_part, preferred_element_type=jnp.float32
    )
    grad_key = jnp.einsum("bhqk,bqhe->bkhe", grad_raw, query, preferred_element_type=jnp.float32)
    return (grad_query, grad_key, grad_value)


def shards_general(
    small_tokens,
    large_tokens,
    small_counts,
    large_counts,
    small_cot,
    large_cot,
    w_qkv,
    w_out,
    w_up,
    w_down,
    norm_params,
    proj_bias,
    up_bias,
):
    gathered = (
        lax.all_gather(w_qkv.astype(jnp.bfloat16), ("dp", "seq"), axis=0, tiled=True),
        lax.all_gather(w_out.astype(jnp.bfloat16), ("dp", "seq"), axis=0, tiled=True),
        lax.all_gather(w_up.astype(jnp.bfloat16), ("dp", "seq"), axis=0, tiled=True),
        lax.all_gather(w_down.astype(jnp.bfloat16), ("dp", "seq"), axis=0, tiled=True),
        lax.all_gather(norm_params.astype(jnp.bfloat16), ("dp", "seq"), axis=1, tiled=True),
        lax.all_gather(proj_bias.astype(jnp.bfloat16), ("dp", "seq"), axis=1, tiled=True),
        lax.all_gather(up_bias.astype(jnp.bfloat16), ("dp", "seq"), axis=0, tiled=True),
    )
    full_qkv, full_out, full_up, full_down, full_norm, full_bias, full_upbias = gathered
    norm_vals = full_norm.astype(jnp.float32)
    bias_vals = full_bias.astype(jnp.float32)
    upbias_vals = full_upbias.astype(jnp.float32)
    factor = HEAD_DIM ** (-0.5)
    small_images, small_len, width_dim = small_tokens.shape
    half_len = large_tokens.shape[1]
    small_rows = small_images * small_len
    head_count = width_dim // HEAD_DIM
    rows_in = jnp.concatenate(
        [small_tokens.reshape(small_rows, width_dim), large_tokens.reshape(half_len, width_dim)]
    ).astype(jnp.float32)
    normed_one, norm_one_back = jax.vjp(norm_rows, rows_in, norm_vals[0], norm_vals[1])
    normed_one = normed_one.astype(jnp.bfloat16)
    qkv_bias = jnp.concatenate([bias_vals[0], jnp.zeros((width_dim,), jnp.float32), bias_vals[1]])
    qkv_rows = (
        jnp.dot(normed_one, full_qkv, preferred_element_type=jnp.float32) + qkv_bias
    ).astype(jnp.bfloat16)
    qkv_heads = qkv_rows.reshape(-1, 3, head_count, HEAD_DIM)
    small_heads = qkv_heads[:small_rows].reshape(small_images, small_len, 3, head_count, HEAD_DIM)
    query_small = small_heads[:, :, 0]
    key_small = small_heads[:, :, 1]
    value_small = small_heads[:, :, 2]
    valid_small = jnp.arange(small_len, dtype=jnp.int32)[None, :] < small_counts[:, None]
    large_heads = qkv_heads[small_rows:]
    query_large = large_heads[:, 0][None]
    key_whole, value_whole = (
        lax.all_gather(large_heads[:, 1], "seq", axis=0, tiled=True),
        lax.all_gather(large_heads[:, 2], "seq", axis=0, tiled=True),
    )
    key_large = key_whole[None]
    value_large = value_whole[None]
    valid_large = jnp.arange(key_whole.shape[0], dtype=jnp.int32)[None, :] < large_counts[:, None]
    mixed_small, total_small = attend(query_small, key_small, value_small, valid_small, factor)
    mixed_large, total_large = attend(query_large, key_large, value_large, valid_large, factor)
    mixed = jnp.concatenate(
        [mixed_small.reshape(small_rows, width_dim), mixed_large.reshape(half_len, width_dim)]
    ).astype(jnp.bfloat16)
    middle = rows_in + jnp.dot(mixed, full_out, preferred_element_type=jnp.float32) + bias_vals[2]
    normed_two, norm_two_back = jax.vjp(norm_rows, middle, norm_vals[2], norm_vals[3])
    normed_two = normed_two.astype(jnp.bfloat16)
    up_proj = jnp.dot(normed_two, full_up, preferred_element_type=jnp.float32) + upbias_vals
    act_full, gelu_back = jax.vjp(gelu_exact, up_proj)
    act_low = act_full.astype(jnp.bfloat16)
    result = middle + jnp.dot(act_low, full_down, preferred_element_type=jnp.float32) + bias_vals[3]
    result_low = result.astype(jnp.bfloat16)
    small_out = result_low[:small_rows].reshape(small_tokens.shape)
    large_out = result_low[small_rows:].reshape(large_tokens.shape)
    back_qkv, back_out, back_up, back_down = (full_qkv, full_out, full_up, full_down)
    grad_rows = jnp.concatenate(
        [small_cot.reshape(small_rows, width_dim), large_cot.reshape(half_len, width_dim)]
    )
    grad_rows_full = grad_rows.astype(jnp.float32)
    grad_down = general_rows(act_low, grad_rows)
    grad_bias_down = jnp.sum(grad_rows, 0, dtype=jnp.float32)
    grad_act = general_cols(grad_rows, back_down)
    (grad_hidden,) = gelu_back(grad_act)
    grad_hidden_low = grad_hidden.astype(jnp.bfloat16)
    grad_up = general_rows(normed_two, grad_hidden_low)
    grad_up_bias = jnp.sum(grad_hidden_low, 0, dtype=jnp.float32)
    grad_normed_two = general_cols(grad_hidden_low, back_up)
    grad_mid_norm, grad_gain_two, grad_shift_two = norm_two_back(grad_normed_two)
    grad_middle = grad_rows_full + grad_mid_norm
    grad_middle_low = grad_middle.astype(jnp.bfloat16)
    grad_out = general_rows(mixed, grad_middle_low)
    grad_bias_out = jnp.sum(grad_middle_low, 0, dtype=jnp.float32)
    grad_mixed = (
        general_cols(grad_middle_low, back_out).astype(jnp.bfloat16).reshape(-1, head_count, HEAD_DIM)
    )
    grad_mixed_small = grad_mixed[:small_rows].reshape(
        small_images, small_len, head_count, HEAD_DIM
    )
    grad_mixed_large = grad_mixed[small_rows:][None]
    gq_small, gk_small, gv_small = attend_back(
        query_small, key_small, value_small, valid_small, total_small, grad_mixed_small, factor
    )
    gq_large, gk_whole, gv_whole = attend_back(
        query_large, key_large, value_large, valid_large, total_large, grad_mixed_large, factor
    )
    gk_large, gv_large = (
        lax.psum_scatter(
            gk_whole[0].astype(jnp.bfloat16), "seq", scatter_dimension=0, tiled=True
        ).astype(jnp.float32),
        lax.psum_scatter(
            gv_whole[0].astype(jnp.bfloat16), "seq", scatter_dimension=0, tiled=True
        ).astype(jnp.float32),
    )
    grad_qkv_small = jnp.stack([gq_small, gk_small, gv_small], 2).reshape(small_rows, 3 * width_dim)
    grad_qkv_large = jnp.stack([gq_large[0], gk_large, gv_large], 1).reshape(
        half_len, 3 * width_dim
    )
    grad_qkv_low = jnp.concatenate([grad_qkv_small, grad_qkv_large]).astype(jnp.bfloat16)
    grad_qkv = general_rows(normed_one, grad_qkv_low)
    grad_bias_query = jnp.sum(grad_qkv_low[:, :width_dim], 0, dtype=jnp.float32)
    grad_bias_value = jnp.sum(grad_qkv_low[:, 2 * width_dim :], 0, dtype=jnp.float32)
    grad_normed_one = general_cols(grad_qkv_low, back_qkv)
    grad_in_norm, grad_gain_one, grad_shift_one = norm_one_back(grad_normed_one)
    grad_input = (grad_middle + grad_in_norm).astype(jnp.bfloat16)
    small_grad = grad_input[:small_rows].reshape(small_tokens.shape)
    large_grad = grad_input[small_rows:].reshape(large_tokens.shape)
    grad_norm_all = jnp.stack([grad_gain_one, grad_shift_one, grad_gain_two, grad_shift_two])
    grad_bias_all = jnp.stack([grad_bias_query, grad_bias_value, grad_bias_out, grad_bias_down])
    shard_qkv, shard_out, shard_up, shard_down, shard_norm, shard_bias, shard_up_bias = (
        lax.psum_scatter(grad_qkv, ("dp", "seq"), scatter_dimension=0, tiled=True),
        lax.psum_scatter(grad_out, ("dp", "seq"), scatter_dimension=0, tiled=True),
        lax.psum_scatter(grad_up, ("dp", "seq"), scatter_dimension=0, tiled=True),
        lax.psum_scatter(grad_down, ("dp", "seq"), scatter_dimension=0, tiled=True),
        lax.psum_scatter(grad_norm_all, ("dp", "seq"), scatter_dimension=1, tiled=True),
        lax.psum_scatter(grad_bias_all, ("dp", "seq"), scatter_dimension=1, tiled=True),
        lax.psum_scatter(grad_up_bias, ("dp", "seq"), scatter_dimension=0, tiled=True),
    )
    return (
        small_out,
        large_out,
        small_grad,
        large_grad,
        shard_qkv,
        shard_out,
        shard_up,
        shard_down,
        shard_norm,
        shard_bias,
        shard_up_bias,
    )


def solution(mesh):
    in_specs = (
        P(("dp", "seq"), None, None),
        P("dp", "seq", None),
        P(("dp", "seq")),
        P("dp"),
        P(("dp", "seq"), None, None),
        P("dp", "seq", None),
        P(("dp", "seq"), None),
        P(("dp", "seq"), None),
        P(("dp", "seq"), None),
        P(("dp", "seq"), None),
        P(None, ("dp", "seq")),
        P(None, ("dp", "seq")),
        P(("dp", "seq")),
    )
    out_specs = (
        P(("dp", "seq"), None, None),
        P("dp", "seq", None),
        P(("dp", "seq"), None, None),
        P("dp", "seq", None),
        P(("dp", "seq"), None),
        P(("dp", "seq"), None),
        P(("dp", "seq"), None),
        P(("dp", "seq"), None),
        P(None, ("dp", "seq")),
        P(None, ("dp", "seq")),
        P(("dp", "seq")),
    )
    body = shards if (mesh.shape["dp"], mesh.shape["seq"]) == (16, 2) else shards_general
    return jax.shard_map(body, mesh=mesh, in_specs=in_specs, out_specs=out_specs, check_vma=False)
```

```python
import functools

import jax
import jax.numpy as jnp
from jax import lax
from jax.experimental import pallas as pl
from jax.experimental.pallas import tpu as pltpu
from jax.sharding import PartitionSpec as P

HEAD_DIM = 64
MESH = pl.DeviceIdType.MESH
BF = jnp.bfloat16
F32 = jnp.float32


def dot(a, b):
    return lax.dot_general(a, b, (((1,), (0,)), ((), ())), preferred_element_type=F32)


def dot_rows(a, b):
    return lax.dot_general(a, b, (((0,), (0,)), ((), ())), preferred_element_type=F32)


def dot_cols(a, b):
    return lax.dot_general(a, b, (((1,), (1,)), ((), ())), preferred_element_type=F32)


def device(x, y, z, c):
    return ((z * 2 + y) * 2 + c, x)


def rcopy(src, dst, send, recv, dev):
    return pltpu.make_async_remote_copy(
        src_ref=src, dst_ref=dst, send_sem=send, recv_sem=recv, device_id=dev, device_id_type=MESH
    )


def shard_at(j):
    return j // 4, (j // 2) % 2, j % 2


def stack_halves(g):
    n = g.shape[1] // 2
    return jnp.concatenate([g[:, :n], g[:, n:]], axis=0)


def rows_of(i, size, base=0):
    return pl.ds(pl.multiple_of(base + i * size, 16), size)


def lanes_of(i, size, base=0):
    return pl.ds(pl.multiple_of(base + i * size, 128), size)


def normalize(v):
    centred = v - jnp.mean(v, -1, keepdims=True)
    scale = lax.rsqrt(jnp.mean(centred * centred, -1, keepdims=True) + 1e-06)
    return centred * scale, scale


def norm_back(v, gain, grad):
    unit, scale = normalize(v)
    lifted = grad * gain
    inner = jnp.mean(lifted * unit, -1, keepdims=True)
    return scale * (lifted - jnp.mean(lifted, -1, keepdims=True) - unit * inner), unit


def gelu_pair(h):
    p = 0.3275911 * 0.7071067811865476
    t = 1.0 / (1.0 + p * abs(h))
    e = jnp.exp(-0.5 * h * h)
    poly = ((((1.061405429 * t - 1.453152027) * t + 1.421413741) * t - 0.284496736) * t + 0.254829592) * t
    q = 0.5 * poly * e
    phi = jnp.where(h >= 0, 1.0 - q, q)
    return h * phi, phi + h * e * 0.3989422804014327


def total(v):
    return jnp.sum(v.astype(F32), 0, keepdims=True)


def heads_forward(Q, KV, MIX, LSE, bias, q0, nq, k0, nk, first, count, unroll=1):
    D = Q.shape[1]
    left = lax.broadcasted_iota(jnp.int32, (nq, 128), 1) < HEAD_DIM

    def pair(hp, _):
        q = Q[q0 : q0 + nq, lanes_of(hp, 128)] * jnp.asarray(HEAD_DIM**-0.5, BF)
        k = KV[k0 : k0 + nk, lanes_of(hp, 128)]
        v = KV[k0 : k0 + nk, lanes_of(hp, 128, D)]
        zero = jnp.zeros_like(q)
        outs = []
        for head in range(2):
            qm = jnp.where(left, q, zero) if head == 0 else jnp.where(left, zero, q)
            s = dot_cols(k, qm) + bias
            top = jnp.max(s, 0, keepdims=True)
            e = jnp.exp(s - top)
            tot = jnp.sum(e, 0, keepdims=True)
            outs.append(dot_rows(v, e.astype(BF)) * (1.0 / tot))
            LSE[pl.ds(2 * hp + head, 1), 0:nq] = top + jnp.log(tot)
        both = jnp.concatenate([outs[0][:HEAD_DIM], outs[1][HEAD_DIM:]], axis=0)
        MIX[q0 : q0 + nq, lanes_of(hp, 128)] = jnp.transpose(both).astype(BF)
        return 0

    lax.fori_loop(0, count, lambda i, _: pair(first + i, _), 0, unroll=unroll)


def heads_backward(Q, KV, MIX, DMIX, LSE, bias, q0, nq, k0, nk, first, count, unroll=1):
    D = Q.shape[1]
    left = lax.broadcasted_iota(jnp.int32, (nq, 128), 1) < HEAD_DIM
    leftk = lax.broadcasted_iota(jnp.int32, (nk, 128), 1) < HEAD_DIM

    def pair(hp, _):
        q = Q[q0 : q0 + nq, lanes_of(hp, 128)] * jnp.asarray(HEAD_DIM**-0.5, BF)
        dm = DMIX[q0 : q0 + nq, lanes_of(hp, 128)]
        k = KV[k0 : k0 + nk, lanes_of(hp, 128)]
        v = KV[k0 : k0 + nk, lanes_of(hp, 128, D)]
        zero = jnp.zeros_like(q)
        weighted = jnp.transpose(dm.astype(F32) * MIX[q0 : q0 + nq, lanes_of(hp, 128)].astype(F32))
        dqs, dks, dvs = [], [], []
        for head in range(2):
            mask = lambda u: jnp.where(left, u, zero) if head == 0 else jnp.where(left, zero, u)
            delta = jnp.sum(weighted[head * HEAD_DIM : (head + 1) * HEAD_DIM], 0, keepdims=True)
            s = dot_cols(k, mask(q)) + bias
            pr = jnp.exp(s - LSE[pl.ds(2 * hp + head, 1), 0:nq])
            dvs.append(dot(pr.astype(BF), dm))
            ds = (pr * (dot_cols(v, mask(dm)) - delta)).astype(BF)
            dks.append(dot(ds, q))
            dqs.append(dot_rows(k, ds))
        both = jnp.concatenate([dqs[0][:HEAD_DIM], dqs[1][HEAD_DIM:]], axis=0) * HEAD_DIM**-0.5
        Q[q0 : q0 + nq, lanes_of(hp, 128)] = jnp.transpose(both).astype(BF)
        KV[k0 : k0 + nk, lanes_of(hp, 128)] = jnp.where(leftk, dks[0], dks[1]).astype(BF)
        KV[k0 : k0 + nk, lanes_of(hp, 128, D)] = jnp.where(leftk, dvs[0], dvs[1]).astype(BF)
        return 0

    lax.fori_loop(0, count, lambda i, _: pair(first + i, _), 0, unroll=unroll)


def store_block(g, SP, w, h):
    for j in range(16):
        z, y, c = shard_at(j)
        for x in range(2):
            r = 48 * j + 24 * x
            SP[w, h, x, y, z, c] = stack_halves(g[r : r + 24]).astype(BF)


def store_down(g, SP, f):
    n = SP.shape[-1]
    for j in range(4):
        for x in range(2):
            for half in range(2):
                r = (2 * j + x) * 96 + 48 * half
                for h in range(2):
                    SP[2 + half, h, x, j // 2, f, j % 2] = g[r : r + 48, h * n : h * n + n].astype(BF)


def layer_kernel(
    xs, xl, cs, cl, count_s, count_l, wqkv, wout, wup, wdown, norm, bias, upbias,
    OUT, DX, gqkv, gout, gup, gdown, SGO,
    X, DY, H1, Q, KV, MIX, MID, H2, ACC, DH2, ACT, DHB, DH1P, LP, LSES, LSEL,
    WQKV, WOUT, WUP, WDOWN, SP, OWN, LC, T, LF, sp, sm, sml, SG, SGL,
    ss, rs, tsem, psem, sms, smr, gs, gr, s2, r2, credit, room,
):
    d = lax.axis_index("dp")
    x, y, z, c = lax.axis_index("seq"), (d // 2) % 2, d // 4, d % 2
    zs = [z + 1 - 2 * (z % 2), 3 - z, (z + 2) % 4]
    sib, xn, yn = device(x, y, z, 1 - c), device(1 - x, y, z, c), device(x, 1 - y, z, c)
    zn = [device(x, y, k, c) for k in zs]
    bar = pltpu.get_barrier_semaphore()
    for p in [sib, xn, yn] + zn:
        pl.semaphore_signal(bar, inc=1, device_id=p, device_id_type=MESH)

    D = xs.shape[1]
    n = D // 2
    ns, nl = xs.shape[0], xl.shape[0]
    r1 = -(-ns // 16) * 16
    rl = -(-nl // 16) * 16
    R = r1 + rl
    RK = R + rl
    RB = R // 2
    zero = functools.partial(jnp.zeros, dtype=BF)
    head = ns - ns % 16

    blocks = [wqkv[:, k * D : (k + 1) * D] for k in range(3)] + [wout[...]]
    blocks = [stack_halves(g) for g in blocks]
    blocks += [wdown[48 * (b // 2) : 48 * (b // 2) + 48, (b % 2) * n : (b % 2) * n + n] for b in range(4)]
    blocks += [stack_halves(wup[:, k * D : (k + 1) * D]) for k in range(4)]
    for b, g in enumerate(blocks):
        OWN[b // 2, b % 2] = g.astype(BF)
    for w in range(6):
        SP[w, c, x, y, z, c] = OWN[w, c]
    pl.semaphore_wait(bar, 6)
    swaps = [rcopy(OWN.at[w, 1 - c], SP.at[w, 1 - c, x, y, z, c], ss.at[w, 0], rs.at[w, 0], sib) for w in range(6)]
    for cp in swaps:
        cp.start()

    X[head:r1, :] = zero((r1 - head, D))
    X[R - 16 : R, :] = zero((16, D))
    X[0:ns, :] = xs[...]
    X[r1 : r1 + nl, :] = xl[...]

    tcp = rcopy(X.at[r1:R], X.at[R:RK], tsem.at[0], tsem.at[1], xn)

    me = d * 2 + x
    k, m = norm.shape[1], upbias.shape[1]

    def placed(v, start):
        wide = jnp.concatenate([v, jnp.zeros((v.shape[0], D - v.shape[1]), F32)], axis=1)
        return pltpu.roll(wide, start, 1)

    row = lax.broadcasted_iota(jnp.int32, (8, D), 0)
    both = jnp.concatenate([norm[...], bias[...]], axis=0).astype(BF).astype(F32)
    top = placed(both, me * k)
    ub = placed(jnp.broadcast_to(upbias[...].astype(BF).astype(F32), (8, m)), lax.rem(me * m, D))
    low = jnp.where(row == (me * m) // D, ub, 0.0)
    sm[...] = jnp.concatenate([top, low], axis=0).astype(BF)

    def join(buf, land, send, recv, ks, devs):
        cps = [rcopy(buf, land.at[i], send.at[i], recv.at[i], dev) for i, dev in zip(ks, devs)]

        def start():
            for cp in cps:
                cp.start()

        def finish():
            for cp in cps:
                cp.wait()
            tot = buf[...].astype(F32)
            for i in ks:
                tot = tot + land[i].astype(F32)
            buf[...] = tot.astype(buf.dtype)

        return start, finish

    def joins(buf, land, send, recv):
        return [
            join(buf, land, send, recv, *a) for a in (([0], [sib]), ([1], [xn]), ([2], [yn]), ([3, 4, 5], zn))
        ]

    smalls = joins(sm, sml, sms, smr)

    pieces = [z] + zs

    def by_core(run):
        for core in range(2):
            pl.when(c == core)(lambda core=core: run(core))

    swapped_gather, swapped_scatter = (3,), (5, 3, 0)

    def roles(swapped):
        return (y, x, yn, xn) if swapped else (x, y, xn, yn)

    def spot(swapped, u, v, *rest):
        return ((v, u) if swapped else (u, v)) + rest

    def mail(w, sem, dev, out, back):
        sw = w in swapped_gather
        sent, got = SP.at[(w, c) + spot(sw, *out)], SP.at[(w, c) + spot(sw, *back)]
        return (
            rcopy(sent, sent, ss.at[w, sem], rs.at[w, sem], dev),
            rcopy(got, got, ss.at[w, sem], rs.at[w, sem], dev),
        )

    def mails(w, core):
        u, v, un, vn = roles(w in swapped_gather)
        if core == 0:
            one = [mail(w, 1 + i, zn[i], (u, v, z), (u, v, zs[i])) for i in range(3)]
            two = [mail(w, 4 + k, vn, (u, v, p), (u, 1 - v, p)) for k, p in enumerate(pieces)]
            three = [mail(w, 8 + k, un, (u, v, p), (1 - u, v, p)) for k, p in enumerate(pieces)]
            three += [mail(w, 12 + k, un, (u, 1 - v, p), (1 - u, 1 - v, p)) for k, p in enumerate(pieces)]
        else:
            one = [mail(w, 1, un, (u, v, z), (1 - u, v, z))]
            two = [mail(w, 2 + i, zn[i], (u, v, z), (u, v, zs[i])) for i in range(3)]
            two += [mail(w, 5 + i, zn[i], (1 - u, v, z), (1 - u, v, zs[i])) for i in range(3)]
            three = [mail(w, 8 + k, vn, (u, v, p), (u, 1 - v, p)) for k, p in enumerate(pieces)]
            three += [mail(w, 12 + k, vn, (1 - u, v, p), (1 - u, 1 - v, p)) for k, p in enumerate(pieces)]
        return one, two, three

    def a1(w):
        swaps[w].wait()

        def run(core):
            one, two, three = mails(w, core)
            first = one + (two[0:1] + three[0:1] if core == 0 else two[0:3] + three[0:1])
            for sent, _ in first:
                sent.start()

        by_core(run)

    def a2(w):
        def run(core):
            one, two, three = mails(w, core)
            for i, (_, got) in enumerate(one):
                got.wait_recv()
                onward = [two[1 + i], three[1 + i]] if core == 0 else two[3:6] + three[4:5]
                for sent, _ in onward:
                    sent.start()

        by_core(run)

    def a3(w):
        def run(core):
            _, two, three = mails(w, core)
            if core == 0:
                for k in range(4):
                    two[k][1].wait_recv()
                    three[4 + k][0].start()
            else:
                for part in range(2):
                    for i in range(3):
                        two[3 * part + i][1].wait_recv()
                        three[4 * part + 1 + i][0].start()

        by_core(run)

    def a4(w):
        def run(core):
            one, two, three = mails(w, core)
            for _, got in three:
                got.wait_recv()
            for sent, _ in one + two + three:
                sent.wait_send()

        by_core(run)
        src = SP.at[w, c]
        rcopy(src, src, ss.at[w, 16], rs.at[w, 16], sib).start()

    def assemble(w, h, dst, col):
        def step(j, _):
            pz, py, pc = shard_at(j)
            a = SP[w, h, 0, py, pz, pc].astype(F32)
            e = SP[w, h, 1, py, pz, pc].astype(F32)
            dst[rows_of(j, 48), col : col + n] = jnp.concatenate([a[:24], e[:24]], axis=0).astype(BF)
            dst[rows_of(j, 48), col + n : col + D] = jnp.concatenate([a[24:], e[24:]], axis=0).astype(BF)
            return 0

        lax.fori_loop(0, 16, step, 0, unroll=4)

    def assemble_down(w, h):
        def step(j, _):
            pz, py, pc = shard_at(j)
            for px in range(2):
                rows = pl.ds(pl.multiple_of(96 * (2 * j + px) + 48 * (w - 2), 16), 48)
                WDOWN[rows, n * h : n * h + n] = SP[w, h, px, py, pz, pc]
            return 0

        lax.fori_loop(0, 16, step, 0, unroll=4)

    def a5(w):
        src, dst = SP.at[w, c], SP.at[w, 1 - c]
        rcopy(src, src, ss.at[w, 16], rs.at[w, 16], sib).wait_send()
        rcopy(dst, dst, ss.at[w, 16], rs.at[w, 16], sib).wait_recv()
        for h in range(2):
            b = 2 * w + h
            if b < 3:
                assemble(w, h, WQKV, b * D)
            elif b == 3:
                assemble(w, h, WOUT, 0)
            elif b < 8:
                assemble_down(w, h)
            else:
                assemble(w, h, WUP, (b - 8) * D)

    def credits(w):
        for i, dev in enumerate([xn, yn] + zn):
            pl.semaphore_signal(room.at[w, i], inc=1, device_id=dev, device_id_type=MESH)

    order = [4, 5, 2, 3, 1, 0]
    backs = [zs[2], zs[1], zs[0], z]

    def add(w, dst, src, count):
        def step(i, _):
            at = (w, c) + dst(i)
            SP[at] = (SP[at].astype(F32) + src(i).astype(F32)).astype(BF)
            return 0

        lax.fori_loop(0, count, step, 0, unroll=min(count, 4))

    def first_copy(i, k):
        w = order[i]
        return rcopy(SP.at[w, 1 - c, :, :, k], LC.at[i % 2, :, :, k], s2.at[w, k], r2.at[w, k], sib)

    def go(i):
        if i >= 2:
            pl.semaphore_wait(credit, 1)
        for k in range(4):
            first_copy(i, k).start()

    def held(w, u, v, *rest):
        return SP.at[(w, c) + spot(w in swapped_scatter, u, v, *rest)]

    def second_copy(w, k, core):
        pz = backs[k]
        u, v, un, vn = roles(w in swapped_scatter)
        every = slice(None)
        dev = (un, vn)[core]
        src = held(w, 1 - u, every, pz) if core == 0 else held(w, every, 1 - v, pz)
        return rcopy(src, SP.at[w, 1 - c, 0, :, k], s2.at[w, 4 + k], r2.at[w, 4 + k], dev)

    def third_copy(w, k, core):
        pz = backs[k]
        u, v, un, vn = roles(w in swapped_scatter)
        sems = (s2.at[w, 8 + k], r2.at[w, 8 + k])
        if core == 0:
            return rcopy(held(w, u, 1 - v, pz), SP.at[w, 1 - c, 1, 0, k], *sems, vn)
        return rcopy(held(w, slice(None), v, pz), SP.at[w, 1 - c, 1, :, k], *sems, zn[2 - k])

    def fourth_copy(w, k, core):
        u, v, un, vn = roles(w in swapped_scatter)
        sems = (s2.at[w, 12 + k], r2.at[w, 12 + k])
        if core == 0:
            return rcopy(SP.at[w, c, x, y, backs[k]], SP.at[w, 1 - c, 1, 1, k], *sems, zn[2 - k])
        return rcopy(held(w, 1 - u, v, z), SP.at[w, 1 - c, 1, 0, 3], *sems, un)

    def last_copy(w):
        return rcopy(T.at[w, 1 - c], LF.at[w], s2.at[w, 15], r2.at[w, 15], sib)

    def deliver(w):
        mine, other = T[w, c], LF[w]
        for h in range(2):
            g = jnp.where(c == h, mine, other)
            b = 2 * w + h
            if 4 <= b < 8:
                half = (b - 4) // 2
                gdown[48 * half : 48 * half + 48, n * h : n * h + n] = g
                continue
            wide = jnp.concatenate([g[0:24], g[24:48]], axis=1)
            if b >= 8:
                gup[:, (b - 8) * D : (b - 7) * D] = wide
            elif b == 2:
                gout[...] = wide
            else:
                g0 = (3, 2, None, 1)[b] - 1
                third = D // 3
                for part in range(3):
                    lo = part * D + g0 * third
                    gqkv[:, lo : lo + third] = wide[:, part * third : (part + 1) * third]

    def back(i, stage):
        w = order[i]
        sw = w in swapped_scatter
        u, v, _, _ = roles(sw)
        side = (1, 0) if sw else (0, 1)
        if stage == 0:
            for k in range(4):
                first_copy(i, k).wait()
                idx = lambda j: (j // 4, (j // 2) % 2, k, j % 2)
                add(w, idx, lambda j: LC[(i % 2,) + idx(j)], 8)
            if i < 4:
                pl.semaphore_signal(credit, inc=1, device_id=sib, device_id_type=MESH)
            credits(w)
        elif stage == 1:

            def run(core):
                pl.semaphore_wait(room.at[w, side[core]], 1)
                for k in range(4):
                    second_copy(w, k, core).start()

            by_core(run)
        elif stage == 2:

            def run(core):
                if core == 0:
                    pl.semaphore_wait(room.at[w, side[1]], 1)
                for k in range(4):
                    second_copy(w, k, core).wait()
                    place = (
                        (lambda j: spot(sw, u, j // 2, backs[k], j % 2)),
                        (lambda j: spot(sw, j // 2, v, backs[k], j % 2)),
                    )[core]
                    add(w, place, lambda j: SP[w, 1 - c, 0, j // 2, k, j % 2], 4)
                    if core == 1 and k < 3:
                        pl.semaphore_wait(room.at[w, 2 + 2 - k], 1)
                    if core == 0 or k < 3:
                        third_copy(w, k, core).start()

            by_core(run)
        elif stage == 3:

            def run(core):
                if core == 0:
                    for k in range(4):
                        third_copy(w, k, core).wait()
                        add(w, lambda j: (x, y, backs[k], j), lambda j: SP[w, 1 - c, 1, 0, k, j], 2)
                        if k < 3:
                            pl.semaphore_wait(room.at[w, 2 + 2 - k], 1)
                            fourth_copy(w, k, core).start()
                    return
                for k in range(3):
                    third_copy(w, k, core).wait()
                three = lambda j: sum(SP[w, 1 - c, 1, j // 2, k, j % 2].astype(F32) for k in range(3))
                add(w, lambda j: spot(sw, j // 2, v, z, j % 2), three, 4)
                pl.semaphore_wait(room.at[w, side[0]], 1)
                fourth_copy(w, 0, core).start()

            by_core(run)
        elif stage == 4:

            def run(core):
                count = 3 if core == 0 else 1
                for k in range(count):
                    fourth_copy(w, k, core).wait()
                for q in range(2):
                    tot = SP[w, c, x, y, z, q].astype(F32)
                    for k in range(count):
                        at = (1, 1, k, q) if core == 0 else (1, 0, 3, q)
                        tot = tot + SP[(w, 1 - c) + at].astype(F32)
                    T[w, q] = tot

            by_core(run)
            last_copy(w).start()
        else:
            last_copy(w).wait()
            deliver(w)

    def norm_one(base, count):
        def step(i, _):
            rows = rows_of(i, size, base)
            unit, _ = normalize(X[rows, :].astype(F32))
            H1[rows, :] = (unit * sp[0:1, :] + sp[1:2, :]).astype(BF)
            return 0

        size = RB if count % RB == 0 else count
        lax.fori_loop(0, count // size, step, 0)

    small_count, large_count = count_s[0], count_l[0]
    kj = lax.broadcasted_iota(jnp.int32, (r1, 1), 0)
    bias_small = jnp.where(kj < small_count, 0.0, -1e30)
    kj = lax.broadcasted_iota(jnp.int32, (2 * rl, 1), 0)
    mine = kj < rl
    inside = jnp.where(mine, kj, kj - rl)
    where = inside + jnp.where(mine, x, 1 - x) * nl
    bias_large = jnp.where((inside < nl) & (where < large_count), 0.0, -1e30)
    small_part = (bias_small, 0, r1, 0, r1)
    large_part = (bias_large, r1, rl, r1, 2 * rl)

    def take_cotangents():
        DY[head:r1, :] = zero((r1 - head, D))
        DY[R - 16 : R, :] = zero((16, D))
        DY[0:ns, :] = cs[...]
        DY[r1 : r1 + nl, :] = cl[...]

    def know_smalls():
        smalls[3][1]()
        sp[...] = sm[...].astype(F32)

    def query():
        Q[...] = (dot(H1[0:R, :], WQKV[:, 0:D]) + sp[4:5, :]).astype(BF)

    def key():
        KV[:, 0:D] = dot(H1[...], WQKV[:, D : 2 * D]).astype(BF)

    def value():
        KV[:, D:] = (dot(H1[...], WQKV[:, 2 * D :]) + sp[5:6, :]).astype(BF)

    def attend_small():
        heads_forward(Q, KV, MIX, LSES, *small_part, 0, 6, unroll=2)

    def attend_large(hp):
        heads_forward(Q, KV, MIX, LSEL, *large_part, hp, 1)

    def project_out():
        MID[...] = dot(MIX[...], WOUT[...])

    def second_norm():
        def step(i, _):
            rows = rows_of(i, RB)
            middle = X[rows, :].astype(F32) + MID[rows, :] + sp[6:7, :]
            MID[rows, :] = middle
            unit, _ = normalize(middle)
            H2[rows, :] = (unit * sp[2:3, :] + sp[3:4, :]).astype(BF)
            ACC[rows, :] = middle + sp[7:8, :]
            return 0

        lax.fori_loop(0, R // RB, step, 0)

    def hidden_units(f):
        hidden = dot(H2[...], WUP[:, lanes_of(f, D)]) + sp[pl.ds(8 + f, 1), :]
        dact = dot_cols(DY[...], WDOWN[rows_of(f, D), :])
        act, slope = gelu_pair(hidden)
        ACT[f] = act.astype(BF)
        dh = (dact * slope).astype(BF)
        DHB[...] = dh
        SG[pl.ds(8 + f, 1), :] = total(dh)

    def grad_up(f):
        store_block(dot_rows(H2[...], DHB[...]), SP, 4 + f // 2, f % 2)

    def grad_down(f):
        store_down(dot_rows(ACT[f], DY[...]), SP, f)

    def forward_down():
        for f in range(4):
            ACC[...] += dot(ACT[f], WDOWN[f * D : (f + 1) * D, :])

    def backward_up(f):
        DH2[...] += dot_cols(DHB[...], WUP[:, lanes_of(f, D)])

    def give_out():
        OUT[...] = ACC[...].astype(BF)

    z1 = jnp.zeros((1, D), F32)

    def second_norm_back():
        def step(i, sums):
            rows = rows_of(i, RB)
            grad = DH2[rows, :]
            dy = DY[rows, :].astype(F32)
            dv, unit = norm_back(MID[rows, :], sp[2:3, :], grad)
            dmid = dy + dv
            MID[rows, :] = dmid
            low = dmid.astype(BF)
            H2[rows, :] = low
            return sums[0] + total(grad * unit), sums[1] + total(grad), sums[2] + total(low), sums[3] + total(dy)

        sums = lax.fori_loop(0, R // RB, step, (z1, z1, z1, z1))
        for i, at in enumerate((2, 3, 6, 7)):
            SG[at : at + 1, :] = sums[i]

    def grad_mixed():
        DHB[...] = dot_cols(H2[...], WOUT[...]).astype(BF)

    def grad_out():
        store_block(dot_rows(MIX[...], H2[...]), SP, 1, 0)

    third = D // 3

    def back_small(g):
        heads_backward(Q, KV, MIX, DHB, LSES, *small_part, 2 * g, 2, unroll=2)

    def back_large(hp):
        heads_backward(Q, KV, MIX, DHB, LSEL, *large_part, hp, 1)

    def grad_heads(g):
        lo, lov = lanes_of(g, third), lanes_of(g, third, D)
        grads = [dot_rows(H1[0:R, :], Q[:, lo]), dot_rows(H1[...], KV[:, lo]), dot_rows(H1[...], KV[:, lov])]
        store_block(jnp.concatenate(grads, axis=1), SP, (2 - g) // 2, 1 - g // 2)

    pcp = rcopy(DH1P, LP, psem.at[0], psem.at[1], xn)

    def grad_partner():
        g = dot_cols(KV[R:RK, 0:D], WQKV[:, D : 2 * D]) + dot_cols(KV[R:RK, D:], WQKV[:, 2 * D :])
        DH1P[...] = g.astype(BF)

    def grad_normed():
        g = dot_cols(Q[...], WQKV[:, 0:D]) + dot_cols(KV[0:R, 0:D], WQKV[:, D : 2 * D])
        DH2[...] = g + dot_cols(KV[0:R, D:], WQKV[:, 2 * D :])

    def first_norm_back(base, count, partner):
        rows = slice(base, base + count)
        grad = DH2[rows, :]
        if partner:
            grad = grad + LP[...].astype(F32)
        dv, _ = norm_back(X[rows, :].astype(F32), sp[0:1, :], grad)
        DX[rows, :] = (MID[rows, :] + dv).astype(BF)

    ends = joins(SG, SGL, gs, gr)

    def first_norm_sums():
        def step(i, sums):
            unit, _ = normalize(X[rows_of(i, RB), :].astype(F32))
            grad = DH2[rows_of(i, RB), :]
            return sums[0] + total(grad * unit), sums[1] + total(grad)

        sums = lax.fori_loop(0, R // RB, step, (z1, z1))
        unit, _ = normalize(X[R:RK, :].astype(F32))
        grad = DH1P[...].astype(F32)
        SG[0:1, :] = sums[0] + total(grad * unit)
        SG[1:2, :] = sums[1] + total(grad)
        SG[4:5, :] = total(Q[...])
        SG[5:6, :] = total(KV[:, D:])

    def clear():
        SG[...] = jnp.zeros(SG.shape, F32)
        DH2[...] = jnp.zeros(DH2.shape, F32)

    def repeat(count, body, after):
        def step(i, _):
            for k, do in enumerate(body):
                do(i)
                for j in range(count):
                    if after[j][k]:
                        pl.when(i == j)(after[j][k])
            return 0

        lax.fori_loop(0, count, step, 0)

    clear()
    a1(0)
    smalls[0][0]()
    smalls[0][1]()
    smalls[1][0]()
    a2(0)
    a1(1)
    tcp.start()
    smalls[1][1]()
    smalls[2][0]()
    smalls[2][1]()
    take_cotangents()
    smalls[3][0]()
    a2(1)
    a3(0)
    know_smalls()
    a1(2)
    norm_one(0, R)
    a3(1)
    a2(2)
    a4(0)
    a1(3)
    a5(0)
    a2(3)
    tcp.wait()
    norm_one(R, rl)
    a1(4)
    query()
    a4(1)
    key()
    a3(2)
    a5(1)
    value()
    a3(3)

    def then_0():
        a2(4)

    def then_1():
        a4(2)

    def then_2():
        a4(3)
        a3(4)

    def then_3():
        a1(5)
        a5(2)

    repeat(6, (attend_large,), ((None,), (then_0,), (then_1,), (then_2,), (then_3,), (None,),))
    attend_small()
    a4(4)
    project_out()
    a5(3)
    a2(5)
    second_norm()
    a5(4)

    def then_4():
        a3(5)

    def then_5():
        a4(5)

    def then_6():
        go(0)
        a5(5)

    def then_7():
        back(0, 0)

    def then_8():
        back(0, 1)

    def then_9():
        go(1)

    def then_10():
        go(2)

    repeat(4, (hidden_units, grad_up, grad_down, backward_up,), ((then_4, None, None, None), (then_5, None, None, then_6), (then_7, None, None, then_8), (None, then_9, then_10, None),))
    second_norm_back()
    back(1, 0)
    grad_mixed()
    grad_out()
    back(1, 1)
    back(2, 0)

    def then_11():
        go(3)
        back(0, 2)
        back(2, 1)

    def then_12():
        back(3, 0)
        back(1, 2)
        go(4)

    def then_13():
        back(3, 1)

    def then_14():
        back(0, 3)
        back(4, 0)

    def then_15():
        back(2, 2)

    def then_16():
        back(4, 1)

    def then_17():
        back(3, 2)

    repeat(3, (back_small, lambda g: back_large(2 * g), lambda g: back_large(2 * g + 1), grad_heads,), ((None, then_11, None, then_12), (then_13, then_14, then_15, then_16), (then_17, None, None, None),))
    go(5)
    back(1, 3)
    grad_partner()
    pcp.start()
    back(0, 4)
    back(2, 3)
    back(5, 0)
    back(4, 2)
    back(1, 4)
    back(5, 1)
    grad_normed()
    first_norm_sums()
    back(3, 3)
    ends[0][0]()
    back(4, 3)
    ends[0][1]()
    ends[1][0]()
    back(5, 2)
    ends[1][1]()
    ends[2][0]()
    back(0, 5)
    first_norm_back(0, r1, False)
    forward_down()
    back(2, 4)
    back(3, 4)
    back(4, 4)
    ends[2][1]()
    back(1, 5)
    ends[3][0]()
    back(5, 3)
    give_out()
    back(2, 5)
    back(3, 5)
    back(4, 5)
    back(5, 4)
    pcp.wait()
    first_norm_back(r1, rl, True)
    back(5, 5)
    ends[3][1]()
    SGO[...] = SG[...]


def deliver_kernel(
    OUT, DX, gqkv, gout, gup, gdown, SG,
    outs, outl, dxs, dxl, oqkv, oout, oup, odown, onorm, obias, oub,
):
    ns, nl = outs.shape[0], outl.shape[0]
    r1 = -(-ns // 16) * 16
    outs[...] = OUT[0:ns, :]
    outl[...] = OUT[r1 : r1 + nl, :]
    dxs[...] = DX[0:ns, :]
    dxl[...] = DX[r1 : r1 + nl, :]
    oqkv[...] = gqkv[...]
    oout[...] = gout[...]
    oup[...] = gup[...]
    odown[...] = gdown[...]
    D = outs.shape[1]
    me = lax.axis_index("dp") * 2 + lax.axis_index("seq")
    k, m = onorm.shape[1], oub.shape[1]
    near = pltpu.roll(SG[0:8, :], lax.rem(D - me * k, D), 1)[:, 0:k]
    onorm[...] = near[0:4]
    obias[...] = near[4:8]
    row = lax.broadcasted_iota(jnp.int32, (8, D), 0)
    picked = total(jnp.where(row == (me * m) // D, SG[8:16, :], 0.0))
    near = pltpu.roll(jnp.broadcast_to(picked, (8, D)), lax.rem(D - lax.rem(me * m, D), D), 1)
    oub[...] = near[0:1, 0:m]


def vm():
    return pl.BlockSpec(memory_space=pltpu.VMEM)


def layer(xs, xl, cs, cl, count_s, count_l, wqkv, wout, wup, wdown, norm, bias, upbias):
    D = xs.shape[1]
    n = D // 2
    r1 = -(-xs.shape[0] // 16) * 16
    rl = -(-xl.shape[0] // 16) * 16
    R = r1 + rl
    RK = R + rl
    sds = jax.ShapeDtypeStruct
    smem = pl.BlockSpec(memory_space=pltpu.SMEM)
    dma, regular = pltpu.SemaphoreType.DMA, pltpu.SemaphoreType.REGULAR
    small = (16, D)
    return pl.pallas_call(
        layer_kernel,
        out_shape=(
            sds((R, D), BF), sds((R, D), BF),
            sds(wqkv.shape, F32), sds(wout.shape, F32), sds(wup.shape, F32), sds(wdown.shape, F32), sds(small, F32),
        ),
        in_specs=[vm()] * 4 + [smem] * 2 + [vm()] * 7,
        out_specs=(vm(),) * 7,
        scratch_shapes=[
            pltpu.VMEM((RK, D), BF),
            pltpu.VMEM((R, D), BF),
            pltpu.VMEM((RK, D), BF),
            pltpu.VMEM((R, D), BF),
            pltpu.VMEM((RK, 2 * D), BF),
            pltpu.VMEM((R, D), BF),
            pltpu.VMEM((R, D), F32),
            pltpu.VMEM((R, D), BF),
            pltpu.VMEM((R, D), F32),
            pltpu.VMEM((R, D), F32),
            pltpu.VMEM((4, R, D), BF),
            pltpu.VMEM((R, D), BF),
            pltpu.VMEM((rl, D), BF),
            pltpu.VMEM((rl, D), BF),
            pltpu.VMEM((16, r1), F32),
            pltpu.VMEM((16, rl), F32),
            pltpu.VMEM((D, 3 * D), BF),
            pltpu.VMEM((D, D), BF),
            pltpu.VMEM((D, 4 * D), BF),
            pltpu.VMEM((4 * D, D), BF),
            pltpu.VMEM((6, 2, 2, 2, 4, 2, 48, n), BF),
            pltpu.VMEM((6, 2, 48, n), BF),
            pltpu.VMEM((2, 2, 2, 4, 2, 48, n), BF),
            pltpu.VMEM((6, 2, 48, n), F32),
            pltpu.VMEM((6, 48, n), F32),
            pltpu.VMEM(small, F32),
            pltpu.VMEM(small, BF),
            pltpu.VMEM((6,) + small, BF),
            pltpu.VMEM(small, F32),
            pltpu.VMEM((6,) + small, F32),
            dma((6, 17)), dma((6, 17)), dma((2,)), dma((2,)), dma((6,)), dma((6,)), dma((6,)), dma((6,)),
            dma((6, 16)), dma((6, 16)), regular, regular((6, 5)),
        ],
        compiler_params=pltpu.CompilerParams(collective_id=1, has_side_effects=True, vmem_limit_bytes=63 << 20),
        name="layer",
    )(xs, xl, cs, cl, count_s, count_l, wqkv, wout, wup, wdown, norm, bias, upbias)


def shards(
    small_tokens, large_tokens, small_counts, large_counts, small_cot, large_cot,
    w_qkv, w_out, w_up, w_down, norm_params, proj_bias, up_bias,
):
    flat = lambda v: v.reshape(v.shape[1:])
    xs, xl, cs, cl = flat(small_tokens), flat(large_tokens), flat(small_cot), flat(large_cot)
    made = layer(
        xs, xl, cs, cl, small_counts, large_counts, w_qkv, w_out, w_up, w_down, norm_params, proj_bias, up_bias[None]
    )
    like = (xs, xl, xs, xl, w_qkv, w_out, w_up, w_down, norm_params, proj_bias, up_bias[None])
    outs, outl, dxs, dxl, gqkv, gout, gup, gdown, gnorm, gbias, gub = pl.pallas_call(
        deliver_kernel,
        out_shape=tuple(jax.ShapeDtypeStruct(v.shape, v.dtype) for v in like),
        in_specs=[vm()] * 7,
        out_specs=(vm(),) * 11,
        compiler_params=pltpu.CompilerParams(vmem_limit_bytes=62 << 20),
        name="deliver",
    )(*made)
    return outs[None], outl[None], dxs[None], dxl[None], gqkv, gout, gup, gdown, gnorm, gbias, gub[0]


def norm_rows(values, gain, shift):
    centre = jnp.mean(values, -1, keepdims=True)
    centered = values - centre
    spread = jnp.mean(centered * centered, -1, keepdims=True)
    return centered * lax.rsqrt(spread + 1e-06) * gain + shift


def gelu_exact(values):
    return jax.nn.gelu(values, approximate=False)


def general_rows(left, right):
    return lax.dot_general(
        left, right, (((0,), (0,)), ((), ())), preferred_element_type=jnp.float32
    )


def general_cols(left, right):
    return lax.dot_general(
        left, right, (((1,), (1,)), ((), ())), preferred_element_type=jnp.float32
    )


def attend(query, key_part, value, valid_keys, factor):
    raw_scores = jnp.einsum("bqhe,bkhe->bhqk", query, key_part, preferred_element_type=jnp.float32)
    scaled = jnp.where(valid_keys[:, None, None, :], raw_scores * factor, -1e30)
    row_top = jnp.max(scaled, -1, keepdims=True)
    expo_rows = jnp.exp(scaled - row_top)
    totals = jnp.sum(expo_rows, -1, keepdims=True)
    probs_full = expo_rows / totals
    mixed = jnp.einsum(
        "bhqk,bkhe->bqhe",
        probs_full.astype(jnp.bfloat16),
        value,
        preferred_element_type=jnp.float32,
    )
    return (mixed, row_top + jnp.log(totals))


def attend_back(query, key_part, value, valid_keys, log_total, grad_mixed, factor):
    raw_scores = jnp.einsum("bqhe,bkhe->bhqk", query, key_part, preferred_element_type=jnp.float32)
    scaled = jnp.where(valid_keys[:, None, None, :], raw_scores * factor, -1e30)
    probs_full = jnp.exp(scaled - log_total)
    grad_value = jnp.einsum(
        "bhqk,bqhe->bkhe",
        probs_full.astype(jnp.bfloat16),
        grad_mixed,
        preferred_element_type=jnp.float32,
    )
    grad_probs = jnp.einsum(
        "bqhe,bkhe->bhqk", grad_mixed, value, preferred_element_type=jnp.float32
    )
    row_delta = jnp.sum(probs_full * grad_probs, -1, keepdims=True)
    grad_raw = (probs_full * (grad_probs - row_delta) * factor).astype(jnp.bfloat16)
    grad_query = jnp.einsum(
        "bhqk,bkhe->bqhe", grad_raw, key_part, preferred_element_type=jnp.float32
    )
    grad_key = jnp.einsum("bhqk,bqhe->bkhe", grad_raw, query, preferred_element_type=jnp.float32)
    return (grad_query, grad_key, grad_value)


def shards_general(
    small_tokens,
    large_tokens,
    small_counts,
    large_counts,
    small_cot,
    large_cot,
    w_qkv,
    w_out,
    w_up,
    w_down,
    norm_params,
    proj_bias,
    up_bias,
):
    gathered = (
        lax.all_gather(w_qkv.astype(jnp.bfloat16), ("dp", "seq"), axis=0, tiled=True),
        lax.all_gather(w_out.astype(jnp.bfloat16), ("dp", "seq"), axis=0, tiled=True),
        lax.all_gather(w_up.astype(jnp.bfloat16), ("dp", "seq"), axis=0, tiled=True),
        lax.all_gather(w_down.astype(jnp.bfloat16), ("dp", "seq"), axis=0, tiled=True),
        lax.all_gather(norm_params.astype(jnp.bfloat16), ("dp", "seq"), axis=1, tiled=True),
        lax.all_gather(proj_bias.astype(jnp.bfloat16), ("dp", "seq"), axis=1, tiled=True),
        lax.all_gather(up_bias.astype(jnp.bfloat16), ("dp", "seq"), axis=0, tiled=True),
    )
    full_qkv, full_out, full_up, full_down, full_norm, full_bias, full_upbias = gathered
    norm_vals = full_norm.astype(jnp.float32)
    bias_vals = full_bias.astype(jnp.float32)
    upbias_vals = full_upbias.astype(jnp.float32)
    factor = HEAD_DIM ** (-0.5)
    small_images, small_len, width_dim = small_tokens.shape
    half_len = large_tokens.shape[1]
    small_rows = small_images * small_len
    head_count = width_dim // HEAD_DIM
    rows_in = jnp.concatenate(
        [small_tokens.reshape(small_rows, width_dim), large_tokens.reshape(half_len, width_dim)]
    ).astype(jnp.float32)
    normed_one, norm_one_back = jax.vjp(norm_rows, rows_in, norm_vals[0], norm_vals[1])
    normed_one = normed_one.astype(jnp.bfloat16)
    qkv_bias = jnp.concatenate([bias_vals[0], jnp.zeros((width_dim,), jnp.float32), bias_vals[1]])
    qkv_rows = (
        jnp.dot(normed_one, full_qkv, preferred_element_type=jnp.float32) + qkv_bias
    ).astype(jnp.bfloat16)
    qkv_heads = qkv_rows.reshape(-1, 3, head_count, HEAD_DIM)
    small_heads = qkv_heads[:small_rows].reshape(small_images, small_len, 3, head_count, HEAD_DIM)
    query_small = small_heads[:, :, 0]
    key_small = small_heads[:, :, 1]
    value_small = small_heads[:, :, 2]
    valid_small = jnp.arange(small_len, dtype=jnp.int32)[None, :] < small_counts[:, None]
    large_heads = qkv_heads[small_rows:]
    query_large = large_heads[:, 0][None]
    key_whole, value_whole = (
        lax.all_gather(large_heads[:, 1], "seq", axis=0, tiled=True),
        lax.all_gather(large_heads[:, 2], "seq", axis=0, tiled=True),
    )
    key_large = key_whole[None]
    value_large = value_whole[None]
    valid_large = jnp.arange(key_whole.shape[0], dtype=jnp.int32)[None, :] < large_counts[:, None]
    mixed_small, total_small = attend(query_small, key_small, value_small, valid_small, factor)
    mixed_large, total_large = attend(query_large, key_large, value_large, valid_large, factor)
    mixed = jnp.concatenate(
        [mixed_small.reshape(small_rows, width_dim), mixed_large.reshape(half_len, width_dim)]
    ).astype(jnp.bfloat16)
    middle = rows_in + jnp.dot(mixed, full_out, preferred_element_type=jnp.float32) + bias_vals[2]
    normed_two, norm_two_back = jax.vjp(norm_rows, middle, norm_vals[2], norm_vals[3])
    normed_two = normed_two.astype(jnp.bfloat16)
    up_proj = jnp.dot(normed_two, full_up, preferred_element_type=jnp.float32) + upbias_vals
    act_full, gelu_back = jax.vjp(gelu_exact, up_proj)
    act_low = act_full.astype(jnp.bfloat16)
    result = middle + jnp.dot(act_low, full_down, preferred_element_type=jnp.float32) + bias_vals[3]
    result_low = result.astype(jnp.bfloat16)
    small_out = result_low[:small_rows].reshape(small_tokens.shape)
    large_out = result_low[small_rows:].reshape(large_tokens.shape)
    back_qkv, back_out, back_up, back_down = (full_qkv, full_out, full_up, full_down)
    grad_rows = jnp.concatenate(
        [small_cot.reshape(small_rows, width_dim), large_cot.reshape(half_len, width_dim)]
    )
    grad_rows_full = grad_rows.astype(jnp.float32)
    grad_down = general_rows(act_low, grad_rows)
    grad_bias_down = jnp.sum(grad_rows, 0, dtype=jnp.float32)
    grad_act = general_cols(grad_rows, back_down)
    (grad_hidden,) = gelu_back(grad_act)
    grad_hidden_low = grad_hidden.astype(jnp.bfloat16)
    grad_up = general_rows(normed_two, grad_hidden_low)
    grad_up_bias = jnp.sum(grad_hidden_low, 0, dtype=jnp.float32)
    grad_normed_two = general_cols(grad_hidden_low, back_up)
    grad_mid_norm, grad_gain_two, grad_shift_two = norm_two_back(grad_normed_two)
    grad_middle = grad_rows_full + grad_mid_norm
    grad_middle_low = grad_middle.astype(jnp.bfloat16)
    grad_out = general_rows(mixed, grad_middle_low)
    grad_bias_out = jnp.sum(grad_middle_low, 0, dtype=jnp.float32)
    grad_mixed = (
        general_cols(grad_middle_low, back_out).astype(jnp.bfloat16).reshape(-1, head_count, HEAD_DIM)
    )
    grad_mixed_small = grad_mixed[:small_rows].reshape(
        small_images, small_len, head_count, HEAD_DIM
    )
    grad_mixed_large = grad_mixed[small_rows:][None]
    gq_small, gk_small, gv_small = attend_back(
        query_small, key_small, value_small, valid_small, total_small, grad_mixed_small, factor
    )
    gq_large, gk_whole, gv_whole = attend_back(
        query_large, key_large, value_large, valid_large, total_large, grad_mixed_large, factor
    )
    gk_large, gv_large = (
        lax.psum_scatter(
            gk_whole[0].astype(jnp.bfloat16), "seq", scatter_dimension=0, tiled=True
        ).astype(jnp.float32),
        lax.psum_scatter(
            gv_whole[0].astype(jnp.bfloat16), "seq", scatter_dimension=0, tiled=True
        ).astype(jnp.float32),
    )
    grad_qkv_small = jnp.stack([gq_small, gk_small, gv_small], 2).reshape(small_rows, 3 * width_dim)
    grad_qkv_large = jnp.stack([gq_large[0], gk_large, gv_large], 1).reshape(
        half_len, 3 * width_dim
    )
    grad_qkv_low = jnp.concatenate([grad_qkv_small, grad_qkv_large]).astype(jnp.bfloat16)
    grad_qkv = general_rows(normed_one, grad_qkv_low)
    grad_bias_query = jnp.sum(grad_qkv_low[:, :width_dim], 0, dtype=jnp.float32)
    grad_bias_value = jnp.sum(grad_qkv_low[:, 2 * width_dim :], 0, dtype=jnp.float32)
    grad_normed_one = general_cols(grad_qkv_low, back_qkv)
    grad_in_norm, grad_gain_one, grad_shift_one = norm_one_back(grad_normed_one)
    grad_input = (grad_middle + grad_in_norm).astype(jnp.bfloat16)
    small_grad = grad_input[:small_rows].reshape(small_tokens.shape)
    large_grad = grad_input[small_rows:].reshape(large_tokens.shape)
    grad_norm_all = jnp.stack([grad_gain_one, grad_shift_one, grad_gain_two, grad_shift_two])
    grad_bias_all = jnp.stack([grad_bias_query, grad_bias_value, grad_bias_out, grad_bias_down])
    shard_qkv, shard_out, shard_up, shard_down, shard_norm, shard_bias, shard_up_bias = (
        lax.psum_scatter(grad_qkv, ("dp", "seq"), scatter_dimension=0, tiled=True),
        lax.psum_scatter(grad_out, ("dp", "seq"), scatter_dimension=0, tiled=True),
        lax.psum_scatter(grad_up, ("dp", "seq"), scatter_dimension=0, tiled=True),
        lax.psum_scatter(grad_down, ("dp", "seq"), scatter_dimension=0, tiled=True),
        lax.psum_scatter(grad_norm_all, ("dp", "seq"), scatter_dimension=1, tiled=True),
        lax.psum_scatter(grad_bias_all, ("dp", "seq"), scatter_dimension=1, tiled=True),
        lax.psum_scatter(grad_up_bias, ("dp", "seq"), scatter_dimension=0, tiled=True),
    )
    return (
        small_out,
        large_out,
        small_grad,
        large_grad,
        shard_qkv,
        shard_out,
        shard_up,
        shard_down,
        shard_norm,
        shard_bias,
        shard_up_bias,
    )


def solution(mesh):
    in_specs = (
        P(("dp", "seq"), None, None),
        P("dp", "seq", None),
        P(("dp", "seq")),
        P("dp"),
        P(("dp", "seq"), None, None),
        P("dp", "seq", None),
        P(("dp", "seq"), None),
        P(("dp", "seq"), None),
        P(("dp", "seq"), None),
        P(("dp", "seq"), None),
        P(None, ("dp", "seq")),
        P(None, ("dp", "seq")),
        P(("dp", "seq")),
    )
    out_specs = (
        P(("dp", "seq"), None, None),
        P("dp", "seq", None),
        P(("dp", "seq"), None, None),
        P("dp", "seq", None),
        P(("dp", "seq"), None),
        P(("dp", "seq"), None),
        P(("dp", "seq"), None),
        P(("dp", "seq"), None),
        P(None, ("dp", "seq")),
        P(None, ("dp", "seq")),
        P(("dp", "seq")),
    )
    body = shards if (mesh.shape["dp"], mesh.shape["seq"]) == (16, 2) else shards_general
    return jax.shard_map(body, mesh=mesh, in_specs=in_specs, out_specs=out_specs, check_vma=False)
```
